32 devices in a mesh: section: 4 (over z), dp: 8 (over y, x, core).
Axes of the slice: x: 2, y: 2, z: 4, core: 2. Of those that a mesh axis runs over, the one named last changes fastest.
Arguments:
- tokens: bfloat16 [2048, 4096], P('dp'), may hold values from -48 to 48
- orig_weight: bfloat16 [1024, 4096], P(('section', 'dp')), may hold values from -6 to 6
- keep_flags: int32 [64], replicated, may hold values from 0 to 1, as said below
Outputs:
- corrected: bfloat16 [1024, 4096], P(('section', 'dp'))
The draws below stay inside these ranges and needn't reach their ends.
Inputs may be any that keep to these rules, and one draw needn't show every extreme that they name: `keep_flags`: exactly 12 of the 64 flags are 1.
All inputs are finite; a program needn't handle non-finite values.
Results may differ from the reference program's by a relative error of at most 0.003.
Values may be sent and summed in bfloat16 or wider, within the bound.
No kernel may reach another device: no remote copies, remote signals or barrier semaphores. Data moves between devices by JAX's collectives and lax.ppermute only.
A program may use at most 64 MiB of HBM per device.

```python
import jax
import jax.numpy as jnp
from jax import lax

K = 4096
NBLK = 64
KEEP_BLK = 12
KEEP = 768
TOK_DEV = 256
ROWS = 1024
TOKENS = 2048


def block_ranks(key):
    return jax.random.permutation(jax.random.fold_in(key, 21), NBLK)


def draw_tokens(key, part):
    key_noise = jax.random.fold_in(key, 11)
    key_latent = jax.random.fold_in(key, 12)
    key_map = jax.random.fold_in(key, 13)
    key_amp = jax.random.fold_in(key, 14)
    key_block = jax.random.fold_in(key, 15)
    key_cols = jax.random.fold_in(key, 16)
    key_sign = jax.random.fold_in(key, 19)
    blocks = TOKENS // TOK_DEV
    factors = max(KEEP // 4, 8)
    noise = jnp.clip(jax.random.normal(key_noise, (TOKENS, K), jnp.float32), -5.0, 5.0)
    latent = jnp.clip(jax.random.normal(key_latent, (TOKENS, factors), jnp.float32), -5.0, 5.0)
    factor_map = jax.random.randint(key_map, (K,), 0, factors)
    signs = (2 * jax.random.randint(key_sign, (K,), 0, 2) - 1).astype(jnp.float32)
    amplitude = 5.9 * signs * jnp.exp(jax.random.uniform(key_amp, (K,), jnp.float32, -0.5, 0.5))
    shared = jnp.take(latent, factor_map, axis=1) * amplitude[None, :]
    mixed = noise + shared
    kept_block = (block_ranks(key) < KEEP_BLK).astype(jnp.float32)
    boost = jnp.repeat(1.0 + 0.41421356 * kept_block, 64)
    col_scale = jnp.exp(jax.random.uniform(key_cols, (K,), jnp.float32, -0.3, 0.3)) * boost
    block_scale = jnp.exp(jax.random.uniform(key_block, (blocks, NBLK), jnp.float32, 0.0, 1.0))
    levels = 1.0 + 2.0 * jnp.arange(blocks, dtype=jnp.float32) / max(blocks - 1, 1)
    region_scale = jnp.repeat(block_scale * levels[:, None], 64, axis=1)
    token_scale = jnp.repeat(region_scale, TOK_DEV, axis=0)
    result = 0.1 * mixed * token_scale * col_scale[None, :]
    result = jnp.clip(result, -48.0, 48.0)
    return result.astype(jnp.bfloat16)


def draw_keep_flags(key, part):
    return (block_ranks(key) < KEEP_BLK).astype(jnp.int32)


def steps_of(own_key, shape, split, smallest, largest):
    loudness, own = 1.0, jax.random.fold_in(own_key, 6)
    for position, shards_of in split:
        draws = jnp.exp(jax.random.uniform(jax.random.fold_in(own, position), (shards_of,), jnp.float32, smallest / len(split), largest / len(split)))
        loudness = loudness * jnp.repeat(draws, shape[position] // shards_of).reshape([-1 if axis == position else 1 for axis in range(len(shape))])
    return loudness


def gaussian(rng, extent, deviation, most, pieces=(), held_as=jnp.bfloat16):
    factor_of = steps_of(rng, extent, pieces, -0.22, 0.18) if pieces else 1.0
    array = jax.random.normal(rng, extent, jnp.float32) * deviation * factor_of
    return jnp.minimum(jnp.maximum(array, -most), most).astype(held_as)


def setup_inputs(seed: int = 0) -> dict:
    splits = jax.random.split(jax.random.key(seed), 4)
    return {
        "tokens": draw_tokens(jax.random.fold_in(splits[3], 71), 0),
        "orig_weight": gaussian(splits[1], (ROWS, K), 1.0, 6.0, ((0, 32),)),
        "keep_flags": draw_keep_flags(jax.random.fold_in(splits[3], 71), 0),
    }


def reference(tokens, orig_weight, keep_flags):
    highest = lax.Precision.HIGHEST
    blocks = jnp.nonzero(keep_flags, size=KEEP_BLK)[0].astype(jnp.int32)
    kept_index = (blocks[:, None] * 64 + jnp.arange(64, dtype=jnp.int32)[None, :]).reshape(-1).astype(jnp.int32)
    kept_tokens = jnp.take(tokens, kept_index, axis=1).astype(jnp.float32)
    wide_tokens = tokens.astype(jnp.float32)
    gramian = jnp.dot(kept_tokens.T, kept_tokens, precision=highest)
    damping = 0.01 * jnp.sum(wide_tokens * wide_tokens) / K
    cross = jnp.dot(kept_tokens.T, wide_tokens, precision=highest)
    right_side = jnp.dot(cross, orig_weight.astype(jnp.float32).T, precision=highest)
    system = gramian + damping * jnp.eye(KEEP, dtype=jnp.float32)
    factor = jnp.linalg.cholesky(system)
    solution = jax.scipy.linalg.cho_solve((factor, True), right_side)
    corrected = jnp.zeros((ROWS, K), jnp.float32).at[:, kept_index].set(solution.T)
    return corrected.astype(jnp.bfloat16)
```

```python
import jax
import jax.numpy as jnp
from jax import lax
from jax.experimental import pallas as pl
from jax.experimental.pallas import tpu as pltpu
from jax.sharding import PartitionSpec as P

KEEP_BLK = 12
PANEL = 128
SUB = 8
EXTRA = 16
VMEM_LIMIT = 56 * 1024 * 1024
NT = (((1,), (1,)), ((), ()))
NN = (((1,), (0,)), ((), ()))


def split3(x):
    hi = x.astype(jnp.bfloat16)
    rest = x - hi.astype(jnp.float32)
    mid = rest.astype(jnp.bfloat16)
    low = (rest - mid.astype(jnp.float32)).astype(jnp.bfloat16)
    return hi, mid, low


def dot32(a, b, dims):
    return lax.dot_general(a, b, dims, preferred_element_type=jnp.float32)


def kept_blocks(flags_ref, index_ref, blocks):
    def step(b, count):
        index_ref[count] = b
        return count + flags_ref[b]

    lax.fori_loop(0, blocks, step, jnp.int32(0))


def select_kernel(flags_ref, tokens_ref, out_ref, index_ref, tile_ref):
    rows, features = tokens_ref.shape
    blocks = flags_ref.shape[0]
    width = features // blocks
    per_tile = 128 // width
    kept_blocks(flags_ref, index_ref, blocks)
    for i in range(KEEP_BLK):
        b = index_ref[i]
        start = pl.multiple_of((b // per_tile) * 128, 128)
        tile_ref[...] = tokens_ref[:, pl.ds(start, 128)].astype(jnp.float32).T
        inner = pl.multiple_of((b % per_tile) * width, width)
        out_ref[i * width:(i + 1) * width, :] = tile_ref[pl.ds(inner, width), :].astype(jnp.bfloat16)
    total = jnp.zeros((rows, 128), jnp.float32)
    for c in range(features // 128):
        piece = tokens_ref[:, c * 128:(c + 1) * 128].astype(jnp.float32)
        total += piece * piece
    squares = jnp.sum(total)
    hi, mid, low = split3(jnp.full((EXTRA, rows), squares, jnp.float32))
    row = lax.broadcasted_iota(jnp.int32, (EXTRA, rows), 0)
    zero = jnp.zeros((EXTRA, rows), jnp.float32)
    carried = jnp.where(
        row == 0,
        hi.astype(jnp.float32),
        jnp.where(row == 1, mid.astype(jnp.float32), jnp.where(row == 2, low.astype(jnp.float32), zero)),
    )
    out_ref[KEEP_BLK * width:, :] = carried.astype(jnp.bfloat16)


def select_kept(tokens, keep_flags):
    rows, features = tokens.shape
    blocks = keep_flags.shape[0]
    width = features // blocks
    kept = KEEP_BLK * width
    return pl.pallas_call(
        select_kernel,
        out_shape=jax.ShapeDtypeStruct((kept + EXTRA, rows), jnp.bfloat16),
        in_specs=[
            pl.BlockSpec(memory_space=pltpu.SMEM),
            pl.BlockSpec(memory_space=pltpu.VMEM),
        ],
        out_specs=pl.BlockSpec(memory_space=pltpu.VMEM),
        scratch_shapes=[
            pltpu.SMEM((blocks + 1,), jnp.int32),
            pltpu.VMEM((128, rows), jnp.float32),
        ],
        compiler_params=pltpu.CompilerParams(vmem_limit_bytes=VMEM_LIMIT),
        name="select_kept",
    )(keep_flags, tokens)


def reciprocal(x):
    r = pl.reciprocal(x, approx=True)
    r = r * (2.0 - x * r)
    return r * (2.0 - x * r)


def lane_column(x, c):
    return jnp.broadcast_to(x[:, c:c + 1], (SUB, 128))


def sublane_row(x, t):
    return jnp.broadcast_to(x[t:t + 1, :], (SUB, 128))


def invert_small(cols, sub):
    cols = list(cols)
    for t in range(SUB):
        r = reciprocal(sublane_row(cols[t], t))
        pivot_col = cols[t]
        here = sub == t
        for j in range(SUB):
            if j != t:
                w = sublane_row(cols[j], t) * r
                cols[j] = jnp.where(here, w, cols[j] - pivot_col * w)
        cols[t] = jnp.where(here, r, -(pivot_col * r))
    return cols


def invert_panel(block):
    size = block.shape[0]
    count = size // SUB
    sub = lax.broadcasted_iota(jnp.int32, (SUB, 128), 0)
    lane = lax.broadcasted_iota(jnp.int32, (SUB, 128), 1)
    rows = [block[i * SUB:(i + 1) * SUB, :] for i in range(count)]
    for s in range(count):
        base = s * SUB
        inside = (lane >= base) & (lane < base + SUB)
        cols = invert_small([lane_column(rows[s], base + j) for j in range(SUB)], sub)
        unit = jnp.where(lane == sub + base, 1.0, 0.0)
        pivot_rows = jnp.where(inside, unit, rows[s])
        new = cols[0] * sublane_row(pivot_rows, 0)
        for j in range(1, SUB):
            new = new + cols[j] * sublane_row(pivot_rows, j)
        spread = [sublane_row(new, j) for j in range(SUB)]
        for i in range(count):
            if i != s:
                change = lane_column(rows[i], base) * spread[0]
                for j in range(1, SUB):
                    change = change + lane_column(rows[i], base + j) * spread[j]
                rows[i] = jnp.where(inside, 0.0, rows[i]) - change
        rows[s] = new
    return jnp.concatenate(rows, axis=0)


def wide_left(x):
    hi, mid, low = split3(x)
    return jnp.concatenate([hi, hi, mid, hi, mid, low], axis=1)


def wide_right(x):
    hi, mid, low = split3(x)
    return jnp.concatenate([hi, mid, hi, low, mid, hi], axis=0)


def invert_kernel(*refs):
    pieces = refs[:-5]
    out_ref, damp_ref, all_ref, w_ref, sem = refs[-5:]
    n = len(pieces)
    kept = out_ref.shape[0]
    rows = pieces[0].shape[1]
    copies = [
        pltpu.make_async_copy(pieces[k], all_ref.at[:, k * rows:(k + 1) * rows], sem.at[k]) for k in range(n)
    ]
    for copy in copies:
        copy.start()
    for copy in copies:
        copy.wait()
    features_total = damp_ref[0]
    total = jnp.float32(0.0)
    for k in range(n):
        total = total + jnp.sum(all_ref[kept:, k * rows:k * rows + 1].astype(jnp.float32))
    damping = 0.01 * total / features_total
    spread = jnp.full((8, 128), damping, jnp.float32)
    scale = (1.0 / spread)[0:1, 0:1]
    chunk = 2048 if (n * rows) % 2048 == 0 else rows
    unit = (
        lax.broadcasted_iota(jnp.int32, (kept, PANEL), 0) - lax.broadcasted_iota(jnp.int32, (kept, PANEL), 1)
    )

    @pl.loop(0, kept // PANEL)
    def _(j):
        at = pl.multiple_of(j * PANEL, PANEL)
        acc = jnp.where(unit == at, 1.0, 0.0)
        for c in range(0, n * rows, chunk):
            part = dot32(all_ref[:kept, c:c + chunk], all_ref[pl.ds(at, PANEL), c:c + chunk], NT)
            acc = acc + part * scale
        out_ref[:, pl.ds(at, PANEL)] = acc

    @pl.loop(0, kept // PANEL)
    def _(p):
        at = pl.multiple_of(p * PANEL, PANEL)
        here = pl.ds(at, PANEL)
        inverse = invert_panel(out_ref[here, here])
        w_ref[...] = dot32(wide_left(inverse), wide_right(out_ref[here, :]), NN)
        w_ref[:, here] = inverse
        column = wide_left(out_ref[:, here])
        out_ref[:, here] = jnp.zeros((kept, PANEL), jnp.float32)
        for c in range(0, kept, 256):
            out_ref[:, c:c + 256] -= dot32(column, wide_right(w_ref[:, c:c + 256]), NN)
        out_ref[here, :] = w_ref[...]

    out_ref[...] = out_ref[...] * scale


def invert(pieces, features):
    kept_extra, rows = pieces[0].shape
    kept = kept_extra - EXTRA
    n = len(pieces)
    any_spec = pl.BlockSpec(memory_space=pl.ANY)

    def body(*refs):
        ins, rest = refs[:n], refs[n:]
        invert_kernel(*ins, rest[0], [float(features)], *rest[1:])

    return pl.pallas_call(
        body,
        out_shape=jax.ShapeDtypeStruct((kept, kept), jnp.float32),
        in_specs=[any_spec] * n,
        out_specs=pl.BlockSpec(memory_space=pltpu.VMEM),
        scratch_shapes=[
            pltpu.VMEM((kept_extra, n * rows), jnp.bfloat16),
            pltpu.VMEM((PANEL, kept), jnp.float32),
            pltpu.SemaphoreType.DMA((n,)),
        ],
        compiler_params=pltpu.CompilerParams(vmem_limit_bytes=VMEM_LIMIT),
        name="invert_system",
    )(*pieces)


def apply_kernel(flags_ref, proj_ref, inverse_ref, *refs):
    n = len(refs) - 3
    pieces, (out_ref, index_ref, wide_ref) = refs[:n], refs[n:]
    own, features = out_ref.shape
    blocks = flags_ref.shape[0]
    width = features // blocks
    per_tile = 128 // width
    kept = inverse_ref.shape[0]
    kept_blocks(flags_ref, index_ref, blocks)
    right = jnp.zeros((own, kept), jnp.float32)
    for k in range(n):
        hi, mid, low = split3(proj_ref[k])
        stacked = dot32(jnp.concatenate([hi, mid, low], axis=0), pieces[k][:kept, :], NT)
        right += stacked[:own] + stacked[own:2 * own] + stacked[2 * own:]
    hi, mid, low = split3(right)
    ihi, imid, ilow = split3(inverse_ref[...])
    first = dot32(jnp.concatenate([hi, mid, low], axis=0), ihi, NN)
    second = dot32(jnp.concatenate([hi, mid], axis=0), imid, NN)
    third = dot32(hi, ilow, NN)
    answer = (
        first[:own] + first[own:2 * own] + second[:own] + first[2 * own:] + second[own:] + third
    )
    wide_ref[...] = jnp.zeros((own, features), jnp.float32)
    place = lax.broadcasted_iota(jnp.int32, (own, 128), 1) // width
    for i in range(KEEP_BLK):
        b = index_ref[i]
        start = pl.multiple_of((b // per_tile) * 128, 128)
        inner = b % per_tile
        t = i // per_tile
        source = answer[:, t * 128:(t + 1) * 128]
        moved = pltpu.roll(source, width, 1)
        same = inner == i % per_tile
        value = jnp.where(same, source, moved)
        old = wide_ref[:, pl.ds(start, 128)]
        wide_ref[:, pl.ds(start, 128)] = jnp.where(place == inner, value, old)
    out_ref[...] = wide_ref[...].astype(jnp.bfloat16)


def apply_inverse(keep_flags, projected, inverse, pieces, features):
    n, own, rows = projected.shape
    blocks = keep_flags.shape[0]
    vmem = pl.BlockSpec(memory_space=pltpu.VMEM)
    return pl.pallas_call(
        apply_kernel,
        out_shape=jax.ShapeDtypeStruct((own, features), jnp.bfloat16),
        in_specs=[pl.BlockSpec(memory_space=pltpu.SMEM)] + [vmem] * (2 + n),
        out_specs=vmem,
        scratch_shapes=[
            pltpu.SMEM((blocks + 1,), jnp.int32),
            pltpu.VMEM((own, features), jnp.float32),
        ],
        compiler_params=pltpu.CompilerParams(vmem_limit_bytes=VMEM_LIMIT),
        name="apply_inverse",
    )(keep_flags, projected, inverse, *pieces)


def solution(mesh):
    n = mesh.shape["dp"]

    def swap(x, k):
        return lax.ppermute(x, "dp", [(d, d ^ k) for d in range(n)])

    def on_device(tokens, orig_weight, keep_flags):
        features = tokens.shape[1]
        own = orig_weight.shape[0]
        kept = select_kept(tokens, keep_flags)
        pieces = [None] * n
        pieces[0] = kept
        for k in range(2, n, 2):
            pieces[k] = swap(kept, k)
        for k in range(0, n, 2):
            pieces[k + 1] = swap(pieces[k], 1)
        weights = lax.all_gather(orig_weight, "dp", axis=0, tiled=True)
        projected = lax.dot_general(weights, tokens, NT, preferred_element_type=jnp.float32)
        me = lax.axis_index("dp")
        parts = []
        for k in range(n):
            part = lax.dynamic_slice_in_dim(projected, (me ^ k) * own, own, axis=0)
            parts.append(part if k == 0 else swap(part, k))
        inverse = invert(pieces, features)
        return apply_inverse(keep_flags, jnp.stack(parts), inverse, pieces, features)

    in_specs = (P("dp", None), P(("section", "dp"), None), P())
    out_specs = P(("section", "dp"), None)
    return jax.shard_map(on_device, mesh=mesh, in_specs=in_specs, out_specs=out_specs, check_vma=False)
```

```python
import functools

import jax
import jax.numpy as jnp
from jax import lax
from jax.experimental import pallas as pl
from jax.experimental.pallas import tpu as pltpu
from jax.sharding import PartitionSpec as P

KEEP_BLK = 12
PANEL = 128
SUB = 8
EXTRA = 16
VMEM_LIMIT = 56 * 1024 * 1024
NT = (((1,), (1,)), ((), ()))
NN = (((1,), (0,)), ((), ()))


def split3(x):
    hi = x.astype(jnp.bfloat16)
    rest = x - hi.astype(jnp.float32)
    mid = rest.astype(jnp.bfloat16)
    low = (rest - mid.astype(jnp.float32)).astype(jnp.bfloat16)
    return hi, mid, low


def dot32(a, b, dims):
    return lax.dot_general(a, b, dims, preferred_element_type=jnp.float32)


def kept_blocks(flags_ref, index_ref):
    count = jnp.int32(0)
    for b in range(flags_ref.shape[0]):
        index_ref[count] = b
        count = count + flags_ref[b]


def select_kernel(flags_ref, tokens_ref, out_ref, index_ref, tile_ref, chunk_ref, tile_sem, chunk_sem):
    rows, features = tokens_ref.shape
    blocks = flags_ref.shape[0]
    width = features // blocks
    per_tile = 128 // width
    chunks = chunk_ref.shape[0]
    step = rows // chunks
    kept_blocks(flags_ref, index_ref)
    tiles = []
    for i in range(KEEP_BLK):
        start = pl.multiple_of((index_ref[i] // per_tile) * 128, 128)
        tiles.append(
            pltpu.make_async_copy(tokens_ref.at[:, pl.ds(start, 128)], tile_ref.at[i], tile_sem.at[i])
        )
        tiles[-1].start()
    reads = []
    for c in range(chunks):
        reads.append(
            pltpu.make_async_copy(tokens_ref.at[c * step:(c + 1) * step, :], chunk_ref.at[c], chunk_sem.at[c])
        )
        reads[-1].start()
    row = lax.broadcasted_iota(jnp.int32, (width, 128), 0)
    lane = lax.broadcasted_iota(jnp.int32, (width, 128), 1)
    for i in range(KEEP_BLK):
        inner = (index_ref[i] % per_tile) * width
        pick = jnp.where(lane == row + inner, 1.0, 0.0).astype(jnp.bfloat16)
        tiles[i].wait()
        out_ref[i * width:(i + 1) * width, :] = dot32(pick, tile_ref[i], NT).astype(jnp.bfloat16)
    total = jnp.zeros((step, 128), jnp.float32)
    for c in range(chunks):
        reads[c].wait()
        for f in range(features // 128):
            piece = chunk_ref[c, :, f * 128:(f + 1) * 128].astype(jnp.float32)
            total += piece * piece
    squares = jnp.sum(total)
    hi, mid, low = split3(jnp.full((EXTRA, rows), squares, jnp.float32))
    row = lax.broadcasted_iota(jnp.int32, (EXTRA, rows), 0)
    carried = jnp.where(
        row == 0,
        hi.astype(jnp.float32),
        jnp.where(row == 1, mid.astype(jnp.float32), jnp.where(row == 2, low.astype(jnp.float32), 0.0)),
    )
    out_ref[KEEP_BLK * width:, :] = carried.astype(jnp.bfloat16)


def select_kept(tokens, keep_flags):
    rows, features = tokens.shape
    blocks = keep_flags.shape[0]
    kept = KEEP_BLK * (features // blocks)
    chunks = 4
    return pl.pallas_call(
        select_kernel,
        out_shape=jax.ShapeDtypeStruct((kept + EXTRA, rows), jnp.bfloat16),
        in_specs=[
            pl.BlockSpec(memory_space=pltpu.SMEM),
            pl.BlockSpec(memory_space=pl.ANY),
        ],
        out_specs=pl.BlockSpec(memory_space=pltpu.VMEM),
        scratch_shapes=[
            pltpu.SMEM((blocks + 1,), jnp.int32),
            pltpu.VMEM((KEEP_BLK, rows, 128), jnp.bfloat16),
            pltpu.VMEM((chunks, rows // chunks, features), jnp.bfloat16),
            pltpu.SemaphoreType.DMA((KEEP_BLK,)),
            pltpu.SemaphoreType.DMA((chunks,)),
        ],
        compiler_params=pltpu.CompilerParams(vmem_limit_bytes=VMEM_LIMIT),
        name="select_kept",
    )(keep_flags, tokens)


def lane_column(x, c):
    return jnp.broadcast_to(x[:, c:c + 1], (SUB, 128))


def sublane_row(x, t):
    return jnp.broadcast_to(x[t:t + 1, :], (SUB, 128))


def tree_sum(terms):
    while len(terms) > 1:
        pairs = [terms[i] + terms[i + 1] for i in range(0, len(terms) - 1, 2)]
        terms = pairs + terms[len(terms) - len(terms) % 2:]
    return terms[0]


def invert_small(cols, sub):
    cols = list(cols)
    r = pl.reciprocal(sublane_row(cols[0], 0), approx=True)
    for t in range(SUB):
        here = sub == t
        after = None
        if t + 1 < SUB:
            product = sublane_row(cols[t + 1], t) * sublane_row(cols[t], t + 1)
            after = pl.reciprocal(sublane_row(cols[t + 1], t + 1) - product * r, approx=True)
        pivot_col = jnp.where(here, -1.0, cols[t])
        for j in range(SUB):
            if j != t:
                w = sublane_row(cols[j], t) * r
                cols[j] = jnp.where(here, 0.0, cols[j]) - pivot_col * w
        cols[t] = -(pivot_col * r)
        r = after
    return cols


def invert_panel(block):
    size = block.shape[0]
    count = size // SUB
    sub = lax.broadcasted_iota(jnp.int32, (SUB, 128), 0)
    lane = lax.broadcasted_iota(jnp.int32, (SUB, 128), 1)
    rows = [block[i * SUB:(i + 1) * SUB, :] for i in range(count)]
    for s in range(count):
        base = s * SUB
        inside = (lane >= base) & (lane < base + SUB)
        cols = invert_small([lane_column(rows[s], base + j) for j in range(SUB)], sub)
        pivot_rows = jnp.where(inside, jnp.where(lane == sub + base, 1.0, 0.0), rows[s])
        new = tree_sum([cols[j] * sublane_row(pivot_rows, j) for j in range(SUB)])
        spread = [sublane_row(new, j) for j in range(SUB)]
        for i in [(s + d) % count for d in range(1, count)]:
            change = tree_sum([lane_column(rows[i], base + j) * spread[j] for j in range(SUB)])
            rows[i] = jnp.where(inside, 0.0, rows[i]) - change
        rows[s] = new
    return jnp.concatenate(rows, axis=0)


def wide_left(x):
    hi, mid, low = split3(x)
    return jnp.concatenate([hi, hi, mid, hi, mid, low], axis=1)


def wide_right(x):
    hi, mid, low = split3(x)
    return jnp.concatenate([hi, mid, hi, low, mid, hi], axis=0)


def sweep(first, last, a_ref, left_ref, right_ref, scale=None):
    kept = a_ref.shape[0]
    left_ref[...] = jnp.zeros_like(left_ref)
    right_ref[...] = jnp.zeros_like(right_ref)
    row = lax.broadcasted_iota(jnp.int32, (kept, PANEL), 0)

    @pl.loop(first, last)
    def _(p):
        at = pl.multiple_of(p * PANEL, PANEL)
        here = pl.ds(at, PANEL)
        inverse = invert_panel(a_ref[here, here] - dot32(left_ref[here, :], right_ref[:, here], NN))
        for c in range(0, kept, 256):
            a_ref[:, c:c + 256] -= dot32(left_ref[...], right_ref[:, c:c + 256], NN)
        column = jnp.where((row >= at) & (row < at + PANEL), 0.0, a_ref[:, here])
        left_ref[...] = wide_left(column)
        a_ref[:, here] = jnp.zeros((kept, PANEL), jnp.float32)
        wide = wide_left(inverse)
        for c in range(0, kept, 256):
            a_ref[here, c:c + 256] = dot32(wide, wide_right(a_ref[here, c:c + 256]), NN)
        a_ref[here, here] = inverse
        right_ref[...] = wide_right(a_ref[here, :])

    for c in range(0, kept, 256):
        value = a_ref[:, c:c + 256] - dot32(left_ref[...], right_ref[:, c:c + 256], NN)
        a_ref[:, c:c + 256] = value if scale is None else value * scale


def first_kernel(features, last, *refs):
    pieces = refs[:-6]
    out_ref, scale_ref, all_ref, left_ref, right_ref, sem = refs[-6:]
    n = len(pieces)
    kept = out_ref.shape[0]
    rows = pieces[0].shape[1]
    copies = [
        pltpu.make_async_copy(pieces[k], all_ref.at[:, k * rows:(k + 1) * rows], sem.at[k]) for k in range(n)
    ]
    for copy in copies:
        copy.start()
    for copy in copies:
        copy.wait()
    total = jnp.float32(0.0)
    for k in range(n):
        total = total + jnp.sum(all_ref[kept:, k * rows:k * rows + 1].astype(jnp.float32))
    scale_ref[...] = 1.0 / jnp.full(scale_ref.shape, 0.01 * total / features, jnp.float32)
    scale = scale_ref[0:1, 0:1]
    chunk = 2048 if (n * rows) % 2048 == 0 else rows
    tile = 256
    unit = lax.broadcasted_iota(jnp.int32, (kept, tile), 0) - lax.broadcasted_iota(jnp.int32, (kept, tile), 1)

    @pl.loop(0, kept // tile)
    def _(j):
        at = pl.multiple_of(j * tile, tile)
        acc = jnp.where(unit == at, 1.0, 0.0)
        for c in range(0, n * rows, chunk):
            part = dot32(all_ref[:kept, c:c + chunk], all_ref[pl.ds(at, tile), c:c + chunk], NT)
            acc = acc + part * scale
        out_ref[:, pl.ds(at, tile)] = acc

    sweep(0, last, out_ref, left_ref, right_ref)


def first_half(pieces, features, last):
    kept_extra, rows = pieces[0].shape
    kept = kept_extra - EXTRA
    n = len(pieces)
    return pl.pallas_call(
        functools.partial(first_kernel, float(features), last),
        out_shape=[
            jax.ShapeDtypeStruct((kept, kept), jnp.float32),
            jax.ShapeDtypeStruct((8, 128), jnp.float32),
        ],
        in_specs=[pl.BlockSpec(memory_space=pl.ANY)] * n,
        out_specs=[pl.BlockSpec(memory_space=pltpu.VMEM)] * 2,
        scratch_shapes=[
            pltpu.VMEM((kept_extra, n * rows), jnp.bfloat16),
            pltpu.VMEM((kept, 6 * PANEL), jnp.bfloat16),
            pltpu.VMEM((6 * PANEL, kept), jnp.bfloat16),
            pltpu.SemaphoreType.DMA((n,)),
        ],
        compiler_params=pltpu.CompilerParams(vmem_limit_bytes=VMEM_LIMIT),
        name="gram_and_first_panels",
    )(*pieces)


def second_kernel(first, a_ref, scale_ref, out_ref, left_ref, right_ref):
    kept = out_ref.shape[0]
    out_ref[...] = a_ref[...]
    sweep(first, kept // PANEL, out_ref, left_ref, right_ref, scale_ref[0:1, 0:1])


def second_half(a, scale, first):
    kept = a.shape[0]
    vmem = pl.BlockSpec(memory_space=pltpu.VMEM)
    return pl.pallas_call(
        functools.partial(second_kernel, first),
        out_shape=jax.ShapeDtypeStruct((kept, kept), jnp.float32),
        in_specs=[vmem, vmem],
        out_specs=vmem,
        scratch_shapes=[
            pltpu.VMEM((kept, 6 * PANEL), jnp.bfloat16),
            pltpu.VMEM((6 * PANEL, kept), jnp.bfloat16),
        ],
        compiler_params=pltpu.CompilerParams(vmem_limit_bytes=VMEM_LIMIT),
        name="last_panels",
    )(a, scale)


def apply_kernel(chips, flags_ref, *refs):
    projected, refs = refs[:chips], refs[chips:]
    inverse_ref, refs = refs[0], refs[1:]
    pieces, (out_ref, index_ref, wide_ref) = refs[:2 * chips], refs[2 * chips:]
    own, features = out_ref.shape
    blocks = flags_ref.shape[0]
    width = features // blocks
    per_tile = 128 // width
    kept = inverse_ref.shape[0]
    rows = pieces[0].shape[1]
    kept_blocks(flags_ref, index_ref)
    right = jnp.zeros((3 * own, kept), jnp.float32)
    for k in range(chips):
        for core in range(2):
            hi, mid, low = split3(projected[k][:, core * rows:(core + 1) * rows])
            right += dot32(jnp.concatenate([hi, mid, low], axis=0), pieces[2 * k + core][:kept, :], NT)
    right = right[:own] + right[own:2 * own] + right[2 * own:]
    hi, mid, low = split3(right)
    ihi, imid, ilow = split3(inverse_ref[...])
    first = dot32(jnp.concatenate([hi, mid, low], axis=0), ihi, NN)
    second = dot32(jnp.concatenate([hi, mid], axis=0), imid, NN)
    third = dot32(hi, ilow, NN)
    answer = first[:own] + first[own:2 * own] + second[:own] + first[2 * own:] + second[own:] + third
    wide_ref[...] = jnp.zeros((own, features), jnp.float32)
    place = lax.broadcasted_iota(jnp.int32, (own, 128), 1) // width
    for i in range(KEEP_BLK):
        b = index_ref[i]
        start = pl.multiple_of((b // per_tile) * 128, 128)
        inner = b % per_tile
        t = i // per_tile
        source = answer[:, t * 128:(t + 1) * 128]
        moved = pltpu.roll(source, width, 1)
        value = jnp.where(inner == i % per_tile, source, moved)
        old = wide_ref[:, pl.ds(start, 128)]
        wide_ref[:, pl.ds(start, 128)] = jnp.where(place == inner, value, old)
    out_ref[...] = wide_ref[...].astype(jnp.bfloat16)


def apply_inverse(keep_flags, projected, inverse, pieces, features):
    own = projected[0].shape[0]
    blocks = keep_flags.shape[0]
    chips = len(projected)
    vmem = pl.BlockSpec(memory_space=pltpu.VMEM)
    return pl.pallas_call(
        functools.partial(apply_kernel, chips),
        out_shape=jax.ShapeDtypeStruct((own, features), jnp.bfloat16),
        in_specs=[pl.BlockSpec(memory_space=pltpu.SMEM)] + [vmem] * (1 + 3 * chips),
        out_specs=vmem,
        scratch_shapes=[
            pltpu.SMEM((blocks + 1,), jnp.int32),
            pltpu.VMEM((own, features), jnp.float32),
        ],
        compiler_params=pltpu.CompilerParams(vmem_limit_bytes=VMEM_LIMIT),
        name="apply_inverse",
    )(keep_flags, *projected, inverse, *pieces)


def solution(mesh):
    n = mesh.shape["dp"]
    others = range(2, n, 2)

    def swap(x, k):
        return lax.ppermute(x, "dp", [(d, d ^ k) for d in range(n)])

    def on_device(tokens, orig_weight, keep_flags):
        features = tokens.shape[1]
        own = orig_weight.shape[0]
        kept = select_kept(tokens, keep_flags)
        panels = (kept.shape[0] - EXTRA) // PANEL
        half = panels // 2
        same = [kept] + [swap(kept, k) for k in others]
        pieces = []
        for piece in same:
            pieces += [piece, swap(piece, 1)]
        pieces, orig_weight = lax.optimization_barrier((pieces, orig_weight))
        sibling = swap(tokens, 1)
        weights = [orig_weight] + [swap(orig_weight, k) for k in others]
        begun, scale = first_half(pieces, features, half)
        begun, weights, sibling = lax.optimization_barrier((begun, weights, sibling))
        stacked = jnp.concatenate(weights, axis=0)
        projected = [
            lax.dot_general(stacked, part, NT, preferred_element_type=jnp.float32) for part in (tokens, sibling)
        ]
        projected = jnp.concatenate(projected, axis=1)
        begun, projected = lax.optimization_barrier((begun, projected))
        parts = [projected[i * own:(i + 1) * own] for i in range(n // 2)]
        parts = [parts[0]] + [swap(part, k) for part, k in zip(parts[1:], others)]
        inverse = second_half(begun, scale, half)
        return apply_inverse(keep_flags, parts, inverse, pieces, features)

    in_specs = (P("dp", None), P(("section", "dp"), None), P())
    out_specs = P(("section", "dp"), None)
    return jax.shard_map(on_device, mesh=mesh, in_specs=in_specs, out_specs=out_specs, check_vma=False)
```

```python
import functools

import jax
import jax.numpy as jnp
from jax import lax
from jax.experimental import pallas as pl
from jax.experimental.pallas import tpu as pltpu
from jax.sharding import PartitionSpec as P

KEEP_BLK = 12
PANEL = 128
SUB = 8
EXTRA = 16
VMEM_LIMIT = 56 * 1024 * 1024
NT = (((1,), (1,)), ((), ()))
NN = (((1,), (0,)), ((), ()))


def split3(x):
    hi = x.astype(jnp.bfloat16)
    rest = x - hi.astype(jnp.float32)
    mid = rest.astype(jnp.bfloat16)
    low = (rest - mid.astype(jnp.float32)).astype(jnp.bfloat16)
    return hi, mid, low


def dot32(a, b, dims):
    return lax.dot_general(a, b, dims, preferred_element_type=jnp.float32)


def kept_blocks(flags_ref, index_ref):
    count = jnp.int32(0)
    for b in range(flags_ref.shape[0]):
        index_ref[count] = b
        count = count + flags_ref[b]


def select_kernel(flags_ref, tokens_ref, out_ref, index_ref, tile_ref, chunk_ref, tile_sem, chunk_sem):
    rows, features = tokens_ref.shape
    blocks = flags_ref.shape[0]
    width = features // blocks
    per_tile = 128 // width
    chunks = chunk_ref.shape[0]
    step = rows // chunks
    kept_blocks(flags_ref, index_ref)
    tiles = []
    for i in range(KEEP_BLK):
        start = pl.multiple_of((index_ref[i] // per_tile) * 128, 128)
        tiles.append(
            pltpu.make_async_copy(tokens_ref.at[:, pl.ds(start, 128)], tile_ref.at[i], tile_sem.at[i])
        )
        tiles[-1].start()
    reads = []
    for c in range(chunks):
        reads.append(
            pltpu.make_async_copy(tokens_ref.at[c * step:(c + 1) * step, :], chunk_ref.at[c], chunk_sem.at[c])
        )
        reads[-1].start()
    row = lax.broadcasted_iota(jnp.int32, (width, 128), 0)
    lane = lax.broadcasted_iota(jnp.int32, (width, 128), 1)
    for copy in tiles + reads:
        copy.wait()
    for i in range(KEEP_BLK):
        inner = (index_ref[i] % per_tile) * width
        pick = jnp.where(lane == row + inner, 1.0, 0.0).astype(jnp.bfloat16)
        out_ref[i * width:(i + 1) * width, :] = dot32(pick, tile_ref[i], NT).astype(jnp.bfloat16)
    total = jnp.zeros((step, 128), jnp.float32)
    for c in range(chunks):
        for f in range(features // 128):
            piece = chunk_ref[c, :, f * 128:(f + 1) * 128].astype(jnp.float32)
            total += piece * piece
    squares = jnp.sum(total)
    hi, mid, low = split3(jnp.full((EXTRA, rows), squares, jnp.float32))
    row = lax.broadcasted_iota(jnp.int32, (EXTRA, rows), 0)
    carried = jnp.where(
        row == 0,
        hi.astype(jnp.float32),
        jnp.where(row == 1, mid.astype(jnp.float32), jnp.where(row == 2, low.astype(jnp.float32), 0.0)),
    )
    out_ref[KEEP_BLK * width:, :] = carried.astype(jnp.bfloat16)


def select_kept(tokens, keep_flags):
    rows, features = tokens.shape
    blocks = keep_flags.shape[0]
    kept = KEEP_BLK * (features // blocks)
    chunks = 4
    return pl.pallas_call(
        select_kernel,
        out_shape=jax.ShapeDtypeStruct((kept + EXTRA, rows), jnp.bfloat16),
        in_specs=[
            pl.BlockSpec(memory_space=pltpu.SMEM),
            pl.BlockSpec(memory_space=pl.ANY),
        ],
        out_specs=pl.BlockSpec(memory_space=pltpu.VMEM),
        scratch_shapes=[
            pltpu.SMEM((blocks + 1,), jnp.int32),
            pltpu.VMEM((KEEP_BLK, rows, 128), jnp.bfloat16),
            pltpu.VMEM((chunks, rows // chunks, features), jnp.bfloat16),
            pltpu.SemaphoreType.DMA((KEEP_BLK,)),
            pltpu.SemaphoreType.DMA((chunks,)),
        ],
        compiler_params=pltpu.CompilerParams(vmem_limit_bytes=VMEM_LIMIT),
        name="select_kept",
    )(keep_flags, tokens)


def lane_column(x, c):
    return jnp.broadcast_to(x[:, c:c + 1], (SUB, 128))


def sublane_row(x, t):
    return jnp.broadcast_to(x[t:t + 1, :], (SUB, 128))


def tree_sum(terms):
    while len(terms) > 1:
        pairs = [terms[i] + terms[i + 1] for i in range(0, len(terms) - 1, 2)]
        terms = pairs + terms[len(terms) - len(terms) % 2:]
    return terms[0]


def sweep_small(block):
    entry = {}
    for j in range(SUB):
        column = lane_column(block[0], block[1] + j)
        for i in range(j + 1):
            entry[i, j] = sublane_row(column, i)
    r = pl.reciprocal(entry[0, 0], approx=True)
    for t in range(SUB):
        after = None
        if t + 1 < SUB:
            square = entry[t, t + 1] * entry[t, t + 1]
            after = pl.reciprocal(entry[t + 1, t + 1] - square * r, approx=True)
        line = [entry[min(i, t), max(i, t)] for i in range(SUB)]
        scaled = [line[i] * r for i in range(SUB)]
        for j in range(SUB):
            for i in range(j + 1):
                if i != t and j != t:
                    entry[i, j] = entry[i, j] - line[i] * scaled[j]
        for i in range(SUB):
            entry[min(i, t), max(i, t)] = -r if i == t else scaled[i]
        r = after
    return entry


def invert_panel(block):
    size = block.shape[0]
    count = size // SUB
    sub = lax.broadcasted_iota(jnp.int32, (SUB, 128), 0)
    lane = lax.broadcasted_iota(jnp.int32, (SUB, 128), 1)
    rows = [block[i * SUB:(i + 1) * SUB, :] for i in range(count)]
    for s in range(count):
        base = s * SUB
        inside = (lane >= base) & (lane < base + SUB)
        entry = sweep_small((rows[s], base))
        pivot_rows = jnp.where(inside, jnp.where(lane == sub + base, 1.0, 0.0), rows[s])
        spread_in = [sublane_row(pivot_rows, j) for j in range(SUB)]
        spread = [
            tree_sum([entry[min(i, j), max(i, j)] * spread_in[j] for j in range(SUB)]) for i in range(SUB)
        ]
        for i in [(s + d) % count for d in range(1, count)]:
            change = tree_sum([lane_column(rows[i], base + j) * spread[j] for j in range(SUB)])
            rows[i] = jnp.where(inside, 0.0, rows[i]) + change
        new = spread[SUB - 1]
        for j in range(SUB - 1):
            new = jnp.where(sub == j, spread[j], new)
        rows[s] = -new
    return jnp.concatenate(rows, axis=0)


def wide_left(x):
    hi, mid, low = split3(x)
    return jnp.concatenate([hi, hi, mid, hi, mid, low], axis=1)


def wide_right(x):
    hi, mid, low = split3(x)
    return jnp.concatenate([hi, mid, hi, low, mid, hi], axis=0)


def sweep(first, last, a_ref, left_ref, right_ref, scale=None):
    kept = a_ref.shape[0]
    left_ref[...] = jnp.zeros_like(left_ref)
    right_ref[...] = jnp.zeros_like(right_ref)
    row = lax.broadcasted_iota(jnp.int32, (kept, PANEL), 0)

    @pl.loop(first, last)
    def _(p):
        at = pl.multiple_of(p * PANEL, PANEL)
        here = pl.ds(at, PANEL)
        inverse = invert_panel(a_ref[here, here] - dot32(left_ref[here, :], right_ref[:, here], NN))
        for c in range(0, kept, 256):
            a_ref[:, c:c + 256] -= dot32(left_ref[...], right_ref[:, c:c + 256], NN)
        column = jnp.where((row >= at) & (row < at + PANEL), 0.0, a_ref[:, here])
        left_ref[...] = wide_left(column)
        a_ref[:, here] = jnp.zeros((kept, PANEL), jnp.float32)
        wide = wide_left(inverse)
        for c in range(0, kept, 256):
            a_ref[here, c:c + 256] = dot32(wide, wide_right(a_ref[here, c:c + 256]), NN)
        a_ref[here, here] = inverse
        right_ref[...] = wide_right(a_ref[here, :])

    for c in range(0, kept, 256):
        value = a_ref[:, c:c + 256] - dot32(left_ref[...], right_ref[:, c:c + 256], NN)
        a_ref[:, c:c + 256] = value if scale is None else value * scale


def place_pieces(pieces, all_ref, sem):
    copies = []
    at = 0
    for k, piece in enumerate(pieces):
        width = piece.shape[1]
        copies.append(pltpu.make_async_copy(piece, all_ref.at[:, at:at + width], sem.at[k]))
        copies[-1].start()
        at += width
    return copies


def first_kernel(features, rows, last, *refs):
    pieces = refs[:-6]
    out_ref, scale_ref, all_ref, left_ref, right_ref, sem = refs[-6:]
    kept = out_ref.shape[0]
    copies = place_pieces(pieces, all_ref, sem)
    for copy in copies:
        copy.wait()
    tokens = all_ref.shape[1]
    total = jnp.float32(0.0)
    for k in range(0, tokens, rows):
        total = total + jnp.sum(all_ref[kept:, k:k + 1].astype(jnp.float32))
    scale_ref[...] = 1.0 / jnp.full(scale_ref.shape, 0.01 * total / features, jnp.float32)
    scale = scale_ref[0:1, 0:1]
    chunk = 2048 if tokens % 2048 == 0 else rows
    tile = 256
    unit = lax.broadcasted_iota(jnp.int32, (kept, tile), 0) - lax.broadcasted_iota(jnp.int32, (kept, tile), 1)

    @pl.loop(0, kept // tile)
    def _(j):
        at = pl.multiple_of(j * tile, tile)
        acc = jnp.where(unit == at, 1.0, 0.0)
        for c in range(0, tokens, chunk):
            part = dot32(all_ref[:kept, c:c + chunk], all_ref[pl.ds(at, tile), c:c + chunk], NT)
            acc = acc + part * scale
        out_ref[:, pl.ds(at, tile)] = acc

    sweep(0, last, out_ref, left_ref, right_ref)


def first_half(pieces, features, last):
    kept_extra, rows = pieces[0].shape
    kept = kept_extra - EXTRA
    n = len(pieces)
    tokens = sum(piece.shape[1] for piece in pieces)
    return pl.pallas_call(
        functools.partial(first_kernel, float(features), rows, last),
        out_shape=[
            jax.ShapeDtypeStruct((kept, kept), jnp.float32),
            jax.ShapeDtypeStruct((8, 128), jnp.float32),
        ],
        in_specs=[pl.BlockSpec(memory_space=pl.ANY)] * n,
        out_specs=[pl.BlockSpec(memory_space=pltpu.VMEM)] * 2,
        scratch_shapes=[
            pltpu.VMEM((kept_extra, tokens), jnp.bfloat16),
            pltpu.VMEM((kept, 6 * PANEL), jnp.bfloat16),
            pltpu.VMEM((6 * PANEL, kept), jnp.bfloat16),
            pltpu.SemaphoreType.DMA((n,)),
        ],
        compiler_params=pltpu.CompilerParams(vmem_limit_bytes=VMEM_LIMIT),
        name="gram_and_first_panels",
    )(*pieces)


def second_kernel(first, a_ref, scale_ref, out_ref, left_ref, right_ref):
    kept = out_ref.shape[0]
    out_ref[...] = a_ref[...]
    sweep(first, kept // PANEL, out_ref, left_ref, right_ref, scale_ref[0:1, 0:1])


def second_half(a, scale, first):
    kept = a.shape[0]
    vmem = pl.BlockSpec(memory_space=pltpu.VMEM)
    return pl.pallas_call(
        functools.partial(second_kernel, first),
        out_shape=jax.ShapeDtypeStruct((kept, kept), jnp.float32),
        in_specs=[vmem, vmem],
        out_specs=vmem,
        scratch_shapes=[
            pltpu.VMEM((kept, 6 * PANEL), jnp.bfloat16),
            pltpu.VMEM((6 * PANEL, kept), jnp.bfloat16),
        ],
        compiler_params=pltpu.CompilerParams(vmem_limit_bytes=VMEM_LIMIT),
        name="last_panels",
    )(a, scale)


def apply_kernel(chips, flags_ref, *refs):
    projected, refs = refs[:chips], refs[chips:]
    inverse_ref, refs = refs[0], refs[1:]
    pieces, (out_ref, index_ref, wide_ref, all_ref, held_ref, sem, held_sem) = refs[:-7], refs[-7:]
    own, features = out_ref.shape
    blocks = flags_ref.shape[0]
    width = features // blocks
    per_tile = 128 // width
    kept = inverse_ref.shape[0]
    fetch = pltpu.make_async_copy(inverse_ref, held_ref, held_sem)
    fetch.start()
    copies = place_pieces(pieces, all_ref, sem)
    kept_blocks(flags_ref, index_ref)
    wide_ref[...] = jnp.zeros((own, features), jnp.float32)
    split = [split3(part[...]) for part in projected]
    left = jnp.concatenate([jnp.concatenate([s[i] for s in split], axis=1) for i in range(3)], axis=0)
    fetch.wait()
    for copy in copies:
        copy.wait()
    right = dot32(left, all_ref[:kept, :], NT)
    right = right[:own] + right[own:2 * own] + right[2 * own:]
    hi, mid, low = split3(right)
    ihi, imid, ilow = split3(held_ref[...])
    first = dot32(jnp.concatenate([hi, mid, low], axis=0), ihi, NN)
    second = dot32(jnp.concatenate([hi, mid], axis=0), imid, NN)
    third = dot32(hi, ilow, NN)
    answer = first[:own] + first[own:2 * own] + second[:own] + first[2 * own:] + second[own:] + third
    place = lax.broadcasted_iota(jnp.int32, (own, 128), 1) // width
    for i in range(KEEP_BLK):
        b = index_ref[i]
        start = pl.multiple_of((b // per_tile) * 128, 128)
        inner = b % per_tile
        t = i // per_tile
        source = answer[:, t * 128:(t + 1) * 128]
        moved = pltpu.roll(source, width, 1)
        value = jnp.where(inner == i % per_tile, source, moved)
        old = wide_ref[:, pl.ds(start, 128)]
        wide_ref[:, pl.ds(start, 128)] = jnp.where(place == inner, value, old)
    out_ref[...] = wide_ref[...].astype(jnp.bfloat16)


def apply_inverse(keep_flags, projected, inverse, pieces, features):
    own = projected[0].shape[0]
    blocks = keep_flags.shape[0]
    chips = len(projected)
    kept = inverse.shape[0]
    tokens = sum(piece.shape[1] for piece in pieces)
    vmem = pl.BlockSpec(memory_space=pltpu.VMEM)
    anywhere = pl.BlockSpec(memory_space=pl.ANY)
    return pl.pallas_call(
        functools.partial(apply_kernel, chips),
        out_shape=jax.ShapeDtypeStruct((own, features), jnp.bfloat16),
        in_specs=[pl.BlockSpec(memory_space=pltpu.SMEM)] + [vmem] * chips + [anywhere] * (1 + len(pieces)),
        out_specs=vmem,
        scratch_shapes=[
            pltpu.SMEM((blocks + 1,), jnp.int32),
            pltpu.VMEM((own, features), jnp.float32),
            pltpu.VMEM((kept + EXTRA, tokens), jnp.bfloat16),
            pltpu.VMEM((kept, kept), jnp.float32),
            pltpu.SemaphoreType.DMA((len(pieces),)),
            pltpu.SemaphoreType.DMA,
        ],
        compiler_params=pltpu.CompilerParams(vmem_limit_bytes=VMEM_LIMIT),
        name="apply_inverse",
    )(keep_flags, *projected, inverse, *pieces)


def solution(mesh):
    n = mesh.shape["dp"]
    others = range(2, n, 2)

    def swap(x, k):
        return lax.ppermute(x, "dp", [(d, d ^ k) for d in range(n)])

    def gather_kept(kept):
        if n != 8:
            return [[kept]] + [[swap(kept, k)] for k in others]
        near = [swap(kept, 2), swap(kept, 4)]
        middle = kept.shape[1] // 2
        far = [swap(near[0][:, :middle], 4), swap(near[1][:, middle:], 2)]
        return [[kept], [near[0]], [near[1]], far]

    def on_device(tokens, orig_weight, keep_flags):
        features = tokens.shape[1]
        own = orig_weight.shape[0]
        kept = select_kept(tokens, keep_flags)
        panels = (kept.shape[0] - EXTRA) // PANEL
        half = panels // 2
        same = gather_kept(kept)
        same[-1], orig_weight = lax.optimization_barrier((same[-1], orig_weight))
        pieces = []
        for group in same:
            pieces += group + [swap(piece, 1) for piece in group]
        sibling = swap(tokens, 1)
        weights = [orig_weight] + [swap(orig_weight, k) for k in others]
        begun, scale = first_half(pieces, features, half)
        begun, weights, sibling = lax.optimization_barrier((begun, weights, sibling))
        stacked = jnp.concatenate(weights, axis=0)
        projected = [
            lax.dot_general(stacked, part, NT, preferred_element_type=jnp.float32) for part in (tokens, sibling)
        ]
        projected = jnp.concatenate(projected, axis=1)
        begun, projected = lax.optimization_barrier((begun, projected))
        parts = [projected[i * own:(i + 1) * own] for i in range(n // 2)]
        parts = [parts[0]] + [swap(part, k) for part, k in zip(parts[1:], others)]
        inverse = second_half(begun, scale, half)
        return apply_inverse(keep_flags, parts, inverse, pieces, features)

    in_specs = (P("dp", None), P(("section", "dp"), None), P())
    out_specs = P(("section", "dp"), None)
    return jax.shard_map(on_device, mesh=mesh, in_specs=in_specs, out_specs=out_specs, check_vma=False)
```

```python
import functools

import jax
import jax.numpy as jnp
from jax import lax
from jax.experimental import pallas as pl
from jax.experimental.pallas import tpu as pltpu
from jax.sharding import PartitionSpec as P

KEEP_BLK = 12
PANEL = 128
SUB = 8
GROUP = 64
EXTRA = 16
VMEM_LIMIT = 56 * 1024 * 1024
NT = (((1,), (1,)), ((), ()))
NN = (((1,), (0,)), ((), ()))


def split3(x):
    hi = x.astype(jnp.bfloat16)
    rest = x - hi.astype(jnp.float32)
    mid = rest.astype(jnp.bfloat16)
    low = (rest - mid.astype(jnp.float32)).astype(jnp.bfloat16)
    return hi, mid, low


def dot32(a, b, dims):
    return lax.dot_general(a, b, dims, preferred_element_type=jnp.float32)


def kept_blocks(flags_ref, index_ref):
    count = jnp.int32(0)
    for b in range(flags_ref.shape[0]):
        index_ref[count] = b
        count = count + flags_ref[b]


def select_kernel(flags_ref, tokens_ref, out_ref, index_ref, held_ref, sem):
    rows, features = tokens_ref.shape
    blocks = flags_ref.shape[0]
    width = features // blocks
    per_tile = 128 // width
    chunks = sem.shape[0]
    step = rows // chunks
    reads = []
    for c in range(chunks):
        part = pl.ds(c * step, step)
        reads.append(pltpu.make_async_copy(tokens_ref.at[part, :], held_ref.at[part, :], sem.at[c]))
        reads[-1].start()
    kept_blocks(flags_ref, index_ref)
    row = lax.broadcasted_iota(jnp.int32, (width, 128), 0)
    lane = lax.broadcasted_iota(jnp.int32, (width, 128), 1)
    for copy in reads:
        copy.wait()
    for i in range(KEEP_BLK):
        b = index_ref[i]
        start = pl.multiple_of((b // per_tile) * 128, 128)
        pick = jnp.where(lane == row + (b % per_tile) * width, 1.0, 0.0).astype(jnp.bfloat16)
        picked = dot32(pick, held_ref[:, pl.ds(start, 128)], NT)
        out_ref[i * width:(i + 1) * width, :] = picked.astype(jnp.bfloat16)
    total = jnp.zeros((step, 128), jnp.float32)
    for c in range(chunks):
        for f in range(features // 128):
            piece = held_ref[c * step:(c + 1) * step, f * 128:(f + 1) * 128].astype(jnp.float32)
            total += piece * piece
    squares = jnp.sum(total)
    hi, mid, low = split3(jnp.full((EXTRA, rows), squares, jnp.float32))
    row = lax.broadcasted_iota(jnp.int32, (EXTRA, rows), 0)
    carried = jnp.where(
        row == 0,
        hi.astype(jnp.float32),
        jnp.where(row == 1, mid.astype(jnp.float32), jnp.where(row == 2, low.astype(jnp.float32), 0.0)),
    )
    out_ref[KEEP_BLK * width:, :] = carried.astype(jnp.bfloat16)


def select_kept(tokens, keep_flags):
    rows, features = tokens.shape
    blocks = keep_flags.shape[0]
    kept = KEEP_BLK * (features // blocks)
    chunks = 4
    return pl.pallas_call(
        select_kernel,
        out_shape=jax.ShapeDtypeStruct((kept + EXTRA, rows), jnp.bfloat16),
        in_specs=[
            pl.BlockSpec(memory_space=pltpu.SMEM),
            pl.BlockSpec(memory_space=pl.ANY),
        ],
        out_specs=pl.BlockSpec(memory_space=pltpu.VMEM),
        scratch_shapes=[
            pltpu.SMEM((blocks + 1,), jnp.int32),
            pltpu.VMEM((rows, features), jnp.bfloat16),
            pltpu.SemaphoreType.DMA((chunks,)),
        ],
        compiler_params=pltpu.CompilerParams(vmem_limit_bytes=VMEM_LIMIT),
        name="select_kept",
    )(keep_flags, tokens)


def lane_column(x, c):
    return jnp.broadcast_to(x[:, c:c + 1], (SUB, 128))


def sublane_row(x, t):
    return jnp.broadcast_to(x[t:t + 1, :], (SUB, 128))


def tree_sum(terms):
    while len(terms) > 1:
        pairs = [terms[i] + terms[i + 1] for i in range(0, len(terms) - 1, 2)]
        terms = pairs + terms[len(terms) - len(terms) % 2:]
    return terms[0]


def solve_small(block, base, rows):
    entry = {}
    for j in range(SUB):
        column = lane_column(block, base + j)
        for i in range(j + 1):
            entry[i, j] = sublane_row(column, i)
    rows = list(rows)
    r = pl.reciprocal(entry[0, 0], approx=True)
    scaled = {}
    for t in range(SUB):
        after = None
        if t + 1 < SUB:
            square = entry[t, t + 1] * entry[t, t + 1]
            after = pl.reciprocal(entry[t + 1, t + 1] - square * r, approx=True)
        for j in range(t + 1, SUB):
            scaled[t, j] = entry[t, j] * r
        for j in range(t + 1, SUB):
            for i in range(t + 1, j + 1):
                entry[i, j] = entry[i, j] - entry[t, i] * scaled[t, j]
            rows[j] = rows[j] - scaled[t, j] * rows[t]
        rows[t] = rows[t] * r
        r = after
    for t in reversed(range(SUB)):
        for j in range(t):
            rows[j] = rows[j] - scaled[j, t] * rows[t]
    return rows


def invert_rows(rows, first, sub, lane, beside):
    count = len(rows)
    for s in range(count):
        base = (first + s) * SUB
        inside = (lane >= base) & (lane < base + SUB)
        pivot_rows = jnp.where(inside, jnp.where(lane == sub + base, 1.0, 0.0), rows[s])
        spread = solve_small(rows[s], base, [sublane_row(pivot_rows, j) for j in range(SUB)])
        for i in [(s + d) % count for d in range(1, count)]:
            change = tree_sum([lane_column(rows[i], base + j) * spread[j] for j in range(SUB)])
            rows[i] = jnp.where(inside, 0.0, rows[i]) - change
        new = spread[SUB - 1]
        for j in range(SUB - 1):
            new = jnp.where(sub == j, spread[j], new)
        rows[s] = new
        if beside:
            beside.pop(0)()
    return rows


def invert_panel(block, beside):
    size = block.shape[0]
    sub = lax.broadcasted_iota(jnp.int32, (SUB, 128), 0)
    lane = lax.broadcasted_iota(jnp.int32, (SUB, 128), 1)
    row_at = lax.broadcasted_iota(jnp.int32, (size, size), 0) // GROUP
    lane_at = lax.broadcasted_iota(jnp.int32, (size, size), 1) // GROUP
    for g in range(size // GROUP):
        low = g * GROUP
        rows = [block[low + i:low + i + SUB, :] for i in range(0, GROUP, SUB)]
        rows = invert_rows(rows, low // SUB, sub, lane, beside)
        group = jnp.concatenate(rows, axis=0)
        parts = [jnp.zeros((low, size), jnp.float32)] * (g > 0) + [group]
        parts += [jnp.zeros((size - low - GROUP, size), jnp.float32)] * (low + GROUP < size)
        full = jnp.concatenate(parts, axis=0)
        column = jnp.where((lane_at == g) & (row_at != g), block, 0.0)
        kept = jnp.where((lane_at == g) | (row_at == g), 0.0, block)
        block = kept + full - dot32(wide_left(column), wide_right(full), NN)
    return block


def wide_left(x):
    hi, mid, low = split3(x)
    return jnp.concatenate([hi, hi, mid, hi, mid, low], axis=1)


def wide_right(x):
    hi, mid, low = split3(x)
    return jnp.concatenate([hi, mid, hi, low, mid, hi], axis=0)


def sweep(first, last, a_ref, left_ref, right_ref, scale=None):
    kept = a_ref.shape[0]
    left_ref[...] = jnp.zeros_like(left_ref)
    right_ref[...] = jnp.zeros_like(right_ref)
    row = lax.broadcasted_iota(jnp.int32, (kept, PANEL), 0)

    @pl.loop(first, last)
    def _(p):
        at = pl.multiple_of(p * PANEL, PANEL)
        here = pl.ds(at, PANEL)

        def update(r, c, half):
            a_ref[r:r + half, c:c + 256] -= dot32(left_ref[r:r + half, :], right_ref[:, c:c + 256], NN)

        beside = []
        for c in range(0, kept, 256):
            for r in range(0, kept, kept // 2):
                beside += [functools.partial(update, r, c, kept // 2), lambda: None]
        start = a_ref[here, here] - dot32(left_ref[here, :], right_ref[:, here], NN)
        inverse = invert_panel(start, beside)
        column = jnp.where((row >= at) & (row < at + PANEL), 0.0, a_ref[:, here])
        left_ref[...] = wide_left(column)
        a_ref[:, here] = jnp.zeros((kept, PANEL), jnp.float32)
        wide = wide_left(inverse)
        for c in range(0, kept, 256):
            a_ref[here, c:c + 256] = dot32(wide, wide_right(a_ref[here, c:c + 256]), NN)
        a_ref[here, here] = inverse
        right_ref[...] = wide_right(a_ref[here, :])

    for c in range(0, kept, 256):
        value = a_ref[:, c:c + 256] - dot32(left_ref[...], right_ref[:, c:c + 256], NN)
        a_ref[:, c:c + 256] = value if scale is None else value * scale


def place_pieces(pieces, all_ref, sem):
    copies = []
    at = 0
    for k, piece in enumerate(pieces):
        width = piece.shape[1]
        copies.append(pltpu.make_async_copy(piece, all_ref.at[:, at:at + width], sem.at[k]))
        copies[-1].start()
        at += width
    return copies


def first_kernel(features, rows, last, *refs):
    pieces = refs[:-6]
    out_ref, scale_ref, all_ref, left_ref, right_ref, sem = refs[-6:]
    kept = out_ref.shape[0]
    copies = place_pieces(pieces, all_ref, sem)
    for copy in copies:
        copy.wait()
    tokens = all_ref.shape[1]
    total = jnp.float32(0.0)
    for k in range(0, tokens, rows):
        total = total + jnp.sum(all_ref[kept:, k:k + 1].astype(jnp.float32))
    scale_ref[...] = 1.0 / jnp.full(scale_ref.shape, 0.01 * total / features, jnp.float32)
    scale = scale_ref[0:1, 0:1]
    chunk = 2048 if tokens % 2048 == 0 else rows
    tile = 256
    unit = lax.broadcasted_iota(jnp.int32, (kept, tile), 0) - lax.broadcasted_iota(jnp.int32, (kept, tile), 1)

    @pl.loop(0, kept // tile)
    def _(j):
        at = pl.multiple_of(j * tile, tile)
        acc = jnp.where(unit == at, 1.0, 0.0)
        for c in range(0, tokens, chunk):
            part = dot32(all_ref[:kept, c:c + chunk], all_ref[pl.ds(at, tile), c:c + chunk], NT)
            acc = acc + part * scale
        out_ref[:, pl.ds(at, tile)] = acc

    sweep(0, last, out_ref, left_ref, right_ref)


def first_half(pieces, features, last):
    kept_extra, rows = pieces[0].shape
    kept = kept_extra - EXTRA
    n = len(pieces)
    tokens = sum(piece.shape[1] for piece in pieces)
    return pl.pallas_call(
        functools.partial(first_kernel, float(features), rows, last),
        out_shape=[
            jax.ShapeDtypeStruct((kept, kept), jnp.float32),
            jax.ShapeDtypeStruct((8, 128), jnp.float32),
        ],
        in_specs=[pl.BlockSpec(memory_space=pl.ANY)] * n,
        out_specs=[pl.BlockSpec(memory_space=pltpu.VMEM)] * 2,
        scratch_shapes=[
            pltpu.VMEM((kept_extra, tokens), jnp.bfloat16),
            pltpu.VMEM((kept, 6 * PANEL), jnp.bfloat16),
            pltpu.VMEM((6 * PANEL, kept), jnp.bfloat16),
            pltpu.SemaphoreType.DMA((n,)),
        ],
        compiler_params=pltpu.CompilerParams(vmem_limit_bytes=VMEM_LIMIT),
        name="gram_and_first_panels",
    )(*pieces)


def second_kernel(first, a_ref, scale_ref, out_ref, left_ref, right_ref):
    kept = out_ref.shape[0]
    out_ref[...] = a_ref[...]
    sweep(first, kept // PANEL, out_ref, left_ref, right_ref, scale_ref[0:1, 0:1])


def second_half(a, scale, first):
    kept = a.shape[0]
    vmem = pl.BlockSpec(memory_space=pltpu.VMEM)
    return pl.pallas_call(
        functools.partial(second_kernel, first),
        out_shape=jax.ShapeDtypeStruct((kept, kept), jnp.float32),
        in_specs=[vmem, vmem],
        out_specs=vmem,
        scratch_shapes=[
            pltpu.VMEM((kept, 6 * PANEL), jnp.bfloat16),
            pltpu.VMEM((6 * PANEL, kept), jnp.bfloat16),
        ],
        compiler_params=pltpu.CompilerParams(vmem_limit_bytes=VMEM_LIMIT),
        name="last_panels",
    )(a, scale)


def apply_kernel(chips, flags_ref, *refs):
    projected, refs = refs[:chips], refs[chips:]
    inverse_ref, refs = refs[0], refs[1:]
    pieces, (out_ref, index_ref, wide_ref, all_ref, held_ref, sem, held_sem) = refs[:-7], refs[-7:]
    own, features = out_ref.shape
    blocks = flags_ref.shape[0]
    width = features // blocks
    per_tile = 128 // width
    kept = inverse_ref.shape[0]
    fetch = pltpu.make_async_copy(inverse_ref, held_ref, held_sem)
    fetch.start()
    copies = place_pieces(pieces, all_ref, sem)
    kept_blocks(flags_ref, index_ref)
    wide_ref[...] = jnp.zeros((own, features), jnp.float32)
    whole = jnp.concatenate([part[...] for part in projected], axis=1)
    left = jnp.concatenate(split3(whole), axis=0)
    for copy in copies:
        copy.wait()
    right = dot32(all_ref[:kept, :], left, NT)
    right = right[:, :own] + right[:, own:2 * own] + right[:, 2 * own:]
    hi, mid, low = split3(right)
    fetch.wait()
    ihi, imid, ilow = split3(held_ref[...])
    first = dot32(ihi, jnp.concatenate([hi, mid, low], axis=1), NN)
    second = dot32(imid, jnp.concatenate([hi, mid], axis=1), NN)
    third = dot32(ilow, hi, NN)
    answer = first[:, 2 * own:] + second[:, own:] + third + first[:, own:2 * own] + second[:, :own] + first[:, :own]
    answer = answer.T
    place = lax.broadcasted_iota(jnp.int32, (own, 128), 1) // width
    for i in range(KEEP_BLK):
        b = index_ref[i]
        start = pl.multiple_of((b // per_tile) * 128, 128)
        inner = b % per_tile
        t = i // per_tile
        source = answer[:, t * 128:(t + 1) * 128]
        moved = pltpu.roll(source, width, 1)
        value = jnp.where(inner == i % per_tile, source, moved)
        old = wide_ref[:, pl.ds(start, 128)]
        wide_ref[:, pl.ds(start, 128)] = jnp.where(place == inner, value, old)
    out_ref[...] = wide_ref[...].astype(jnp.bfloat16)


def apply_inverse(keep_flags, projected, inverse, pieces, features):
    own = projected[0].shape[0]
    blocks = keep_flags.shape[0]
    chips = len(projected)
    kept = inverse.shape[0]
    tokens = sum(piece.shape[1] for piece in pieces)
    vmem = pl.BlockSpec(memory_space=pltpu.VMEM)
    anywhere = pl.BlockSpec(memory_space=pl.ANY)
    return pl.pallas_call(
        functools.partial(apply_kernel, chips),
        out_shape=jax.ShapeDtypeStruct((own, features), jnp.bfloat16),
        in_specs=[pl.BlockSpec(memory_space=pltpu.SMEM)] + [vmem] * chips + [anywhere] * (1 + len(pieces)),
        out_specs=vmem,
        scratch_shapes=[
            pltpu.SMEM((blocks + 1,), jnp.int32),
            pltpu.VMEM((own, features), jnp.float32),
            pltpu.VMEM((kept + EXTRA, tokens), jnp.bfloat16),
            pltpu.VMEM((kept, kept), jnp.float32),
            pltpu.SemaphoreType.DMA((len(pieces),)),
            pltpu.SemaphoreType.DMA,
        ],
        compiler_params=pltpu.CompilerParams(vmem_limit_bytes=VMEM_LIMIT),
        name="apply_inverse",
    )(keep_flags, *projected, inverse, *pieces)


def solution(mesh):
    n = mesh.shape["dp"]
    others = range(2, n, 2)

    def swap(x, k):
        return lax.ppermute(x, "dp", [(d, d ^ k) for d in range(n)])

    def gather_kept(kept):
        if n != 8:
            return [[kept]] + [[swap(kept, k)] for k in others]
        near = [swap(kept, 2), swap(kept, 4)]
        middle = kept.shape[1] // 2
        far = [swap(near[0][:, :middle], 4), swap(near[1][:, middle:], 2)]
        return [[kept], [near[0]], [near[1]], far]

    def on_device(tokens, orig_weight, keep_flags):
        features = tokens.shape[1]
        own = orig_weight.shape[0]
        kept = select_kept(tokens, keep_flags)
        panels = (kept.shape[0] - EXTRA) // PANEL
        half = panels // 2
        same = gather_kept(kept)
        same[-1], orig_weight = lax.optimization_barrier((same[-1], orig_weight))
        pieces = []
        for group in same:
            pieces += group + [swap(piece, 1) for piece in group]
        sibling = swap(tokens, 1)
        weights = [orig_weight] + [swap(orig_weight, k) for k in others]
        begun, scale = first_half(pieces, features, half)
        begun, weights, sibling = lax.optimization_barrier((begun, weights, sibling))
        stacked = jnp.concatenate(weights, axis=0)
        projected = [
            lax.dot_general(stacked, part, NT, preferred_element_type=jnp.float32) for part in (tokens, sibling)
        ]
        projected = jnp.concatenate(projected, axis=1)
        begun, projected = lax.optimization_barrier((begun, projected))
        parts = [projected[i * own:(i + 1) * own] for i in range(n // 2)]
        parts = [parts[0]] + [swap(part, k) for part, k in zip(parts[1:], others)]
        inverse = second_half(begun, scale, half)
        return apply_inverse(keep_flags, parts, inverse, pieces, features)

    in_specs = (P("dp", None), P(("section", "dp"), None), P())
    out_specs = P(("section", "dp"), None)
    return jax.shard_map(on_device, mesh=mesh, in_specs=in_specs, out_specs=out_specs, check_vma=False)
```

```python
import functools

import jax
import jax.numpy as jnp
from jax import lax
from jax.experimental import pallas as pl
from jax.experimental.pallas import tpu as pltpu
from jax.sharding import PartitionSpec as P

KEEP_BLK = 12
PANEL = 128
SUB = 8
EXTRA = 16
VMEM_LIMIT = 32 * 1024 * 1024
NT = (((1,), (1,)), ((), ()))
NN = (((1,), (0,)), ((), ()))


def split3(x):
    hi = x.astype(jnp.bfloat16)
    rest = x - hi.astype(jnp.float32)
    mid = rest.astype(jnp.bfloat16)
    low = (rest - mid.astype(jnp.float32)).astype(jnp.bfloat16)
    return hi, mid, low


def dot32(a, b, dims):
    return lax.dot_general(a, b, dims, preferred_element_type=jnp.float32)


def kept_blocks(flags_ref, index_ref):
    count = jnp.int32(0)
    for b in range(flags_ref.shape[0]):
        index_ref[count] = b
        count = count + flags_ref[b]


def select_kernel(flags_ref, tokens_ref, out_ref, index_ref, held_ref, sem):
    rows, features = tokens_ref.shape
    blocks = flags_ref.shape[0]
    width = features // blocks
    per_tile = 128 // width
    chunks = sem.shape[0]
    step = rows // chunks
    reads = []
    for c in range(chunks):
        part = pl.ds(c * step, step)
        reads.append(pltpu.make_async_copy(tokens_ref.at[part, :], held_ref.at[part, :], sem.at[c]))
        reads[-1].start()
    kept_blocks(flags_ref, index_ref)
    row = lax.broadcasted_iota(jnp.int32, (width, 128), 0)
    lane = lax.broadcasted_iota(jnp.int32, (width, 128), 1)
    for copy in reads:
        copy.wait()
    for i in range(KEEP_BLK):
        b = index_ref[i]
        start = pl.multiple_of((b // per_tile) * 128, 128)
        pick = jnp.where(lane == row + (b % per_tile) * width, 1.0, 0.0).astype(jnp.bfloat16)
        picked = dot32(pick, held_ref[:, pl.ds(start, 128)], NT)
        out_ref[i * width:(i + 1) * width, :] = picked.astype(jnp.bfloat16)
    total = jnp.zeros((step, 128), jnp.float32)
    for c in range(chunks):
        for f in range(features // 128):
            piece = held_ref[c * step:(c + 1) * step, f * 128:(f + 1) * 128].astype(jnp.float32)
            total += piece * piece
    squares = jnp.sum(total)
    hi, mid, low = split3(jnp.full((EXTRA, rows), squares, jnp.float32))
    row = lax.broadcasted_iota(jnp.int32, (EXTRA, rows), 0)
    carried = jnp.where(
        row == 0,
        hi.astype(jnp.float32),
        jnp.where(row == 1, mid.astype(jnp.float32), jnp.where(row == 2, low.astype(jnp.float32), 0.0)),
    )
    out_ref[KEEP_BLK * width:, :] = carried.astype(jnp.bfloat16)


def select_kept(tokens, keep_flags):
    rows, features = tokens.shape
    blocks = keep_flags.shape[0]
    kept = KEEP_BLK * (features // blocks)
    chunks = 4
    return pl.pallas_call(
        select_kernel,
        out_shape=jax.ShapeDtypeStruct((kept + EXTRA, rows), jnp.bfloat16),
        in_specs=[
            pl.BlockSpec(memory_space=pltpu.SMEM),
            pl.BlockSpec(memory_space=pl.ANY),
        ],
        out_specs=pl.BlockSpec(memory_space=pltpu.VMEM),
        scratch_shapes=[
            pltpu.SMEM((blocks + 1,), jnp.int32),
            pltpu.VMEM((rows, features), jnp.bfloat16),
            pltpu.SemaphoreType.DMA((chunks,)),
        ],
        compiler_params=pltpu.CompilerParams(vmem_limit_bytes=VMEM_LIMIT),
        name="select_kept",
    )(keep_flags, tokens)


def lane_column(x, c):
    return jnp.broadcast_to(x[:, c:c + 1], (SUB, 128))


def sublane_row(x, t):
    return jnp.broadcast_to(x[t:t + 1, :], (SUB, 128))


def tree_sum(terms):
    while len(terms) > 1:
        pairs = [terms[i] + terms[i + 1] for i in range(0, len(terms) - 1, 2)]
        terms = pairs + terms[len(terms) - len(terms) % 2:]
    return terms[0]


def solve_small(block, base, rows):
    entry = {}
    for j in range(SUB):
        column = lane_column(block, base + j)
        for i in range(j + 1):
            entry[i, j] = sublane_row(column, i)
    rows = list(rows)
    inverse = {}
    for t in range(0, SUB, 2):
        u = t + 1
        a, b, c = entry[t, t], entry[t, u], entry[u, u]
        first = pl.reciprocal(a, approx=True)
        second = a * pl.reciprocal(a * c - b * b, approx=True)
        step = b * first
        later = range(u + 1, SUB)
        one = {j: entry[t, j] * first for j in later}
        rest = {j: entry[u, j] - b * one[j] for j in later}
        for j in later:
            for i in range(u + 1, j + 1):
                partial = entry[i, j] - entry[t, i] * one[j]
                entry[i, j] = partial - (rest[i] * rest[j]) * second
        two = {j: rest[j] * second for j in later}
        rows[u] = rows[u] - step * rows[t]
        inverse[u, t] = -step
        for k in range(t):
            inverse[u, k] = inverse[u, k] - step * inverse[t, k]
        for j in later:
            rows[j] = (rows[j] - one[j] * rows[t]) - two[j] * rows[u]
            for k in range(t):
                inverse[j, k] = (inverse[j, k] - one[j] * inverse[t, k]) - two[j] * inverse[u, k]
            inverse[j, t] = -one[j] - two[j] * inverse[u, t]
            inverse[j, u] = -two[j]
        rows[t] = rows[t] * first
        rows[u] = rows[u] * second
    return [
        tree_sum([rows[i]] + [inverse[j, i] * rows[j] for j in range(i + 1, SUB)]) for i in range(SUB)
    ]


def invert_panel(block, beside=()):
    size = block.shape[0]
    count = size // SUB
    beside = list(beside)
    sub = lax.broadcasted_iota(jnp.int32, (SUB, 128), 0)
    lane = lax.broadcasted_iota(jnp.int32, (SUB, 128), 1)
    rows = [block[i * SUB:(i + 1) * SUB, :] for i in range(count)]
    for s in range(count):
        base = s * SUB
        inside = (lane >= base) & (lane < base + SUB)
        pivot_rows = jnp.where(inside, jnp.where(lane == sub + base, 1.0, 0.0), rows[s])
        spread = solve_small(rows[s], base, [sublane_row(pivot_rows, j) for j in range(SUB)])
        for i in [(s + d) % count for d in range(1, count)]:
            change = tree_sum([lane_column(rows[i], base + j) * spread[j] for j in range(SUB)])
            rows[i] = jnp.where(inside, 0.0, rows[i]) - change
        new = spread[SUB - 1]
        for j in range(SUB - 1):
            new = jnp.where(sub == j, spread[j], new)
        rows[s] = new
        if beside:
            beside.pop(0)()
    return jnp.concatenate(rows, axis=0)


def wide_left(x):
    hi, mid, low = split3(x)
    return jnp.concatenate([hi, hi, mid, hi, mid, low], axis=1)


def wide_right(x):
    hi, mid, low = split3(x)
    return jnp.concatenate([hi, mid, hi, low, mid, hi], axis=0)


def pending_updates(a_ref, left_ref, right_ref):
    kept = a_ref.shape[0]
    half = kept // 2

    def update(r, c):
        a_ref[r:r + half, c:c + 256] -= dot32(left_ref[r:r + half, :], right_ref[:, c:c + 256], NN)

    return [functools.partial(update, r, c) for c in range(0, kept, 256) for r in range(0, kept, half)]


def sweep(first, last, a_ref, left_ref, right_ref):
    kept = a_ref.shape[0]
    left_ref[...] = jnp.zeros_like(left_ref)
    right_ref[...] = jnp.zeros_like(right_ref)
    row = lax.broadcasted_iota(jnp.int32, (kept, PANEL), 0)

    @pl.loop(first, last)
    def _(p):
        at = pl.multiple_of(p * PANEL, PANEL)
        here = pl.ds(at, PANEL)
        start = a_ref[here, here] - dot32(left_ref[here, :], right_ref[:, here], NN)
        inverse = invert_panel(start, pending_updates(a_ref, left_ref, right_ref))
        column = jnp.where((row >= at) & (row < at + PANEL), 0.0, a_ref[:, here])
        left_ref[...] = wide_left(column)
        a_ref[:, here] = jnp.zeros((kept, PANEL), jnp.float32)
        wide = wide_left(inverse)
        for c in range(0, kept, 256):
            a_ref[here, c:c + 256] = dot32(wide, wide_right(a_ref[here, c:c + 256]), NN)
        a_ref[here, here] = inverse
        right_ref[...] = wide_right(a_ref[here, :])


def place_pieces(pieces, all_ref, sem):
    copies = []
    at = 0
    for k, piece in enumerate(pieces):
        width = piece.shape[1]
        copies.append(pltpu.make_async_copy(piece, all_ref.at[:, at:at + width], sem.at[k]))
        copies[-1].start()
        at += width
    return copies


def first_kernel(features, rows, last, *refs):
    pieces = refs[:-6]
    out_ref, scale_ref, all_ref, left_ref, right_ref, sem = refs[-6:]
    kept = out_ref.shape[0]
    copies = place_pieces(pieces, all_ref, sem)
    for copy in copies:
        copy.wait()
    tokens = all_ref.shape[1]
    total = jnp.float32(0.0)
    for k in range(0, tokens, rows):
        total = total + jnp.sum(all_ref[kept:, k:k + 1].astype(jnp.float32))
    scale_ref[...] = 1.0 / jnp.full(scale_ref.shape, 0.01 * total / features, jnp.float32)
    scale = scale_ref[0:1, 0:1]
    chunk = 2048 if tokens % 2048 == 0 else rows
    tile = 256
    unit = lax.broadcasted_iota(jnp.int32, (kept, tile), 0) - lax.broadcasted_iota(jnp.int32, (kept, tile), 1)

    @pl.loop(0, kept // tile)
    def _(j):
        at = pl.multiple_of(j * tile, tile)
        acc = jnp.where(unit == at, 1.0, 0.0)
        for c in range(0, tokens, chunk):
            part = dot32(all_ref[:kept, c:c + chunk], all_ref[pl.ds(at, tile), c:c + chunk], NT)
            acc = acc + part * scale
        out_ref[:, pl.ds(at, tile)] = acc

    sweep(0, last, out_ref, left_ref, right_ref)
    for update in pending_updates(out_ref, left_ref, right_ref):
        update()


def first_half(pieces, features, last):
    kept_extra, rows = pieces[0].shape
    kept = kept_extra - EXTRA
    n = len(pieces)
    tokens = sum(piece.shape[1] for piece in pieces)
    return pl.pallas_call(
        functools.partial(first_kernel, float(features), rows, last),
        out_shape=[
            jax.ShapeDtypeStruct((kept, kept), jnp.float32),
            jax.ShapeDtypeStruct((8, 128), jnp.float32),
        ],
        in_specs=[pl.BlockSpec(memory_space=pl.ANY)] * n,
        out_specs=[pl.BlockSpec(memory_space=pltpu.VMEM)] * 2,
        scratch_shapes=[
            pltpu.VMEM((kept_extra, tokens), jnp.bfloat16),
            pltpu.VMEM((kept, 6 * PANEL), jnp.bfloat16),
            pltpu.VMEM((6 * PANEL, kept), jnp.bfloat16),
            pltpu.SemaphoreType.DMA((n,)),
        ],
        compiler_params=pltpu.CompilerParams(vmem_limit_bytes=VMEM_LIMIT),
        name="gram_and_first_panels",
    )(*pieces)


def dot_small(x, y):
    rows = x.shape[0]
    hi, mid, low = split3(x)
    yhi, ymid, ylow = split3(y)
    first = dot32(jnp.concatenate([hi, mid, low], axis=0), yhi, NN)
    second = dot32(jnp.concatenate([hi, mid], axis=0), ymid, NN)
    third = dot32(hi, ylow, NN)
    small = first[2 * rows:] + second[rows:] + third
    return small + (first[rows:2 * rows] + second[:rows]) + first[:rows]


def second_kernel(chips, first, copies, flags_ref, *refs):
    projected, refs = refs[:chips], refs[chips:]
    start_ref, scale_ref, refs = refs[0], refs[1], refs[2:]
    pieces, refs = refs[:-7], refs[-7:]
    out_ref, index_ref, wide_ref, all_ref, a_ref, left_ref, right_ref = refs[:7]
    own, features = out_ref.shape
    blocks = flags_ref.shape[0]
    width = features // blocks
    per_tile = 128 // width
    kept = a_ref.shape[0]
    kept_blocks(flags_ref, index_ref)
    wide_ref[...] = jnp.zeros((own, features), jnp.float32)
    a_ref[...] = start_ref[...]
    last = kept // PANEL - 1
    sweep(first, last, a_ref, left_ref, right_ref)
    for copy in copies:
        copy.wait()

    at = last * PANEL
    held = {}

    def make_right():
        whole = jnp.concatenate([part[...] for part in projected], axis=1)
        right = dot32(jnp.concatenate(split3(whole), axis=0), all_ref[:kept, :], NT)
        held["right"] = right[:own] + right[own:2 * own] + right[2 * own:]

    def make_tail():
        held["tail"] = held["right"][:, at:] - dot_small(held["right"][:, :at], a_ref[:at, at:])

    def make_base(c):
        held[c] = dot_small(held["right"][:, :at], a_ref[:at, c:c + PANEL])

    work = pending_updates(a_ref, left_ref, right_ref) + [make_right, make_tail]
    work += [functools.partial(make_base, c) for c in range(0, at, PANEL)]
    start = a_ref[at:, at:] - dot32(left_ref[at:, :], right_ref[:, at:], NN)
    inverse = invert_panel(start, work)
    tail = dot_small(held["tail"], inverse)
    scale = scale_ref[0:1, 0:1]
    answer = [(held[c] + dot_small(tail, a_ref[at:, c:c + PANEL])) * scale for c in range(0, at, PANEL)]
    answer.append(tail * scale)
    place = lax.broadcasted_iota(jnp.int32, (own, 128), 1) // width
    for i in range(KEEP_BLK):
        b = index_ref[i]
        start = pl.multiple_of((b // per_tile) * 128, 128)
        inner = b % per_tile
        source = answer[i // per_tile]
        moved = pltpu.roll(source, width, 1)
        value = jnp.where(inner == i % per_tile, source, moved)
        old = wide_ref[:, pl.ds(start, 128)]
        wide_ref[:, pl.ds(start, 128)] = jnp.where(place == inner, value, old)
    out_ref[...] = wide_ref[...].astype(jnp.bfloat16)


def second_half(keep_flags, projected, a, scale, pieces, features, first):
    own = projected[0].shape[0]
    blocks = keep_flags.shape[0]
    chips = len(projected)
    kept = a.shape[0]
    count = len(pieces)
    tokens = sum(piece.shape[1] for piece in pieces)
    vmem = pl.BlockSpec(memory_space=pltpu.VMEM)
    anywhere = pl.BlockSpec(memory_space=pl.ANY)

    def body(*refs):
        refs, sem = refs[:-1], refs[-1]
        ins = 3 + chips
        copies = place_pieces(refs[ins:ins + count], refs[ins + count + 3], sem)
        second_kernel(chips, first, copies, *refs)

    return pl.pallas_call(
        body,
        out_shape=jax.ShapeDtypeStruct((own, features), jnp.bfloat16),
        in_specs=[pl.BlockSpec(memory_space=pltpu.SMEM)] + [vmem] * (chips + 2) + [anywhere] * count,
        out_specs=vmem,
        scratch_shapes=[
            pltpu.SMEM((blocks + 1,), jnp.int32),
            pltpu.VMEM((own, features), jnp.float32),
            pltpu.VMEM((kept + EXTRA, tokens), jnp.bfloat16),
            pltpu.VMEM((kept, kept), jnp.float32),
            pltpu.VMEM((kept, 6 * PANEL), jnp.bfloat16),
            pltpu.VMEM((6 * PANEL, kept), jnp.bfloat16),
            pltpu.SemaphoreType.DMA((count,)),
        ],
        compiler_params=pltpu.CompilerParams(vmem_limit_bytes=VMEM_LIMIT),
        name="last_panels_and_solution",
    )(keep_flags, *projected, a, scale, *pieces)


def solution(mesh):
    n = mesh.shape["dp"]
    others = range(2, n, 2)

    def swap(x, k):
        return lax.ppermute(x, "dp", [(d, d ^ k) for d in range(n)])

    def gather_kept(kept):
        if n != 8:
            return [[kept]] + [[swap(kept, k)] for k in others]
        near = [swap(kept, 2), swap(kept, 4)]
        middle = kept.shape[1] // 2
        far = [swap(near[0][:, :middle], 4), swap(near[1][:, middle:], 2)]
        return [[kept], [near[0]], [near[1]], far]

    def on_device(tokens, orig_weight, keep_flags):
        features = tokens.shape[1]
        own = orig_weight.shape[0]
        kept = select_kept(tokens, keep_flags)
        panels = (kept.shape[0] - EXTRA) // PANEL
        half = panels // 2
        same = gather_kept(kept)
        same[-1], orig_weight = lax.optimization_barrier((same[-1], orig_weight))
        pieces = []
        for group in same:
            pieces += group + [swap(piece, 1) for piece in group]
        sibling = swap(tokens, 1)
        groups = [list(range(core, n, 2)) for core in range(2)]
        weights = lax.all_gather(orig_weight, "dp", axis=0, tiled=True, axis_index_groups=groups)
        begun, scale = first_half(pieces, features, half)
        begun, weights, sibling = lax.optimization_barrier((begun, weights, sibling))
        projected = [
            lax.dot_general(weights, part, NT, preferred_element_type=jnp.float32) for part in (tokens, sibling)
        ]
        projected = jnp.concatenate(projected, axis=1)
        chip = lax.axis_index("dp") // 2
        parts = []
        for k in range(0, n, 2):
            part = lax.dynamic_slice_in_dim(projected, (chip ^ (k // 2)) * own, own, axis=0)
            parts.append(swap(part, k) if k else part)
        return second_half(keep_flags, parts, begun, scale, pieces, features, half)

    in_specs = (P("dp", None), P(("section", "dp"), None), P())
    out_specs = P(("section", "dp"), None)
    return jax.shard_map(on_device, mesh=mesh, in_specs=in_specs, out_specs=out_specs, check_vma=False)
```

```python
import functools

import jax
import jax.numpy as jnp
from jax import lax
from jax.experimental import pallas as pl
from jax.experimental.pallas import tpu as pltpu
from jax.sharding import PartitionSpec as P

KEEP_BLK = 12
PANEL = 128
SUB = 8
EXTRA = 16
VMEM_LIMIT = 32 * 1024 * 1024
NT = (((1,), (1,)), ((), ()))
NN = (((1,), (0,)), ((), ()))


def split3(x):
    hi = x.astype(jnp.bfloat16)
    rest = x - hi.astype(jnp.float32)
    mid = rest.astype(jnp.bfloat16)
    low = (rest - mid.astype(jnp.float32)).astype(jnp.bfloat16)
    return hi, mid, low


def dot32(a, b, dims):
    return lax.dot_general(a, b, dims, preferred_element_type=jnp.float32)


def kept_blocks(flags_ref, index_ref):
    count = jnp.int32(0)
    for b in range(flags_ref.shape[0]):
        index_ref[count] = b
        count = count + flags_ref[b]


def select_kernel(flags_ref, tokens_ref, out_ref, index_ref, held_ref, sem):
    rows, features = tokens_ref.shape
    blocks = flags_ref.shape[0]
    width = features // blocks
    per_tile = 128 // width
    chunks = sem.shape[0]
    step = rows // chunks
    reads = []
    for c in range(chunks):
        part = pl.ds(c * step, step)
        reads.append(pltpu.make_async_copy(tokens_ref.at[part, :], held_ref.at[part, :], sem.at[c]))
        reads[-1].start()
    kept_blocks(flags_ref, index_ref)
    row = lax.broadcasted_iota(jnp.int32, (width, 128), 0)
    lane = lax.broadcasted_iota(jnp.int32, (width, 128), 1)
    for copy in reads:
        copy.wait()
    for i in range(KEEP_BLK):
        b = index_ref[i]
        start = pl.multiple_of((b // per_tile) * 128, 128)
        pick = jnp.where(lane == row + (b % per_tile) * width, 1.0, 0.0).astype(jnp.bfloat16)
        picked = dot32(pick, held_ref[:, pl.ds(start, 128)], NT)
        out_ref[i * width:(i + 1) * width, :] = picked.astype(jnp.bfloat16)
    total = jnp.zeros((step, 128), jnp.float32)
    for c in range(chunks):
        for f in range(features // 128):
            piece = held_ref[c * step:(c + 1) * step, f * 128:(f + 1) * 128].astype(jnp.float32)
            total += piece * piece
    squares = jnp.sum(total)
    hi, mid, low = split3(jnp.full((EXTRA, rows), squares, jnp.float32))
    row = lax.broadcasted_iota(jnp.int32, (EXTRA, rows), 0)
    carried = jnp.where(
        row == 0,
        hi.astype(jnp.float32),
        jnp.where(row == 1, mid.astype(jnp.float32), jnp.where(row == 2, low.astype(jnp.float32), 0.0)),
    )
    out_ref[KEEP_BLK * width:, :] = carried.astype(jnp.bfloat16)


def select_kept(tokens, keep_flags):
    rows, features = tokens.shape
    blocks = keep_flags.shape[0]
    kept = KEEP_BLK * (features // blocks)
    chunks = 4
    return pl.pallas_call(
        select_kernel,
        out_shape=jax.ShapeDtypeStruct((kept + EXTRA, rows), jnp.bfloat16),
        in_specs=[
            pl.BlockSpec(memory_space=pltpu.SMEM),
            pl.BlockSpec(memory_space=pl.ANY),
        ],
        out_specs=pl.BlockSpec(memory_space=pltpu.VMEM),
        scratch_shapes=[
            pltpu.SMEM((blocks + 1,), jnp.int32),
            pltpu.VMEM((rows, features), jnp.bfloat16),
            pltpu.SemaphoreType.DMA((chunks,)),
        ],
        compiler_params=pltpu.CompilerParams(vmem_limit_bytes=VMEM_LIMIT),
        name="select_kept",
    )(keep_flags, tokens)


def lane_column(x, c):
    return jnp.broadcast_to(x[:, c:c + 1], (SUB, 128))


def sublane_row(x, t):
    return jnp.broadcast_to(x[t:t + 1, :], (SUB, 128))


def tree_sum(terms):
    while len(terms) > 1:
        pairs = [terms[i] + terms[i + 1] for i in range(0, len(terms) - 1, 2)]
        terms = pairs + terms[len(terms) - len(terms) % 2:]
    return terms[0]


def block_entries(block, base):
    entry = {}
    for j in range(SUB):
        column = lane_column(block, base + j)
        for i in range(j + 1):
            entry[i, j] = sublane_row(column, i)
    return entry


def solve_small(entry, rows, cross, ahead):
    entry, rows, cross, ahead = dict(entry), list(rows), list(cross), list(ahead)
    inverse = {}
    following = {}
    for t in range(0, SUB, 2):
        u = t + 1
        a, b, c = entry[t, t], entry[t, u], entry[u, u]
        first = pl.reciprocal(a, approx=True)
        second = a * pl.reciprocal(a * c - b * b, approx=True)
        step = b * first
        later = range(u + 1, SUB)
        one = {j: entry[t, j] * first for j in later}
        rest = {j: entry[u, j] - b * one[j] for j in later}
        for j in later:
            for i in range(u + 1, j + 1):
                partial = entry[i, j] - entry[t, i] * one[j]
                entry[i, j] = partial - (rest[i] * rest[j]) * second
        two = {j: rest[j] * second for j in later}
        if cross:
            cross[u] = cross[u] - step * cross[t]
            for j in later:
                cross[j] = (cross[j] - one[j] * cross[t]) - two[j] * cross[u]
            if u + 1 < SUB:
                left, right = cross[t] * first, cross[u] * second
                for j in range(SUB):
                    ahead[j] = (ahead[j] - left * sublane_row(cross[t], j)) - right * sublane_row(cross[u], j)
            else:
                left = [sublane_row(cross[t], j) for j in range(SUB)]
                right = [sublane_row(cross[u], j) for j in range(SUB)]
                for j in range(SUB):
                    for i in range(j + 1):
                        value = sublane_row(ahead[j], i) - (left[i] * left[j]) * first
                        following[i, j] = value - (right[i] * right[j]) * second
        rows[u] = rows[u] - step * rows[t]
        inverse[u, t] = -step
        for k in range(t):
            inverse[u, k] = inverse[u, k] - step * inverse[t, k]
        for j in later:
            rows[j] = (rows[j] - one[j] * rows[t]) - two[j] * rows[u]
            for k in range(t):
                inverse[j, k] = (inverse[j, k] - one[j] * inverse[t, k]) - two[j] * inverse[u, k]
            inverse[j, t] = -one[j] - two[j] * inverse[u, t]
            inverse[j, u] = -two[j]
        rows[t] = rows[t] * first
        rows[u] = rows[u] * second
    rows = [
        tree_sum([rows[i]] + [inverse[j, i] * rows[j] for j in range(i + 1, SUB)]) for i in range(SUB)
    ]
    return rows, following


def invert_panel(block, beside=()):
    size = block.shape[0]
    count = size // SUB
    sub = lax.broadcasted_iota(jnp.int32, (SUB, 128), 0)
    lane = lax.broadcasted_iota(jnp.int32, (SUB, 128), 1)
    rows = [block[i * SUB:(i + 1) * SUB, :] for i in range(count)]
    entry = block_entries(rows[0], 0)
    done = 0
    for s in range(count):
        base = s * SUB
        inside = (lane >= base) & (lane < base + SUB)
        cross, ahead = [], []
        if s + 1 < count:
            cross = [lane_column(rows[s + 1], base + j) for j in range(SUB)]
            ahead = [lane_column(rows[s + 1], base + SUB + j) for j in range(SUB)]
        pivot_rows = jnp.where(inside, jnp.where(lane == sub + base, 1.0, 0.0), rows[s])
        spread, entry = solve_small(entry, [sublane_row(pivot_rows, j) for j in range(SUB)], cross, ahead)
        for i in [(s + d) % count for d in range(1, count)]:
            columns = cross if i == s + 1 else [lane_column(rows[i], base + j) for j in range(SUB)]
            change = tree_sum([columns[j] * spread[j] for j in range(SUB)])
            rows[i] = jnp.where(inside, 0.0, rows[i]) - change
        new = spread[SUB - 1]
        for j in range(SUB - 1):
            new = jnp.where(sub == j, spread[j], new)
        rows[s] = new
        until = len(beside) * (s + 1) // count
        for task in beside[done:until]:
            task()
        done = until
    return jnp.concatenate(rows, axis=0)


def wide_left(x):
    hi, mid, low = split3(x)
    return jnp.concatenate([hi, hi, mid, hi, mid, low], axis=1)


def wide_right(x):
    hi, mid, low = split3(x)
    return jnp.concatenate([hi, mid, hi, low, mid, hi], axis=0)


def settle_tasks(at, state):
    a_ref, pivot_ref, wide_ref, _, w_ref, left_ref, right_ref = state
    kept = a_ref.shape[0]
    half = kept // 2
    here = pl.ds(at, PANEL)
    row = lax.broadcasted_iota(jnp.int32, (kept, PANEL), 0)

    def make_w(c):
        w_ref[:, c:c + 256] = dot32(wide_ref[...], wide_right(a_ref[here, c:c + 256]), NN)

    def make_left():
        w_ref[:, here] = pivot_ref[...]
        left_ref[...] = wide_left(jnp.where((row >= at) & (row < at + PANEL), 0.0, a_ref[:, here]))
        a_ref[:, here] = jnp.zeros((kept, PANEL), jnp.float32)

    def make_right(c):
        right_ref[:, c:c + 256] = wide_right(w_ref[:, c:c + 256])

    def update(r, c):
        a_ref[r:r + half, c:c + 256] -= dot32(left_ref[r:r + half, :], right_ref[:, c:c + 256], NN)

    def place():
        a_ref[here, :] = w_ref[...]

    tasks = [functools.partial(make_w, c) for c in range(0, kept, 256)] + [make_left]
    tasks += [functools.partial(make_right, c) for c in range(0, kept, 256)]
    tasks += [functools.partial(update, r, c) for c in range(0, kept, 256) for r in range(0, kept, half)]
    return tasks + [place]


def panel(at, state, beside):
    a_ref, pivot_ref, wide_ref, next_ref = state[:4]
    here, after = pl.ds(at, PANEL), pl.ds(at + PANEL, PANEL)
    inverse = invert_panel(next_ref[...], beside)
    wide = wide_left(inverse)
    crossing = dot32(wide, wide_right(a_ref[here, after]), NN)
    next_ref[...] = a_ref[after, after] - dot32(wide_left(a_ref[after, here]), wide_right(crossing), NN)
    pivot_ref[...] = inverse
    wide_ref[...] = wide


def panels(first, last, state):
    @pl.loop(first, last)
    def _(p):
        at = pl.multiple_of(p * PANEL, PANEL)
        panel(at, state, settle_tasks(pl.multiple_of(at - PANEL, PANEL), state))


def place_pieces(pieces, all_ref, sem):
    copies = []
    at = 0
    for k, piece in enumerate(pieces):
        width = piece.shape[1]
        copies.append(pltpu.make_async_copy(piece, all_ref.at[:, at:at + width], sem.at[k]))
        copies[-1].start()
        at += width
    return copies


def first_kernel(features, rows, last, *refs):
    pieces, refs = refs[:-9], refs[-9:]
    a_ref, scale_ref, pivot_ref, wide_ref, next_ref, all_ref, w_ref, left_ref, right_ref = refs
    kept = a_ref.shape[0]
    tokens = all_ref.shape[1]
    total = jnp.float32(0.0)
    for k in range(0, tokens, rows):
        total = total + jnp.sum(all_ref[kept:, k:k + 1].astype(jnp.float32))
    scale_ref[...] = 1.0 / jnp.full(scale_ref.shape, 0.01 * total / features, jnp.float32)
    scale = scale_ref[0:1, 0:1]
    chunk = 2048 if tokens % 2048 == 0 else rows

    def gram(at, tile):
        row = lax.broadcasted_iota(jnp.int32, (kept, tile), 0)
        lane = lax.broadcasted_iota(jnp.int32, (kept, tile), 1)
        acc = jnp.where(row == lane + at, 1.0, 0.0)
        for c in range(0, tokens, chunk):
            part = dot32(all_ref[:kept, c:c + chunk], all_ref[at:at + tile, c:c + chunk], NT)
            acc = acc + part * scale
        a_ref[:, at:at + tile] = acc

    gram(0, 256)
    next_ref[...] = a_ref[:PANEL, :PANEL]
    state = (a_ref, pivot_ref, wide_ref, next_ref, w_ref, left_ref, right_ref)
    panel(0, state, [functools.partial(gram, at, 256) for at in range(256, kept, 256)])
    panels(1, last, state)


def state_shapes(kept):
    return [
        jax.ShapeDtypeStruct((PANEL, PANEL), jnp.float32),
        jax.ShapeDtypeStruct((PANEL, 6 * PANEL), jnp.bfloat16),
        jax.ShapeDtypeStruct((PANEL, PANEL), jnp.float32),
    ]


def first_half(pieces, features, last):
    kept_extra, rows = pieces[0].shape
    kept = kept_extra - EXTRA
    count = len(pieces)
    tokens = sum(piece.shape[1] for piece in pieces)

    def body(*refs):
        refs, sem = refs[:-1], refs[-1]
        for copy in place_pieces(refs[:count], refs[count + 5], sem):
            copy.wait()
        first_kernel(float(features), rows, last, *refs)

    return pl.pallas_call(
        body,
        out_shape=[
            jax.ShapeDtypeStruct((kept, kept), jnp.float32),
            jax.ShapeDtypeStruct((8, 128), jnp.float32),
        ]
        + state_shapes(kept),
        in_specs=[pl.BlockSpec(memory_space=pl.ANY)] * count,
        out_specs=[pl.BlockSpec(memory_space=pltpu.VMEM)] * 5,
        scratch_shapes=[
            pltpu.VMEM((kept_extra, tokens), jnp.bfloat16),
            pltpu.VMEM((PANEL, kept), jnp.float32),
            pltpu.VMEM((kept, 6 * PANEL), jnp.bfloat16),
            pltpu.VMEM((6 * PANEL, kept), jnp.bfloat16),
            pltpu.SemaphoreType.DMA((count,)),
        ],
        compiler_params=pltpu.CompilerParams(vmem_limit_bytes=VMEM_LIMIT),
        name="gram_and_first_panels",
    )(*pieces)


def dot_small(x, y):
    rows = x.shape[0]
    hi, mid, low = split3(x)
    yhi, ymid, ylow = split3(y)
    first = dot32(jnp.concatenate([hi, mid, low], axis=0), yhi, NN)
    second = dot32(jnp.concatenate([hi, mid], axis=0), ymid, NN)
    third = dot32(hi, ylow, NN)
    small = first[2 * rows:] + second[rows:] + third
    return small + (first[rows:2 * rows] + second[:rows]) + first[:rows]


def second_kernel(chips, first, copies, flags_ref, *refs):
    projected, refs = refs[:chips], refs[chips:]
    begun, scale_ref, refs = refs[:4], refs[4], refs[5:]
    out_ref, index_ref, wide_out_ref, all_ref = refs[-11:-7]
    state = refs[-7:]
    a_ref, next_ref = state[0], state[3]
    own, features = out_ref.shape
    blocks = flags_ref.shape[0]
    width = features // blocks
    per_tile = 128 // width
    kept = a_ref.shape[0]
    kept_blocks(flags_ref, index_ref)
    wide_out_ref[...] = jnp.zeros((own, features), jnp.float32)
    for target, source in zip(state, begun):
        target[...] = source[...]
    last = kept // PANEL - 1
    panels(first, last, state)
    for copy in copies:
        copy.wait()

    at = last * PANEL
    held = {}

    def make_right():
        whole = jnp.concatenate([part[...] for part in projected], axis=1)
        right = dot32(jnp.concatenate(split3(whole), axis=0), all_ref[:kept, :], NT)
        held["right"] = right[:own] + right[own:2 * own] + right[2 * own:]

    def make_tail():
        held["tail"] = held["right"][:, at:] - dot_small(held["right"][:, :at], a_ref[:at, at:])

    def make_base(c):
        held[c] = dot_small(held["right"][:, :at], a_ref[:at, c:c + PANEL])

    work = [make_right] + settle_tasks(at - PANEL, state) + [make_tail]
    work += [functools.partial(make_base, c) for c in range(0, at, PANEL)]
    inverse = invert_panel(next_ref[...], work)
    tail = dot_small(held["tail"], inverse)
    scale = scale_ref[0:1, 0:1]
    answer = [(held[c] + dot_small(tail, a_ref[at:, c:c + PANEL])) * scale for c in range(0, at, PANEL)]
    answer.append(tail * scale)
    place = lax.broadcasted_iota(jnp.int32, (own, 128), 1) // width
    for i in range(KEEP_BLK):
        b = index_ref[i]
        start = pl.multiple_of((b // per_tile) * 128, 128)
        inner = b % per_tile
        source = answer[i // per_tile]
        moved = pltpu.roll(source, width, 1)
        value = jnp.where(inner == i % per_tile, source, moved)
        old = wide_out_ref[:, pl.ds(start, 128)]
        wide_out_ref[:, pl.ds(start, 128)] = jnp.where(place == inner, value, old)
    out_ref[...] = wide_out_ref[...].astype(jnp.bfloat16)


def second_half(keep_flags, projected, begun, scale, pieces, features, first):
    own = projected[0].shape[0]
    blocks = keep_flags.shape[0]
    chips = len(projected)
    kept = begun[0].shape[0]
    count = len(pieces)
    tokens = sum(piece.shape[1] for piece in pieces)
    vmem = pl.BlockSpec(memory_space=pltpu.VMEM)
    anywhere = pl.BlockSpec(memory_space=pl.ANY)

    def body(*refs):
        refs, sem = refs[:-1], refs[-1]
        ins = 6 + chips
        copies = place_pieces(refs[ins:ins + count], refs[ins + count + 3], sem)
        second_kernel(chips, first, copies, *refs)

    return pl.pallas_call(
        body,
        out_shape=jax.ShapeDtypeStruct((own, features), jnp.bfloat16),
        in_specs=[pl.BlockSpec(memory_space=pltpu.SMEM)] + [vmem] * (chips + 5) + [anywhere] * count,
        out_specs=vmem,
        scratch_shapes=[
            pltpu.SMEM((blocks + 1,), jnp.int32),
            pltpu.VMEM((own, features), jnp.float32),
            pltpu.VMEM((kept + EXTRA, tokens), jnp.bfloat16),
            pltpu.VMEM((kept, kept), jnp.float32),
        ]
        + [pltpu.VMEM(item.shape, item.dtype) for item in state_shapes(kept)]
        + [
            pltpu.VMEM((PANEL, kept), jnp.float32),
            pltpu.VMEM((kept, 6 * PANEL), jnp.bfloat16),
            pltpu.VMEM((6 * PANEL, kept), jnp.bfloat16),
            pltpu.SemaphoreType.DMA((count,)),
        ],
        compiler_params=pltpu.CompilerParams(vmem_limit_bytes=VMEM_LIMIT),
        name="last_panels_and_solution",
    )(keep_flags, *projected, *begun, scale, *pieces)


def solution(mesh):
    n = mesh.shape["dp"]
    others = range(2, n, 2)

    def swap(x, k):
        return lax.ppermute(x, "dp", [(d, d ^ k) for d in range(n)])

    def gather_kept(kept):
        if n != 8:
            same = [kept] + [swap(kept, k) for k in others]
            return [part for piece in same for part in (piece, swap(piece, 1))], same[-1]
        near = [swap(kept, 2), swap(kept, 4)]
        sibling = swap(kept, 1)
        near, sibling = lax.optimization_barrier((near, sibling))
        middle = kept.shape[1] // 2
        far = [swap(near[0][:, :middle], 4), swap(near[1][:, middle:], 2)]
        near_sibling = [swap(piece, 1) for piece in near]
        far, near_sibling = lax.optimization_barrier((far, near_sibling))
        pieces = [kept, sibling, near[0], near_sibling[0], near[1], near_sibling[1]]
        return pieces + far + [swap(piece, 1) for piece in far], far

    def on_device(tokens, orig_weight, keep_flags):
        features = tokens.shape[1]
        own = orig_weight.shape[0]
        kept = select_kept(tokens, keep_flags)
        panels = (kept.shape[0] - EXTRA) // PANEL
        half = panels // 2
        pieces, arrived = gather_kept(kept)
        orig_weight, arrived = lax.optimization_barrier((orig_weight, arrived))
        sibling = swap(tokens, 1)
        weights = [orig_weight] + [swap(orig_weight, k) for k in others]
        a, scale, *state = first_half(pieces, features, half)
        a, weights, sibling = lax.optimization_barrier((a, weights, sibling))
        stacked = jnp.concatenate(weights, axis=0)
        projected = [
            lax.dot_general(stacked, part, NT, preferred_element_type=jnp.float32) for part in (tokens, sibling)
        ]
        projected = lax.optimization_barrier(jnp.concatenate(projected, axis=1))
        parts = [projected[i * own:(i + 1) * own] for i in range(n // 2)]
        parts = [parts[0]] + [swap(part, k) for part, k in zip(parts[1:], others)]
        return second_half(keep_flags, parts, (a, *state), scale, pieces, features, half)

    in_specs = (P("dp", None), P(("section", "dp"), None), P())
    out_specs = P(("section", "dp"), None)
    return jax.shard_map(on_device, mesh=mesh, in_specs=in_specs, out_specs=out_specs, check_vma=False)
```

```python
import functools

import jax
import jax.numpy as jnp
from jax import lax
from jax.experimental import pallas as pl
from jax.experimental.pallas import tpu as pltpu
from jax.sharding import PartitionSpec as P

KEEP_BLK = 12
PANEL = 128
SUB = 8
EXTRA = 16
VMEM_LIMIT = 32 * 1024 * 1024
NT = (((1,), (1,)), ((), ()))
NN = (((1,), (0,)), ((), ()))


def split3(x):
    hi = x.astype(jnp.bfloat16)
    rest = x - hi.astype(jnp.float32)
    mid = rest.astype(jnp.bfloat16)
    low = (rest - mid.astype(jnp.float32)).astype(jnp.bfloat16)
    return hi, mid, low


def dot32(a, b, dims):
    return lax.dot_general(a, b, dims, preferred_element_type=jnp.float32)


def kept_blocks(flags_ref, index_ref):
    count = jnp.int32(0)
    for b in range(flags_ref.shape[0]):
        index_ref[count] = b
        count = count + flags_ref[b]


def select_kernel(flags_ref, tokens_ref, out_ref, index_ref, held_ref, sem):
    rows, features = tokens_ref.shape
    blocks = flags_ref.shape[0]
    width = features // blocks
    per_tile = 128 // width
    chunks = sem.shape[0]
    step = rows // chunks
    reads = []
    for c in range(chunks):
        part = pl.ds(c * step, step)
        reads.append(pltpu.make_async_copy(tokens_ref.at[part, :], held_ref.at[part, :], sem.at[c]))
        reads[-1].start()
    kept_blocks(flags_ref, index_ref)
    row = lax.broadcasted_iota(jnp.int32, (width, 128), 0)
    lane = lax.broadcasted_iota(jnp.int32, (width, 128), 1)
    for copy in reads:
        copy.wait()
    for i in range(KEEP_BLK):
        b = index_ref[i]
        start = pl.multiple_of((b // per_tile) * 128, 128)
        pick = jnp.where(lane == row + (b % per_tile) * width, 1.0, 0.0).astype(jnp.bfloat16)
        picked = dot32(pick, held_ref[:, pl.ds(start, 128)], NT)
        out_ref[i * width:(i + 1) * width, :] = picked.astype(jnp.bfloat16)
    total = jnp.zeros((step, 128), jnp.float32)
    for c in range(chunks):
        for f in range(features // 128):
            piece = held_ref[c * step:(c + 1) * step, f * 128:(f + 1) * 128].astype(jnp.float32)
            total += piece * piece
    squares = jnp.sum(total)
    hi, mid, low = split3(jnp.full((EXTRA, rows), squares, jnp.float32))
    row = lax.broadcasted_iota(jnp.int32, (EXTRA, rows), 0)
    carried = jnp.where(
        row == 0,
        hi.astype(jnp.float32),
        jnp.where(row == 1, mid.astype(jnp.float32), jnp.where(row == 2, low.astype(jnp.float32), 0.0)),
    )
    out_ref[KEEP_BLK * width:, :] = carried.astype(jnp.bfloat16)


def select_kept(tokens, keep_flags):
    rows, features = tokens.shape
    blocks = keep_flags.shape[0]
    kept = KEEP_BLK * (features // blocks)
    chunks = 4
    return pl.pallas_call(
        select_kernel,
        out_shape=jax.ShapeDtypeStruct((kept + EXTRA, rows), jnp.bfloat16),
        in_specs=[
            pl.BlockSpec(memory_space=pltpu.SMEM),
            pl.BlockSpec(memory_space=pl.ANY),
        ],
        out_specs=pl.BlockSpec(memory_space=pltpu.VMEM),
        scratch_shapes=[
            pltpu.SMEM((blocks + 1,), jnp.int32),
            pltpu.VMEM((rows, features), jnp.bfloat16),
            pltpu.SemaphoreType.DMA((chunks,)),
        ],
        compiler_params=pltpu.CompilerParams(vmem_limit_bytes=VMEM_LIMIT),
        name="select_kept",
    )(keep_flags, tokens)


def lane_column(x, c):
    return jnp.broadcast_to(x[:, c:c + 1], (SUB, 128))


def sublane_row(x, t):
    return jnp.broadcast_to(x[t:t + 1, :], (SUB, 128))


def tree_sum(terms):
    while len(terms) > 1:
        pairs = [terms[i] + terms[i + 1] for i in range(0, len(terms) - 1, 2)]
        terms = pairs + terms[len(terms) - len(terms) % 2:]
    return terms[0]


def block_entries(block, base):
    entry = {}
    for j in range(SUB):
        column = lane_column(block, base + j)
        for i in range(j + 1):
            entry[i, j] = sublane_row(column, i)
    return entry


def solve_small(entry, rows, cross, ahead):
    entry, rows, cross, ahead = dict(entry), list(rows), list(cross), list(ahead)
    inverse = {}
    following = {}
    for t in range(0, SUB, 2):
        u = t + 1
        a, b, c = entry[t, t], entry[t, u], entry[u, u]
        first = pl.reciprocal(a, approx=True)
        second = a * pl.reciprocal(a * c - b * b, approx=True)
        step = b * first
        later = range(u + 1, SUB)
        one = {j: entry[t, j] * first for j in later}
        rest = {j: entry[u, j] - b * one[j] for j in later}
        for j in later:
            for i in range(u + 1, j + 1):
                partial = entry[i, j] - entry[t, i] * one[j]
                entry[i, j] = partial - (rest[i] * rest[j]) * second
        two = {j: rest[j] * second for j in later}
        if cross:
            cross[u] = cross[u] - step * cross[t]
            for j in later:
                cross[j] = (cross[j] - one[j] * cross[t]) - two[j] * cross[u]
            if u + 1 < SUB:
                left, right = cross[t] * first, cross[u] * second
                for j in range(SUB):
                    ahead[j] = (ahead[j] - left * sublane_row(cross[t], j)) - right * sublane_row(cross[u], j)
            else:
                left = [sublane_row(cross[t], j) for j in range(SUB)]
                right = [sublane_row(cross[u], j) for j in range(SUB)]
                for j in range(SUB):
                    for i in range(j + 1):
                        value = sublane_row(ahead[j], i) - (left[i] * left[j]) * first
                        following[i, j] = value - (right[i] * right[j]) * second
        rows[u] = rows[u] - step * rows[t]
        inverse[u, t] = -step
        for k in range(t):
            inverse[u, k] = inverse[u, k] - step * inverse[t, k]
        for j in later:
            rows[j] = (rows[j] - one[j] * rows[t]) - two[j] * rows[u]
            for k in range(t):
                inverse[j, k] = (inverse[j, k] - one[j] * inverse[t, k]) - two[j] * inverse[u, k]
            inverse[j, t] = -one[j] - two[j] * inverse[u, t]
            inverse[j, u] = -two[j]
        rows[t] = rows[t] * first
        rows[u] = rows[u] * second
    rows = [
        tree_sum([rows[i]] + [inverse[j, i] * rows[j] for j in range(i + 1, SUB)]) for i in range(SUB)
    ]
    return rows, following


def invert_panel(block, beside=()):
    size = block.shape[0]
    count = size // SUB
    sub = lax.broadcasted_iota(jnp.int32, (SUB, 128), 0)
    lane = lax.broadcasted_iota(jnp.int32, (SUB, 128), 1)
    rows = [block[i * SUB:(i + 1) * SUB, :] for i in range(count)]
    entry = block_entries(rows[0], 0)
    done = 0
    for s in range(count):
        base = s * SUB
        inside = (lane >= base) & (lane < base + SUB)
        cross, ahead = [], []
        if s + 1 < count:
            cross = [lane_column(rows[s + 1], base + j) for j in range(SUB)]
            ahead = [lane_column(rows[s + 1], base + SUB + j) for j in range(SUB)]
        pivot_rows = jnp.where(inside, jnp.where(lane == sub + base, 1.0, 0.0), rows[s])
        spread, entry = solve_small(entry, [sublane_row(pivot_rows, j) for j in range(SUB)], cross, ahead)
        for i in [(s + d) % count for d in range(1, count)]:
            columns = cross if i == s + 1 else [lane_column(rows[i], base + j) for j in range(SUB)]
            change = tree_sum([columns[j] * spread[j] for j in range(SUB)])
            rows[i] = jnp.where(inside, 0.0, rows[i]) - change
        new = spread[SUB - 1]
        for j in range(SUB - 1):
            new = jnp.where(sub == j, spread[j], new)
        rows[s] = new
        until = len(beside) * (s + 1) // count
        for task in beside[done:until]:
            task()
        done = until
    return jnp.concatenate(rows, axis=0)


def wide_left(x):
    hi, mid, low = split3(x)
    return jnp.concatenate([hi, hi, mid, hi, mid, low], axis=1)


def wide_right(x):
    hi, mid, low = split3(x)
    return jnp.concatenate([hi, mid, hi, low, mid, hi], axis=0)


def spans(low, high):
    first = low + (high - low) % 256
    starts = ([low] if first > low else []) + list(range(first, high, 256))
    return list(zip(starts, starts[1:] + [high]))


def settle_tasks(p, state):
    a_ref, wide_ref, _, w_ref, left_ref, right_ref = state
    kept = a_ref.shape[0]
    at = p * PANEL
    low = at + PANEL
    here = slice(at, low)

    def make_w(c, d):
        value = dot32(wide_ref[...], wide_right(a_ref[here, c:d]), NN)
        w_ref[:, c:d] = value
        right_ref[:, c:d] = wide_right(value)

    def make_left():
        left_ref[low:, :] = wide_left(a_ref[low:, here])

    def update(c, d):
        a_ref[low:, c:d] -= dot32(left_ref[low:, :], right_ref[:, c:d], NN)

    def place():
        a_ref[here, low:] = w_ref[:, low:]

    tasks = [functools.partial(make_w, c, d) for c, d in spans(low, kept)] + [make_left]
    return tasks + [functools.partial(update, c, d) for c, d in spans(low, kept)] + [place]


def panel(p, state, pivot_ref, beside):
    a_ref, wide_ref, next_ref = state[:3]
    here, after = slice(p * PANEL, (p + 1) * PANEL), slice((p + 1) * PANEL, (p + 2) * PANEL)
    inverse = invert_panel(next_ref[...], beside)
    wide = wide_left(inverse)
    crossing = dot32(wide, wide_right(a_ref[here, after]), NN)
    next_ref[...] = a_ref[after, after] - dot32(wide_left(a_ref[after, here]), wide_right(crossing), NN)
    pivot_ref[...] = inverse
    wide_ref[...] = wide


def place_pieces(pieces, all_ref, sem):
    copies = []
    at = 0
    for k, piece in enumerate(pieces):
        width = piece.shape[1]
        copies.append(pltpu.make_async_copy(piece, all_ref.at[:, at:at + width], sem.at[k]))
        copies[-1].start()
        at += width
    return copies


def first_kernel(features, rows, last, *refs):
    pieces, refs = refs[:-9], refs[-9:]
    a_ref, scale_ref, pivot_ref, wide_ref, next_ref, all_ref, w_ref, left_ref, right_ref = refs
    kept = a_ref.shape[0]
    tokens = all_ref.shape[1]
    total = jnp.float32(0.0)
    for k in range(0, tokens, rows):
        total = total + jnp.sum(all_ref[kept:, k:k + 1].astype(jnp.float32))
    scale_ref[...] = 1.0 / jnp.full(scale_ref.shape, 0.01 * total / features, jnp.float32)
    scale = scale_ref[0:1, 0:1]
    chunk = 2048 if tokens % 2048 == 0 else rows

    def gram(at, tile):
        row = lax.broadcasted_iota(jnp.int32, (kept, tile), 0)
        lane = lax.broadcasted_iota(jnp.int32, (kept, tile), 1)
        acc = jnp.where(row == lane + at, 1.0, 0.0)
        for c in range(0, tokens, chunk):
            part = dot32(all_ref[:kept, c:c + chunk], all_ref[at:at + tile, c:c + chunk], NT)
            acc = acc + part * scale
        a_ref[:, at:at + tile] = acc

    gram(0, 256)
    next_ref[...] = a_ref[:PANEL, :PANEL]
    state = (a_ref, wide_ref, next_ref, w_ref, left_ref, right_ref)
    for p in range(last):
        if p:
            tasks = settle_tasks(p - 1, state)
        else:
            tasks = [functools.partial(gram, at, 256) for at in range(256, kept, 256)]
        panel(p, state, pivot_ref.at[p], tasks)


def first_half(pieces, features, last):
    kept_extra, rows = pieces[0].shape
    kept = kept_extra - EXTRA
    count = len(pieces)
    tokens = sum(piece.shape[1] for piece in pieces)

    def body(*refs):
        refs, sem = refs[:-1], refs[-1]
        for copy in place_pieces(refs[:count], refs[count + 5], sem):
            copy.wait()
        first_kernel(float(features), rows, last, *refs)

    return pl.pallas_call(
        body,
        out_shape=[
            jax.ShapeDtypeStruct((kept, kept), jnp.float32),
            jax.ShapeDtypeStruct((8, 128), jnp.float32),
            jax.ShapeDtypeStruct((last, PANEL, PANEL), jnp.float32),
            jax.ShapeDtypeStruct((PANEL, 6 * PANEL), jnp.bfloat16),
            jax.ShapeDtypeStruct((PANEL, PANEL), jnp.float32),
        ],
        in_specs=[pl.BlockSpec(memory_space=pl.ANY)] * count,
        out_specs=[pl.BlockSpec(memory_space=pltpu.VMEM)] * 5,
        scratch_shapes=[
            pltpu.VMEM((kept_extra, tokens), jnp.bfloat16),
            pltpu.VMEM((PANEL, kept), jnp.float32),
            pltpu.VMEM((kept, 6 * PANEL), jnp.bfloat16),
            pltpu.VMEM((6 * PANEL, kept), jnp.bfloat16),
            pltpu.SemaphoreType.DMA((count,)),
        ],
        compiler_params=pltpu.CompilerParams(vmem_limit_bytes=VMEM_LIMIT),
        name="gram_and_first_panels",
    )(*pieces)


def dot_small(x, y, dims=NN):
    rows = x.shape[0]
    hi, mid, low = split3(x)
    yhi, ymid, ylow = split3(y)
    first = dot32(jnp.concatenate([hi, mid, low], axis=0), yhi, dims)
    second = dot32(jnp.concatenate([hi, mid], axis=0), ymid, dims)
    third = dot32(hi, ylow, dims)
    small = first[2 * rows:] + second[rows:] + third
    return small + (first[rows:2 * rows] + second[:rows]) + first[:rows]


def second_kernel(chips, first, copies, flags_ref, *refs):
    projected, refs = refs[:chips], refs[chips:]
    start_ref, early_ref, start_wide_ref, start_next_ref, scale_ref = refs[:5]
    out_ref, index_ref, wide_out_ref, all_ref, late_ref = refs[-11:-6]
    state = refs[-6:]
    a_ref, wide_ref, next_ref = state[:3]
    own, features = out_ref.shape
    blocks = flags_ref.shape[0]
    width = features // blocks
    per_tile = 128 // width
    kept = a_ref.shape[0]
    last = kept // PANEL - 1
    at = last * PANEL
    kept_blocks(flags_ref, index_ref)
    wide_out_ref[...] = jnp.zeros((own, features), jnp.float32)
    live = (first - 1) * PANEL
    a_ref[live:, live:] = start_ref[live:, live:]
    wide_ref[...] = start_wide_ref[...]
    next_ref[...] = start_next_ref[...]
    held = {}

    def block(p):
        return slice(p * PANEL, (p + 1) * PANEL)

    def factor(p):
        return (start_ref if p < first - 1 else a_ref)[block(p), (p + 1) * PANEL:]

    def pivot(p):
        return early_ref[p] if p < first else late_ref[p - first]

    def make_right():
        whole = jnp.concatenate([part[...] for part in projected], axis=1)
        right = dot32(jnp.concatenate(split3(whole), axis=0), all_ref[:kept, :], NT)
        held["right"] = right[:own] + right[own:2 * own] + right[2 * own:]

    def forward(p):
        right = held["right"]
        held["z", p] = right[:, :PANEL]
        held["right"] = right[:, PANEL:] - dot_small(right[:, :PANEL], factor(p))

    def scaled(p):
        held["zd", p] = dot_small(held["z", p], pivot(p))

    def backward(p):
        if p == last:
            row = lax.broadcasted_iota(jnp.int32, (own + PANEL, PANEL), 0)
            lane = lax.broadcasted_iota(jnp.int32, (own + PANEL, PANEL), 1)
            held["back"] = jnp.where(row == lane + own, 1.0, 0.0)
        else:
            base = jnp.concatenate([held["zd", p], jnp.zeros((PANEL, PANEL), jnp.float32)], axis=0)
            value = base - dot_small(held["back"], factor(p), NT)
            held["back"] = jnp.concatenate([value, held["back"]], axis=1)

    for p in range(first, last):
        tasks = settle_tasks(p - 1, state)
        if p == last - 1:
            for copy in copies:
                copy.wait()
            tasks = [make_right] + [functools.partial(forward, q) for q in range(p - 1)] + tasks
            tasks += [functools.partial(forward, p - 1)] + [functools.partial(scaled, q) for q in range(p)]
        panel(p, state, late_ref.at[p - first], tasks)
    tasks = settle_tasks(last - 1, state)
    tasks += [functools.partial(forward, last - 1), functools.partial(scaled, last - 1)]
    tasks += [functools.partial(backward, p) for p in reversed(range(last + 1))]
    inverse = invert_panel(next_ref[...], tasks)
    tail = dot_small(held["right"], inverse)
    scale = scale_ref[0:1, 0:1]
    front = held["back"][:own, :at] + dot_small(tail, held["back"][own:, :at])
    answer = [front[:, c:c + PANEL] * scale for c in range(0, at, PANEL)] + [tail * scale]
    place = lax.broadcasted_iota(jnp.int32, (own, 128), 1) // width
    for i in range(KEEP_BLK):
        b = index_ref[i]
        start = pl.multiple_of((b // per_tile) * 128, 128)
        inner = b % per_tile
        source = answer[i // per_tile]
        moved = pltpu.roll(source, width, 1)
        value = jnp.where(inner == i % per_tile, source, moved)
        old = wide_out_ref[:, pl.ds(start, 128)]
        wide_out_ref[:, pl.ds(start, 128)] = jnp.where(place == inner, value, old)
    out_ref[...] = wide_out_ref[...].astype(jnp.bfloat16)


def second_half(keep_flags, projected, begun, scale, pieces, features, first):
    own = projected[0].shape[0]
    blocks = keep_flags.shape[0]
    chips = len(projected)
    kept = begun[0].shape[0]
    count = len(pieces)
    tokens = sum(piece.shape[1] for piece in pieces)
    vmem = pl.BlockSpec(memory_space=pltpu.VMEM)
    anywhere = pl.BlockSpec(memory_space=pl.ANY)

    def body(*refs):
        refs, sem = refs[:-1], refs[-1]
        ins = 6 + chips
        copies = place_pieces(refs[ins:ins + count], refs[ins + count + 3], sem)
        second_kernel(chips, first, copies, *refs)

    return pl.pallas_call(
        body,
        out_shape=jax.ShapeDtypeStruct((own, features), jnp.bfloat16),
        in_specs=[pl.BlockSpec(memory_space=pltpu.SMEM)] + [vmem] * (chips + 5) + [anywhere] * count,
        out_specs=vmem,
        scratch_shapes=[
            pltpu.SMEM((blocks + 1,), jnp.int32),
            pltpu.VMEM((own, features), jnp.float32),
            pltpu.VMEM((kept + EXTRA, tokens), jnp.bfloat16),
            pltpu.VMEM((kept // PANEL - 1 - first, PANEL, PANEL), jnp.float32),
            pltpu.VMEM((kept, kept), jnp.float32),
            pltpu.VMEM((PANEL, 6 * PANEL), jnp.bfloat16),
            pltpu.VMEM((PANEL, PANEL), jnp.float32),
            pltpu.VMEM((PANEL, kept), jnp.float32),
            pltpu.VMEM((kept, 6 * PANEL), jnp.bfloat16),
            pltpu.VMEM((6 * PANEL, kept), jnp.bfloat16),
            pltpu.SemaphoreType.DMA((count,)),
        ],
        compiler_params=pltpu.CompilerParams(vmem_limit_bytes=VMEM_LIMIT),
        name="last_panels_and_solution",
    )(keep_flags, *projected, *begun, scale, *pieces)


def solution(mesh):
    n = mesh.shape["dp"]
    others = range(2, n, 2)

    def swap(x, k):
        return lax.ppermute(x, "dp", [(d, d ^ k) for d in range(n)])

    def gather_kept(kept):
        if n != 8:
            same = [kept] + [swap(kept, k) for k in others]
            return [part for piece in same for part in (piece, swap(piece, 1))], same[-1]
        near = [swap(kept, 2), swap(kept, 4)]
        sibling = swap(kept, 1)
        near, sibling = lax.optimization_barrier((near, sibling))
        middle = kept.shape[1] // 2
        far = [swap(near[0][:, :middle], 4), swap(near[1][:, middle:], 2)]
        near_sibling = [swap(piece, 1) for piece in near]
        far, near_sibling = lax.optimization_barrier((far, near_sibling))
        pieces = [kept, sibling, near[0], near_sibling[0], near[1], near_sibling[1]]
        return pieces + far + [swap(piece, 1) for piece in far], far

    def on_device(tokens, orig_weight, keep_flags):
        features = tokens.shape[1]
        own = orig_weight.shape[0]
        kept = select_kept(tokens, keep_flags)
        panels = (kept.shape[0] - EXTRA) // PANEL
        half = panels // 2
        pieces, arrived = gather_kept(kept)
        orig_weight, arrived = lax.optimization_barrier((orig_weight, arrived))
        sibling = swap(tokens, 1)
        weights = [orig_weight] + [swap(orig_weight, k) for k in others]
        a, scale, *state = first_half(pieces, features, half)
        a, weights, sibling = lax.optimization_barrier((a, weights, sibling))
        stacked = jnp.concatenate(weights, axis=0)
        projected = [
            lax.dot_general(stacked, part, NT, preferred_element_type=jnp.float32) for part in (tokens, sibling)
        ]
        projected = lax.optimization_barrier(jnp.concatenate(projected, axis=1))
        parts = [projected[i * own:(i + 1) * own] for i in range(n // 2)]
        parts = [parts[0]] + [swap(part, k) for part, k in zip(parts[1:], others)]
        return second_half(keep_flags, parts, (a, *state), scale, pieces, features, half)

    in_specs = (P("dp", None), P(("section", "dp"), None), P())
    out_specs = P(("section", "dp"), None)
    return jax.shard_map(on_device, mesh=mesh, in_specs=in_specs, out_specs=out_specs, check_vma=False)
```

```python
import functools

import jax
import jax.numpy as jnp
from jax import lax
from jax.experimental import pallas as pl
from jax.experimental.pallas import tpu as pltpu
from jax.sharding import PartitionSpec as P

KEEP_BLK = 12
PANEL = 128
SUB = 8
EXTRA = 16
VMEM_LIMIT = 32 * 1024 * 1024
VMEM_LARGE = 60 * 1024 * 1024
NT = (((1,), (1,)), ((), ()))
NN = (((1,), (0,)), ((), ()))


def split3(x):
    hi = x.astype(jnp.bfloat16)
    rest = x - hi.astype(jnp.float32)
    mid = rest.astype(jnp.bfloat16)
    low = (rest - mid.astype(jnp.float32)).astype(jnp.bfloat16)
    return hi, mid, low


def dot32(a, b, dims):
    return lax.dot_general(a, b, dims, preferred_element_type=jnp.float32)


def kept_blocks(flags_ref, index_ref):
    count = jnp.int32(0)
    for b in range(flags_ref.shape[0]):
        index_ref[count] = b
        count = count + flags_ref[b]


def select_kernel(flags_ref, tokens_ref, out_ref, index_ref, held_ref, sem):
    rows, features = tokens_ref.shape
    blocks = flags_ref.shape[0]
    width = features // blocks
    per_tile = 128 // width
    chunks = sem.shape[0]
    step = rows // chunks
    reads = []
    for c in range(chunks):
        part = pl.ds(c * step, step)
        reads.append(pltpu.make_async_copy(tokens_ref.at[part, :], held_ref.at[part, :], sem.at[c]))
        reads[-1].start()
    kept_blocks(flags_ref, index_ref)
    row = lax.broadcasted_iota(jnp.int32, (width, 128), 0)
    lane = lax.broadcasted_iota(jnp.int32, (width, 128), 1)
    for copy in reads:
        copy.wait()
    for i in range(KEEP_BLK):
        b = index_ref[i]
        start = pl.multiple_of((b // per_tile) * 128, 128)
        pick = jnp.where(lane == row + (b % per_tile) * width, 1.0, 0.0).astype(jnp.bfloat16)
        picked = dot32(pick, held_ref[:, pl.ds(start, 128)], NT)
        out_ref[i * width:(i + 1) * width, :] = picked.astype(jnp.bfloat16)
    total = jnp.zeros((step, 128), jnp.float32)
    for c in range(chunks):
        for f in range(features // 128):
            piece = held_ref[c * step:(c + 1) * step, f * 128:(f + 1) * 128].astype(jnp.float32)
            total += piece * piece
    squares = jnp.sum(total)
    hi, mid, low = split3(jnp.full((EXTRA, rows), squares, jnp.float32))
    row = lax.broadcasted_iota(jnp.int32, (EXTRA, rows), 0)
    carried = jnp.where(
        row == 0,
        hi.astype(jnp.float32),
        jnp.where(row == 1, mid.astype(jnp.float32), jnp.where(row == 2, low.astype(jnp.float32), 0.0)),
    )
    out_ref[KEEP_BLK * width:, :] = carried.astype(jnp.bfloat16)


def select_kept(tokens, keep_flags):
    rows, features = tokens.shape
    blocks = keep_flags.shape[0]
    kept = KEEP_BLK * (features // blocks)
    chunks = 4
    return pl.pallas_call(
        select_kernel,
        out_shape=jax.ShapeDtypeStruct((kept + EXTRA, rows), jnp.bfloat16),
        in_specs=[
            pl.BlockSpec(memory_space=pltpu.SMEM),
            pl.BlockSpec(memory_space=pl.ANY),
        ],
        out_specs=pl.BlockSpec(memory_space=pltpu.VMEM),
        scratch_shapes=[
            pltpu.SMEM((blocks + 1,), jnp.int32),
            pltpu.VMEM((rows, features), jnp.bfloat16),
            pltpu.SemaphoreType.DMA((chunks,)),
        ],
        compiler_params=pltpu.CompilerParams(vmem_limit_bytes=VMEM_LARGE),
        name="select_kept",
    )(keep_flags, tokens)


def lane_column(x, c):
    return jnp.broadcast_to(x[:, c:c + 1], (SUB, 128))


def sublane_row(x, t):
    return jnp.broadcast_to(x[t:t + 1, :], (SUB, 128))


def tree_sum(terms):
    while len(terms) > 1:
        pairs = [terms[i] + terms[i + 1] for i in range(0, len(terms) - 1, 2)]
        terms = pairs + terms[len(terms) - len(terms) % 2:]
    return terms[0]


def block_entries(block, base):
    entry = {}
    for j in range(SUB):
        column = lane_column(block, base + j)
        for i in range(j + 1):
            entry[i, j] = sublane_row(column, i)
    return entry


def solve_small(entry, rows, cross, ahead):
    entry, rows, cross, ahead = dict(entry), list(rows), list(cross), list(ahead)
    lower = {}
    for t in range(0, SUB, 2):
        u = t + 1
        a, b, c = entry[t, t], entry[t, u], entry[u, u]
        first = pl.reciprocal(a, approx=True)
        second = a * pl.reciprocal(a * c - b * b, approx=True)
        lower[u, t] = b * first
        later = range(u + 1, SUB)
        rest = {}
        for j in later:
            lower[j, t] = entry[t, j] * first
            rest[j] = entry[u, j] - b * lower[j, t]
        for j in later:
            for i in range(u + 1, j + 1):
                partial = entry[i, j] - entry[t, i] * lower[j, t]
                entry[i, j] = partial - (rest[i] * rest[j]) * second
        for j in later:
            lower[j, u] = rest[j] * second
        for part in (cross, rows):
            if part:
                part[u] = part[u] - lower[u, t] * part[t]
                for j in later:
                    part[j] = (part[j] - lower[j, t] * part[t]) - lower[j, u] * part[u]
        if cross:
            left, right = cross[t] * first, cross[u] * second
            for j in range(SUB):
                ahead[j] = (ahead[j] - left * sublane_row(cross[t], j)) - right * sublane_row(cross[u], j)
        rows[t] = rows[t] * first
        rows[u] = rows[u] * second
    following = {(i, j): sublane_row(ahead[j], i) for j in range(SUB) for i in range(j + 1) if cross}
    for t in reversed(range(SUB)):
        for j in range(t):
            rows[j] = rows[j] - lower[t, j] * rows[t]
    return rows, following


def factor_panel(block, beside=()):
    size = block.shape[0]
    count = size // SUB
    sub = lax.broadcasted_iota(jnp.int32, (SUB, 128), 0)
    lane = lax.broadcasted_iota(jnp.int32, (SUB, 128), 1)
    rows = [block[i * SUB:(i + 1) * SUB, :] for i in range(count)]
    entry = block_entries(rows[0], 0)
    lower, scaled = [], []
    done = 0
    for s in range(count):
        base = s * SUB
        inside = (lane >= base) & (lane < base + SUB)
        cross, ahead = [], []
        if s + 1 < count:
            cross = [lane_column(rows[s + 1], base + j) for j in range(SUB)]
            ahead = [lane_column(rows[s + 1], base + SUB + j) for j in range(SUB)]
        pivot_rows = jnp.where(inside, jnp.where(lane == sub + base, 1.0, 0.0), rows[s])
        spread, entry = solve_small(entry, [sublane_row(pivot_rows, j) for j in range(SUB)], cross, ahead)
        for i in range(s + 1, count):
            columns = cross if i == s + 1 else [lane_column(rows[i], base + j) for j in range(SUB)]
            change = tree_sum([columns[j] * spread[j] for j in range(SUB)])
            rows[i] = jnp.where(inside, 0.0, rows[i]) - change
        new = spread[SUB - 1]
        for j in range(SUB - 1):
            new = jnp.where(sub == j, spread[j], new)
        lower.append(jnp.where(lane < base + SUB, pivot_rows, 0.0))
        scaled.append(jnp.where(lane < base + SUB, new, 0.0))
        until = len(beside) * (s + 1) // count
        for task in beside[done:until]:
            task()
        done = until
    return jnp.concatenate(lower, axis=0), jnp.concatenate(scaled, axis=0)


def wide_left(x):
    hi, mid, low = split3(x)
    return jnp.concatenate([hi, hi, mid, hi, mid, low], axis=1)


def wide_right(x):
    hi, mid, low = split3(x)
    return jnp.concatenate([hi, mid, hi, low, mid, hi], axis=0)


def wide_across(x):
    hi, mid, low = split3(x)
    return jnp.concatenate([hi, mid, hi, low, mid, hi], axis=1)


def spans(low, high):
    first = low + (high - low) % 256
    starts = ([low] if first > low else []) + list(range(first, high, 256))
    return list(zip(starts, starts[1:] + [high]))


def settle_tasks(p, state, lower_ref, scaled_ref):
    a_ref, offset, _, w_ref, left_ref, right_ref = state
    kept = w_ref.shape[1]
    at = p * PANEL
    low = at + PANEL
    here = slice(at - offset, low - offset)
    rest = slice(low - offset, kept - offset)

    def make_w(c, d):
        value = dot32(wide_left(scaled_ref[...]), wide_right(a_ref[here, c - offset:d - offset]), NN)
        right_ref[:, c:d] = wide_right(value)

    def make_left():
        value = dot32(wide_left(a_ref[rest, here]), wide_across(lower_ref[...]), NT)
        left_ref[low:, :] = wide_left(value)

    def update(c, d):
        a_ref[rest, c - offset:d - offset] -= dot32(left_ref[low:, :], right_ref[:, c:d], NN)

    def place(c, d):
        a_ref[here, c - offset:d - offset] = dot32(wide_left(lower_ref[...].T), right_ref[:, c:d], NN)

    ranges = spans(low, kept)
    tasks = [functools.partial(make_w, c, d) for c, d in ranges] + [make_left]
    tasks += [functools.partial(update, c, d) for c, d in ranges]
    return tasks + [functools.partial(place, c, d) for c, d in ranges]


def panel(p, state, factors_ref, beside):
    a_ref, offset, next_ref = state[:3]
    at = p * PANEL - offset
    here, after = slice(at, at + PANEL), slice(at + PANEL, at + 2 * PANEL)
    lower, scaled = factor_panel(next_ref[...], beside)
    left = dot32(wide_left(a_ref[after, here]), wide_across(lower), NT)
    right = dot32(wide_left(scaled), wide_right(a_ref[here, after]), NN)
    next_ref[...] = a_ref[after, after] - dot32(wide_left(left), wide_right(right), NN)
    factors_ref[0] = lower
    factors_ref[1] = scaled


def factors_shape(count):
    return jax.ShapeDtypeStruct((count, 2, PANEL, PANEL), jnp.float32)


def work_scratch(kept):
    return [
        pltpu.VMEM((8, kept), jnp.float32),
        pltpu.VMEM((kept, 6 * PANEL), jnp.bfloat16),
        pltpu.VMEM((6 * PANEL, kept), jnp.bfloat16),
    ]


def place_pieces(pieces, all_ref, sem):
    copies = []
    at = 0
    for k, piece in enumerate(pieces):
        width = piece.shape[1]
        copies.append(pltpu.make_async_copy(piece, all_ref.at[:, at:at + width], sem.at[k]))
        copies[-1].start()
        at += width
    return copies


def first_kernel(features, rows, last, *refs):
    a_ref, scale_ref, factors_ref, next_ref, all_ref, w_ref, left_ref, right_ref = refs[-8:]
    kept = a_ref.shape[0]
    tokens = all_ref.shape[1]
    total = jnp.float32(0.0)
    for k in range(0, tokens, rows):
        total = total + jnp.sum(all_ref[kept:, k:k + 1].astype(jnp.float32))
    scale_ref[...] = 1.0 / jnp.full(scale_ref.shape, 0.01 * total / features, jnp.float32)
    scale = scale_ref[0:1, 0:1]
    chunk = 2048 if tokens % 2048 == 0 else rows

    def gram(at, tile):
        row = lax.broadcasted_iota(jnp.int32, (kept, tile), 0)
        lane = lax.broadcasted_iota(jnp.int32, (kept, tile), 1)
        acc = jnp.where(row == lane + at, 1.0, 0.0)
        for c in range(0, tokens, chunk):
            part = dot32(all_ref[:kept, c:c + chunk], all_ref[at:at + tile, c:c + chunk], NT)
            acc = acc + part * scale
        a_ref[:, at:at + tile] = acc

    gram(0, 256)
    next_ref[...] = a_ref[:PANEL, :PANEL]
    state = (a_ref, 0, next_ref, w_ref, left_ref, right_ref)
    for p in range(last):
        if p:
            tasks = settle_tasks(p - 1, state, factors_ref.at[p - 1, 0], factors_ref.at[p - 1, 1])
        else:
            tasks = [functools.partial(gram, at, 256) for at in range(256, kept, 256)]
        panel(p, state, factors_ref.at[p], tasks)


def first_half(pieces, features, last):
    kept_extra, rows = pieces[0].shape
    kept = kept_extra - EXTRA
    count = len(pieces)
    tokens = sum(piece.shape[1] for piece in pieces)

    def body(*refs):
        refs, sem = refs[:-1], refs[-1]
        for copy in place_pieces(refs[:count], refs[count + 4], sem):
            copy.wait()
        first_kernel(float(features), rows, last, *refs)

    return pl.pallas_call(
        body,
        out_shape=[
            jax.ShapeDtypeStruct((kept, kept), jnp.float32),
            jax.ShapeDtypeStruct((8, 128), jnp.float32),
            factors_shape(last),
            jax.ShapeDtypeStruct((PANEL, PANEL), jnp.float32),
        ],
        in_specs=[pl.BlockSpec(memory_space=pl.ANY)] * count,
        out_specs=[pl.BlockSpec(memory_space=pltpu.VMEM)] * 4,
        scratch_shapes=[
            pltpu.VMEM((kept_extra, tokens), jnp.bfloat16),
            *work_scratch(kept),
            pltpu.SemaphoreType.DMA((count,)),
        ],
        compiler_params=pltpu.CompilerParams(vmem_limit_bytes=VMEM_LIMIT),
        name="gram_and_first_panels",
    )(*pieces)


def dot_small(x, y, dims=NN):
    rows = x.shape[0]
    hi, mid, low = split3(x)
    yhi, ymid, ylow = split3(y)
    first = dot32(jnp.concatenate([hi, mid, low], axis=0), yhi, dims)
    second = dot32(jnp.concatenate([hi, mid], axis=0), ymid, dims)
    third = dot32(hi, ylow, dims)
    small = first[2 * rows:] + second[rows:] + third
    return small + (first[rows:2 * rows] + second[:rows]) + first[:rows]


def middle_kernel(first, last, start_ref, early_ref, start_next_ref, a_ref, factors_ref, next_ref, *work):
    kept = start_ref.shape[0]
    offset = kept - a_ref.shape[0]
    a_ref[...] = start_ref[offset:, offset:]
    next_ref[...] = start_next_ref[...]
    state = (a_ref, offset, next_ref, *work)
    for p in range(first, last):
        source = early_ref.at[p - 1] if p == first else factors_ref.at[p - 1 - first]
        panel(p, state, factors_ref.at[p - first], settle_tasks(p - 1, state, source.at[0], source.at[1]))


def middle_part(a, factors, follow, first, last):
    kept = a.shape[0]
    left = kept - (first - 1) * PANEL
    vmem = pl.BlockSpec(memory_space=pltpu.VMEM)
    return pl.pallas_call(
        functools.partial(middle_kernel, first, last),
        out_shape=[
            jax.ShapeDtypeStruct((left, left), jnp.float32),
            factors_shape(last - first),
            jax.ShapeDtypeStruct((PANEL, PANEL), jnp.float32),
        ],
        in_specs=[vmem] * 3,
        out_specs=[vmem] * 3,
        scratch_shapes=work_scratch(kept),
        compiler_params=pltpu.CompilerParams(vmem_limit_bytes=VMEM_LIMIT),
        name="middle_panels",
    )(a, factors, follow)


def last_kernel(chips, begin, middle, copies, flags_ref, *refs):
    projected, refs = refs[:chips], refs[chips:]
    scale_ref, whole_ref, early_ref, start_ref, mid_ref, start_next_ref = refs[:6]
    out_ref, index_ref, wide_out_ref, all_ref, late_ref, a_ref, next_ref = refs[-10:-3]
    work = refs[-3:]
    own, features = out_ref.shape
    blocks = flags_ref.shape[0]
    width = features // blocks
    per_tile = 128 // width
    kept = whole_ref.shape[0]
    last = kept // PANEL - 1
    at = last * PANEL
    kept_blocks(flags_ref, index_ref)
    wide_out_ref[...] = jnp.zeros((own, features), jnp.float32)
    offset = kept - a_ref.shape[0]
    cut = start_ref.shape[0] - a_ref.shape[0]
    a_ref[...] = start_ref[cut:, cut:]
    next_ref[...] = start_next_ref[...]
    state = (a_ref, offset, next_ref, *work)
    held = {}

    def factor(p):
        source, skip = a_ref, offset
        if p < begin - 1:
            source, skip = whole_ref, 0
        elif p < middle - 1:
            source, skip = start_ref, kept - start_ref.shape[0]
        low = p * PANEL - skip
        return source[low:low + PANEL, low + PANEL:]

    def factors(p):
        if p < begin:
            return early_ref.at[p]
        return mid_ref.at[p - begin] if p < middle else late_ref.at[p - middle]

    def settle(p):
        return settle_tasks(p, state, factors(p).at[0], factors(p).at[1])

    def make_right():
        whole = jnp.concatenate([part[...] for part in projected], axis=1)
        right = dot32(jnp.concatenate(split3(whole), axis=0), all_ref[:kept, :], NT)
        held["right"] = right[:own] + right[own:2 * own] + right[2 * own:]

    def forward(p):
        right = held["right"]
        held["z", p] = right[:, :PANEL]
        held["right"] = right[:, PANEL:] - dot_small(right[:, :PANEL], factor(p))

    def scaled(p):
        held["zd", p] = dot_small(dot_small(held["z", p], factors(p)[0], NT), factors(p)[1])

    def backward(p):
        if p == last:
            row = lax.broadcasted_iota(jnp.int32, (own + PANEL, PANEL), 0)
            lane = lax.broadcasted_iota(jnp.int32, (own + PANEL, PANEL), 1)
            held["back"] = jnp.where(row == lane + own, 1.0, 0.0)
        else:
            base = jnp.concatenate([held["zd", p], jnp.zeros((PANEL, PANEL), jnp.float32)], axis=0)
            value = base - dot_small(held["back"], factor(p), NT)
            held["back"] = jnp.concatenate([value, held["back"]], axis=1)

    for copy in copies:
        copy.wait()
    for p in range(middle, last):
        tasks = settle(p - 1)
        if p == last - 1:
            tasks = [make_right] + [functools.partial(forward, q) for q in range(p - 1)] + tasks
            tasks += [functools.partial(forward, p - 1)] + [functools.partial(scaled, q) for q in range(p)]
        panel(p, state, late_ref.at[p - middle], tasks)
    tasks = settle(last - 1)
    tasks += [functools.partial(forward, last - 1), functools.partial(scaled, last - 1)]
    tasks += [functools.partial(backward, p) for p in reversed(range(last + 1))]
    lower, upper = factor_panel(next_ref[...], tasks)
    tail = dot_small(dot_small(held["right"], lower, NT), upper)
    scale = scale_ref[0:1, 0:1]
    front = held["back"][:own, :at] + dot_small(tail, held["back"][own:, :at])
    answer = [front[:, c:c + PANEL] * scale for c in range(0, at, PANEL)] + [tail * scale]
    place = lax.broadcasted_iota(jnp.int32, (own, 128), 1) // width
    for i in range(KEEP_BLK):
        b = index_ref[i]
        start = pl.multiple_of((b // per_tile) * 128, 128)
        inner = b % per_tile
        source = answer[i // per_tile]
        moved = pltpu.roll(source, width, 1)
        value = jnp.where(inner == i % per_tile, source, moved)
        old = wide_out_ref[:, pl.ds(start, 128)]
        wide_out_ref[:, pl.ds(start, 128)] = jnp.where(place == inner, value, old)
    out_ref[...] = wide_out_ref[...].astype(jnp.bfloat16)


def last_part(keep_flags, projected, begun, pieces, features, begin, middle):
    own = projected[0].shape[0]
    blocks = keep_flags.shape[0]
    chips = len(projected)
    kept = begun[1].shape[0]
    count = len(pieces)
    tokens = sum(piece.shape[1] for piece in pieces)
    left = kept - (middle - 1) * PANEL
    vmem = pl.BlockSpec(memory_space=pltpu.VMEM)
    anywhere = pl.BlockSpec(memory_space=pl.ANY)

    def body(*refs):
        refs, sem = refs[:-1], refs[-1]
        ins = 1 + chips + len(begun)
        copies = place_pieces(refs[ins:ins + count], refs[ins + count + 3], sem)
        last_kernel(chips, begin, middle, copies, *refs)

    return pl.pallas_call(
        body,
        out_shape=jax.ShapeDtypeStruct((own, features), jnp.bfloat16),
        in_specs=[pl.BlockSpec(memory_space=pltpu.SMEM)] + [vmem] * (chips + len(begun)) + [anywhere] * count,
        out_specs=vmem,
        scratch_shapes=[
            pltpu.SMEM((blocks + 1,), jnp.int32),
            pltpu.VMEM((own, features), jnp.float32),
            pltpu.VMEM((kept + EXTRA, tokens), jnp.bfloat16),
            pltpu.VMEM((kept // PANEL - 1 - middle, 2, PANEL, PANEL), jnp.float32),
            pltpu.VMEM((left, left), jnp.float32),
            pltpu.VMEM((PANEL, PANEL), jnp.float32),
            *work_scratch(kept),
            pltpu.SemaphoreType.DMA((count,)),
        ],
        compiler_params=pltpu.CompilerParams(vmem_limit_bytes=VMEM_LIMIT),
        name="last_panels_and_solution",
    )(keep_flags, *projected, *begun, *pieces)


def solution(mesh):
    n = mesh.shape["dp"]
    others = range(2, n, 2)

    def swap(x, k):
        return lax.ppermute(x, "dp", [(d, d ^ k) for d in range(n)])

    def gather_kept(kept):
        if n != 8:
            same = [kept] + [swap(kept, k) for k in others]
            return [part for piece in same for part in (piece, swap(piece, 1))], same[-1]
        near = [swap(kept, 2), swap(kept, 4)]
        sibling = swap(kept, 1)
        near, sibling = lax.optimization_barrier((near, sibling))
        middle = kept.shape[1] // 2
        far = [swap(near[0][:, :middle], 4), swap(near[1][:, middle:], 2)]
        near_sibling = [swap(piece, 1) for piece in near]
        far, near_sibling = lax.optimization_barrier((far, near_sibling))
        pieces = [kept, sibling, near[0], near_sibling[0], near[1], near_sibling[1]]
        return pieces + far + [swap(piece, 1) for piece in far], far

    def on_device(tokens, orig_weight, keep_flags):
        features = tokens.shape[1]
        own = orig_weight.shape[0]
        kept = select_kept(tokens, keep_flags)
        panels = (kept.shape[0] - EXTRA) // PANEL
        begin = panels // 2
        middle = begin + 1
        tokens, kept = lax.optimization_barrier((tokens, kept))
        pieces, arrived = gather_kept(kept)
        orig_weight, arrived = lax.optimization_barrier((orig_weight, arrived))
        sibling = swap(tokens, 1)
        weights = [orig_weight] + [swap(orig_weight, k) for k in others]
        a, scale, factors, follow = first_half(pieces, features, begin)
        a, weights, sibling = lax.optimization_barrier((a, weights, sibling))
        stacked = jnp.concatenate(weights, axis=0)
        projected = [
            lax.dot_general(stacked, part, NT, preferred_element_type=jnp.float32) for part in (tokens, sibling)
        ]
        projected, a = lax.optimization_barrier((jnp.concatenate(projected, axis=1), a))
        parts = [projected[i * own:(i + 1) * own] for i in range(n // 2)]
        parts = [parts[0]] + [swap(part, k) for part, k in zip(parts[1:], others)]
        rest, more, follow = middle_part(a, factors, follow, begin, middle)
        begun = (scale, a, factors, rest, more, follow)
        return last_part(keep_flags, parts, begun, pieces, features, begin, middle)

    in_specs = (P("dp", None), P(("section", "dp"), None), P())
    out_specs = P(("section", "dp"), None)
    return jax.shard_map(on_device, mesh=mesh, in_specs=in_specs, out_specs=out_specs, check_vma=False)
```

```python
import functools

import jax
import jax.numpy as jnp
from jax import lax
from jax.experimental import pallas as pl
from jax.experimental.pallas import tpu as pltpu
from jax.sharding import PartitionSpec as P

KEEP_BLK = 12
PANEL = 128
SUB = 8
EXTRA = 16
VMEM_LIMIT = 32 * 1024 * 1024
NT = (((1,), (1,)), ((), ()))
NN = (((1,), (0,)), ((), ()))


def split3(x):
    hi = x.astype(jnp.bfloat16)
    rest = x - hi.astype(jnp.float32)
    mid = rest.astype(jnp.bfloat16)
    low = (rest - mid.astype(jnp.float32)).astype(jnp.bfloat16)
    return hi, mid, low


def dot32(a, b, dims):
    return lax.dot_general(a, b, dims, preferred_element_type=jnp.float32)


def kept_blocks(flags_ref, index_ref):
    count = jnp.int32(0)
    for b in range(flags_ref.shape[0]):
        index_ref[count] = b
        count = count + flags_ref[b]


def select_kernel(flags_in_ref, tokens_ref, out_ref, flags_ref, index_ref, held_ref, sem, flags_sem):
    rows, features = tokens_ref.shape
    blocks = flags_ref.shape[0]
    width = features // blocks
    per_tile = 128 // width
    chunks = sem.shape[0]
    step = rows // chunks
    fetch = pltpu.make_async_copy(flags_in_ref, flags_ref, flags_sem)
    fetch.start()
    reads = []
    for c in range(chunks):
        part = pl.ds(c * step, step)
        reads.append(pltpu.make_async_copy(tokens_ref.at[part, :], held_ref.at[part, :], sem.at[c]))
        reads[-1].start()
    fetch.wait()
    kept_blocks(flags_ref, index_ref)
    row = lax.broadcasted_iota(jnp.int32, (width, 128), 0)
    lane = lax.broadcasted_iota(jnp.int32, (width, 128), 1)
    total = jnp.zeros((step, 128), jnp.float32)
    for c in range(chunks):
        reads[c].wait()
        part = slice(c * step, (c + 1) * step)
        for i in range(KEEP_BLK):
            b = index_ref[i]
            start = pl.multiple_of((b // per_tile) * 128, 128)
            pick = jnp.where(lane == row + (b % per_tile) * width, 1.0, 0.0).astype(jnp.bfloat16)
            picked = dot32(pick, held_ref[part, pl.ds(start, 128)], NT)
            out_ref[i * width:(i + 1) * width, part] = picked.astype(jnp.bfloat16)
        for f in range(features // 128):
            piece = held_ref[part, f * 128:(f + 1) * 128].astype(jnp.float32)
            total += piece * piece
    squares = jnp.sum(total)
    hi, mid, low = split3(jnp.full((EXTRA, rows), squares, jnp.float32))
    row = lax.broadcasted_iota(jnp.int32, (EXTRA, rows), 0)
    carried = jnp.where(
        row == 0,
        hi.astype(jnp.float32),
        jnp.where(row == 1, mid.astype(jnp.float32), jnp.where(row == 2, low.astype(jnp.float32), 0.0)),
    )
    out_ref[KEEP_BLK * width:, :] = carried.astype(jnp.bfloat16)


def select_kept(tokens, keep_flags):
    rows, features = tokens.shape
    blocks = keep_flags.shape[0]
    kept = KEEP_BLK * (features // blocks)
    chunks = rows // 128
    return pl.pallas_call(
        select_kernel,
        out_shape=jax.ShapeDtypeStruct((kept + EXTRA, rows), jnp.bfloat16),
        in_specs=[pl.BlockSpec(memory_space=pltpu.HBM)] * 2,
        out_specs=pl.BlockSpec(memory_space=pltpu.VMEM),
        scratch_shapes=[
            pltpu.SMEM((blocks,), jnp.int32),
            pltpu.SMEM((blocks + 1,), jnp.int32),
            pltpu.VMEM((rows, features), jnp.bfloat16),
            pltpu.SemaphoreType.DMA((chunks,)),
            pltpu.SemaphoreType.DMA,
        ],
        compiler_params=pltpu.CompilerParams(vmem_limit_bytes=VMEM_LIMIT),
        name="select_kept",
    )(keep_flags, tokens)


def lane_column(x, c):
    return jnp.broadcast_to(x[:, c:c + 1], (SUB, 128))


def sublane_row(x, t):
    return jnp.broadcast_to(x[t:t + 1, :], (SUB, 128))


def tree_sum(terms):
    while len(terms) > 1:
        pairs = [terms[i] + terms[i + 1] for i in range(0, len(terms) - 1, 2)]
        terms = pairs + terms[len(terms) - len(terms) % 2:]
    return terms[0]


def block_entries(block, base):
    entry = {}
    for j in range(SUB):
        column = lane_column(block, base + j)
        for i in range(j + 1):
            entry[i, j] = sublane_row(column, i)
    return entry


def solve_small(entry, rows, cross, ahead):
    entry, rows, cross, ahead = dict(entry), list(rows), list(cross), list(ahead)
    lower = {}
    for t in range(0, SUB, 2):
        u = t + 1
        a, b, c = entry[t, t], entry[t, u], entry[u, u]
        first = pl.reciprocal(a, approx=True)
        second = a * pl.reciprocal(a * c - b * b, approx=True)
        lower[u, t] = b * first
        later = range(u + 1, SUB)
        rest = {}
        for j in later:
            lower[j, t] = entry[t, j] * first
            rest[j] = entry[u, j] - b * lower[j, t]
        for j in later:
            for i in range(u + 1, j + 1):
                partial = entry[i, j] - entry[t, i] * lower[j, t]
                entry[i, j] = partial - (rest[i] * rest[j]) * second
        for j in later:
            lower[j, u] = rest[j] * second
        for part in (cross, rows):
            if part:
                part[u] = part[u] - lower[u, t] * part[t]
                for j in later:
                    part[j] = (part[j] - lower[j, t] * part[t]) - lower[j, u] * part[u]
        if cross:
            left, right = cross[t] * first, cross[u] * second
            for j in range(SUB):
                ahead[j] = (ahead[j] - left * sublane_row(cross[t], j)) - right * sublane_row(cross[u], j)
        rows[t] = rows[t] * first
        rows[u] = rows[u] * second
    following = {(i, j): sublane_row(ahead[j], i) for j in range(SUB) for i in range(j + 1) if cross}
    for t in reversed(range(SUB)):
        for j in range(t):
            rows[j] = rows[j] - lower[t, j] * rows[t]
    return rows, following


def factor_panel(block, beside=()):
    size = block.shape[0]
    count = size // SUB
    sub = lax.broadcasted_iota(jnp.int32, (SUB, 128), 0)
    lane = lax.broadcasted_iota(jnp.int32, (SUB, 128), 1)
    rows = [block[i * SUB:(i + 1) * SUB, :] for i in range(count)]
    entry = block_entries(rows[0], 0)
    lower, scaled = [], []
    done = 0
    for s in range(count):
        base = s * SUB
        inside = (lane >= base) & (lane < base + SUB)
        cross, ahead = [], []
        if s + 1 < count:
            cross = [lane_column(rows[s + 1], base + j) for j in range(SUB)]
            ahead = [lane_column(rows[s + 1], base + SUB + j) for j in range(SUB)]
        pivot_rows = jnp.where(inside, jnp.where(lane == sub + base, 1.0, 0.0), rows[s])
        spread, entry = solve_small(entry, [sublane_row(pivot_rows, j) for j in range(SUB)], cross, ahead)
        for i in range(s + 1, count):
            columns = cross if i == s + 1 else [lane_column(rows[i], base + j) for j in range(SUB)]
            change = tree_sum([columns[j] * spread[j] for j in range(SUB)])
            rows[i] = jnp.where(inside, 0.0, rows[i]) - change
        new = spread[SUB - 1]
        for j in range(SUB - 1):
            new = jnp.where(sub == j, spread[j], new)
        lower.append(jnp.where(lane < base + SUB, pivot_rows, 0.0))
        scaled.append(jnp.where(lane < base + SUB, new, 0.0))
        until = len(beside) * (s + 1) // count
        for task in beside[done:until]:
            task()
        done = until
    return jnp.concatenate(lower, axis=0), jnp.concatenate(scaled, axis=0)


def wide_left(x):
    hi, mid, low = split3(x)
    return jnp.concatenate([hi, hi, mid, hi, mid, low], axis=1)


def wide_right(x):
    hi, mid, low = split3(x)
    return jnp.concatenate([hi, mid, hi, low, mid, hi], axis=0)


def wide_across(x):
    hi, mid, low = split3(x)
    return jnp.concatenate([hi, mid, hi, low, mid, hi], axis=1)


def spans(low, high):
    first = low + (high - low) % 256
    starts = ([low] if first > low else []) + list(range(first, high, 256))
    return list(zip(starts, starts[1:] + [high]))


def settle_tasks(p, state, lower_ref, scaled_ref):
    a_ref, offset, _, w_ref, left_ref, right_ref = state
    kept = w_ref.shape[1]
    at = p * PANEL
    low = at + PANEL
    here = slice(at - offset, low - offset)
    rest = slice(low - offset, kept - offset)

    def make_w(c, d):
        value = dot32(wide_left(scaled_ref[...]), wide_right(a_ref[here, c - offset:d - offset]), NN)
        right_ref[:, c:d] = wide_right(value)

    def make_left():
        value = dot32(wide_left(a_ref[rest, here]), wide_across(lower_ref[...]), NT)
        left_ref[low:, :] = wide_left(value)

    def update(c, d):
        a_ref[rest, c - offset:d - offset] -= dot32(left_ref[low:, :], right_ref[:, c:d], NN)

    def place(c, d):
        a_ref[here, c - offset:d - offset] = dot32(wide_left(lower_ref[...].T), right_ref[:, c:d], NN)

    ranges = spans(low, kept)
    tasks = [functools.partial(make_w, c, d) for c, d in ranges] + [make_left]
    tasks += [functools.partial(update, c, d) for c, d in ranges]
    return tasks + [functools.partial(place, c, d) for c, d in ranges]


def panel(p, state, factors_ref, beside):
    a_ref, offset, next_ref = state[:3]
    at = p * PANEL - offset
    here, after = slice(at, at + PANEL), slice(at + PANEL, at + 2 * PANEL)
    lower, scaled = factor_panel(next_ref[...], beside)
    left = dot32(wide_left(a_ref[after, here]), wide_across(lower), NT)
    right = dot32(wide_left(scaled), wide_right(a_ref[here, after]), NN)
    next_ref[...] = a_ref[after, after] - dot32(wide_left(left), wide_right(right), NN)
    factors_ref[0] = lower
    factors_ref[1] = scaled


def factors_shape(count):
    return jax.ShapeDtypeStruct((count, 2, PANEL, PANEL), jnp.float32)


def work_scratch(kept):
    return [
        pltpu.VMEM((8, kept), jnp.float32),
        pltpu.VMEM((kept, 6 * PANEL), jnp.bfloat16),
        pltpu.VMEM((6 * PANEL, kept), jnp.bfloat16),
    ]


def place_pieces(pieces, all_ref, sem, chip=None, rows=0):
    copies = []
    at = 0
    for k, piece in enumerate(pieces):
        width = piece.shape[1]
        start = at
        if chip is not None:
            group = 2 * rows
            start = pl.multiple_of((chip ^ (at // group)) * group + at % group, 128)
        copies.append(pltpu.make_async_copy(piece, all_ref.at[:, pl.ds(start, width)], sem.at[k]))
        copies[-1].start()
        at += width
    return copies


def gram_columns(all_ref, kept, at, tile, rows):
    tokens = all_ref.shape[1]
    chunk = min(tokens, 2048) if tokens % 512 == 0 else rows
    acc = None
    for c in range(0, tokens, chunk):
        part = dot32(all_ref[:kept, c:c + chunk], all_ref[at:at + tile, c:c + chunk], NT)
        acc = part if acc is None else acc + part
    return acc


def square_sum(all_ref, kept, rows):
    total = jnp.float32(0.0)
    for k in range(0, all_ref.shape[1], rows):
        total = total + jnp.sum(all_ref[kept:, k:k + 1].astype(jnp.float32))
    return total


def early_gram(pieces):
    kept_extra, rows = pieces[0].shape
    kept = kept_extra - EXTRA
    count = len(pieces)
    tokens = sum(piece.shape[1] for piece in pieces)

    def body(*refs):
        out_ref, squares_ref, all_ref, sem = refs[count:]
        for copy in place_pieces(refs[:count], all_ref, sem):
            copy.wait()
        squares_ref[...] = jnp.full(squares_ref.shape, square_sum(all_ref, kept, rows), jnp.float32)
        for at in range(0, kept, 256):
            out_ref[:, at:at + 256] = gram_columns(all_ref, kept, at, 256, rows)

    return pl.pallas_call(
        body,
        out_shape=[
            jax.ShapeDtypeStruct((kept, kept), jnp.float32),
            jax.ShapeDtypeStruct((8, 128), jnp.float32),
        ],
        in_specs=[pl.BlockSpec(memory_space=pl.ANY)] * count,
        out_specs=[pl.BlockSpec(memory_space=pltpu.VMEM)] * 2,
        scratch_shapes=[
            pltpu.VMEM((kept_extra, tokens), jnp.bfloat16),
            pltpu.SemaphoreType.DMA((count,)),
        ],
        compiler_params=pltpu.CompilerParams(vmem_limit_bytes=VMEM_LIMIT),
        cost_estimate=pl.CostEstimate(
            flops=2 * kept * kept * tokens, bytes_accessed=8 * kept * kept, transcendentals=0
        ),
        name="early_gram",
    )(*pieces)


def first_kernel(features, rows, last, early_ref, squares_ref, *refs):
    a_ref, scale_ref, factors_ref, next_ref, all_ref, w_ref, left_ref, right_ref = refs[-8:]
    kept = a_ref.shape[0]
    total = squares_ref[...] + square_sum(all_ref, kept, rows)
    scale_ref[...] = 1.0 / (0.01 * total / features)
    scale = scale_ref[0:1, 0:1]

    def gram(at, tile):
        row = lax.broadcasted_iota(jnp.int32, (kept, tile), 0)
        lane = lax.broadcasted_iota(jnp.int32, (kept, tile), 1)
        value = early_ref[:, at:at + tile] + gram_columns(all_ref, kept, at, tile, rows)
        a_ref[:, at:at + tile] = value * scale + jnp.where(row == lane + at, 1.0, 0.0)

    gram(0, 256)
    next_ref[...] = a_ref[:PANEL, :PANEL]
    state = (a_ref, 0, next_ref, w_ref, left_ref, right_ref)
    for p in range(last):
        if p:
            tasks = settle_tasks(p - 1, state, factors_ref.at[p - 1, 0], factors_ref.at[p - 1, 1])
        else:
            tasks = [functools.partial(gram, at, 256) for at in range(256, kept, 256)]
        panel(p, state, factors_ref.at[p], tasks)


def first_part(early, squares, pieces, rows, features, last):
    kept = early.shape[0]
    count = len(pieces)
    tokens = sum(piece.shape[1] for piece in pieces)
    vmem = pl.BlockSpec(memory_space=pltpu.VMEM)

    def body(*refs):
        refs, sem = refs[:-1], refs[-1]
        for copy in place_pieces(refs[2:count + 2], refs[count + 6], sem):
            copy.wait()
        first_kernel(float(features), rows, last, *refs)

    return pl.pallas_call(
        body,
        out_shape=[
            jax.ShapeDtypeStruct((kept, kept), jnp.float32),
            jax.ShapeDtypeStruct((8, 128), jnp.float32),
            factors_shape(last),
            jax.ShapeDtypeStruct((PANEL, PANEL), jnp.float32),
        ],
        in_specs=[vmem] * 2 + [pl.BlockSpec(memory_space=pl.ANY)] * count,
        out_specs=[vmem] * 4,
        scratch_shapes=[
            pltpu.VMEM((kept + EXTRA, tokens), jnp.bfloat16),
            *work_scratch(kept),
            pltpu.SemaphoreType.DMA((count,)),
        ],
        compiler_params=pltpu.CompilerParams(vmem_limit_bytes=VMEM_LIMIT),
        name="gram_and_first_panels",
    )(early, squares, *pieces)


def dot_small(x, y, dims=NN):
    rows = x.shape[0]
    hi, mid, low = split3(x)
    yhi, ymid, ylow = split3(y)
    first = dot32(jnp.concatenate([hi, mid, low], axis=0), yhi, dims)
    second = dot32(jnp.concatenate([hi, mid], axis=0), ymid, dims)
    third = dot32(hi, ylow, dims)
    small = first[2 * rows:] + second[rows:] + third
    return small + (first[rows:2 * rows] + second[:rows]) + first[:rows]


def middle_kernel(first, last, start_ref, early_ref, start_next_ref, a_ref, factors_ref, next_ref, *work):
    kept = start_ref.shape[0]
    offset = kept - a_ref.shape[0]
    a_ref[...] = start_ref[offset:, offset:]
    next_ref[...] = start_next_ref[...]
    state = (a_ref, offset, next_ref, *work)
    for p in range(first, last):
        source = early_ref.at[p - 1] if p == first else factors_ref.at[p - 1 - first]
        panel(p, state, factors_ref.at[p - first], settle_tasks(p - 1, state, source.at[0], source.at[1]))


def middle_part(a, factors, follow, first, last):
    kept = a.shape[0]
    left = kept - (first - 1) * PANEL
    vmem = pl.BlockSpec(memory_space=pltpu.VMEM)
    return pl.pallas_call(
        functools.partial(middle_kernel, first, last),
        out_shape=[
            jax.ShapeDtypeStruct((left, left), jnp.float32),
            factors_shape(last - first),
            jax.ShapeDtypeStruct((PANEL, PANEL), jnp.float32),
        ],
        in_specs=[vmem] * 3,
        out_specs=[vmem] * 3,
        scratch_shapes=work_scratch(kept),
        compiler_params=pltpu.CompilerParams(vmem_limit_bytes=VMEM_LIMIT),
        name="middle_panels",
    )(a, factors, follow)


def last_kernel(begin, middle, copies, flags_ref, _, projected_ref, *refs):
    scale_ref, whole_ref, early_ref, start_ref, mid_ref, start_next_ref = refs[:6]
    out_ref, index_ref, wide_out_ref, all_ref, late_ref, a_ref, next_ref = refs[-10:-3]
    work = refs[-3:]
    own, features = out_ref.shape
    blocks = flags_ref.shape[0]
    width = features // blocks
    per_tile = 128 // width
    kept = whole_ref.shape[0]
    last = kept // PANEL - 1
    at = last * PANEL
    kept_blocks(flags_ref, index_ref)
    wide_out_ref[...] = jnp.zeros((own, features), jnp.float32)
    offset = kept - a_ref.shape[0]
    cut = start_ref.shape[0] - a_ref.shape[0]
    a_ref[...] = start_ref[cut:, cut:]
    next_ref[...] = start_next_ref[...]
    state = (a_ref, offset, next_ref, *work)
    held = {}

    def factor(p):
        source, skip = a_ref, offset
        if p < begin - 1:
            source, skip = whole_ref, 0
        elif p < middle - 1:
            source, skip = start_ref, kept - start_ref.shape[0]
        low = p * PANEL - skip
        return source[low:low + PANEL, low + PANEL:]

    def factors(p):
        if p < begin:
            return early_ref.at[p]
        return mid_ref.at[p - begin] if p < middle else late_ref.at[p - middle]

    def settle(p):
        return settle_tasks(p, state, factors(p).at[0], factors(p).at[1])

    def make_right():
        whole = jnp.concatenate([projected_ref[k] for k in range(projected_ref.shape[0])], axis=1)
        right = dot32(jnp.concatenate(split3(whole), axis=0), all_ref[:kept, :], NT)
        held["right"] = right[:own] + right[own:2 * own] + right[2 * own:]

    def forward(p):
        right = held["right"]
        held["z", p] = right[:, :PANEL]
        held["right"] = right[:, PANEL:] - dot_small(right[:, :PANEL], factor(p))

    def scaled(p):
        held["zd", p] = dot_small(dot_small(held["z", p], factors(p)[0], NT), factors(p)[1])

    def backward(p):
        if p == last:
            row = lax.broadcasted_iota(jnp.int32, (own + PANEL, PANEL), 0)
            lane = lax.broadcasted_iota(jnp.int32, (own + PANEL, PANEL), 1)
            held["back"] = jnp.where(row == lane + own, 1.0, 0.0)
        else:
            base = jnp.concatenate([held["zd", p], jnp.zeros((PANEL, PANEL), jnp.float32)], axis=0)
            value = base - dot_small(held["back"], factor(p), NT)
            held["back"] = jnp.concatenate([value, held["back"]], axis=1)

    def await_pieces():
        for copy in copies:
            copy.wait()

    for p in range(middle, last):
        tasks = settle(p - 1)
        if p == last - 1:
            tasks += [await_pieces, make_right] + [functools.partial(forward, q) for q in range(p)]
            tasks += [functools.partial(scaled, q) for q in range(p)]
        panel(p, state, late_ref.at[p - middle], tasks)
    tasks = settle(last - 1)
    tasks += [functools.partial(forward, last - 1), functools.partial(scaled, last - 1)]
    tasks += [functools.partial(backward, p) for p in reversed(range(last + 1))]
    lower, upper = factor_panel(next_ref[...], tasks)
    tail = dot_small(dot_small(held["right"], lower, NT), upper)
    scale = scale_ref[0:1, 0:1]
    front = held["back"][:own, :at] + dot_small(tail, held["back"][own:, :at])
    answer = [front[:, c:c + PANEL] * scale for c in range(0, at, PANEL)] + [tail * scale]
    place = lax.broadcasted_iota(jnp.int32, (own, 128), 1) // width
    for i in range(KEEP_BLK):
        b = index_ref[i]
        start = pl.multiple_of((b // per_tile) * 128, 128)
        inner = b % per_tile
        source = answer[i // per_tile]
        moved = pltpu.roll(source, width, 1)
        value = jnp.where(inner == i % per_tile, source, moved)
        old = wide_out_ref[:, pl.ds(start, 128)]
        wide_out_ref[:, pl.ds(start, 128)] = jnp.where(place == inner, value, old)
    out_ref[...] = wide_out_ref[...].astype(jnp.bfloat16)


def last_part(keep_flags, chip, projected, begun, pieces, features, begin, middle):
    own = projected.shape[1]
    blocks = keep_flags.shape[0]
    kept = begun[1].shape[0]
    count = len(pieces)
    tokens = sum(piece.shape[1] for piece in pieces)
    rows = pieces[0].shape[1]
    left = kept - (middle - 1) * PANEL
    smem = pl.BlockSpec(memory_space=pltpu.SMEM)
    vmem = pl.BlockSpec(memory_space=pltpu.VMEM)
    anywhere = pl.BlockSpec(memory_space=pl.ANY)

    def body(*refs):
        refs, sem = refs[:-1], refs[-1]
        ins = 3 + len(begun)
        copies = place_pieces(refs[ins:ins + count], refs[ins + count + 3], sem, refs[1][0], rows)
        last_kernel(begin, middle, copies, *refs)

    return pl.pallas_call(
        body,
        out_shape=jax.ShapeDtypeStruct((own, features), jnp.bfloat16),
        in_specs=[smem] * 2 + [vmem] * (1 + len(begun)) + [anywhere] * count,
        out_specs=vmem,
        scratch_shapes=[
            pltpu.SMEM((blocks + 1,), jnp.int32),
            pltpu.VMEM((own, features), jnp.float32),
            pltpu.VMEM((kept + EXTRA, tokens), jnp.bfloat16),
            pltpu.VMEM((kept // PANEL - 1 - middle, 2, PANEL, PANEL), jnp.float32),
            pltpu.VMEM((left, left), jnp.float32),
            pltpu.VMEM((PANEL, PANEL), jnp.float32),
            *work_scratch(kept),
            pltpu.SemaphoreType.DMA((count,)),
        ],
        compiler_params=pltpu.CompilerParams(vmem_limit_bytes=VMEM_LIMIT),
        name="last_panels_and_solution",
    )(keep_flags, chip, projected, *begun, *pieces)


def solution(mesh):
    n = mesh.shape["dp"]
    others = range(2, n, 2)

    def swap(x, k):
        return lax.ppermute(x, "dp", [(d, d ^ k) for d in range(n)])

    def gather_kept(kept):
        if n != 8:
            same = [kept] + [swap(kept, k) for k in others]
            pieces = [part for piece in same for part in (piece, swap(piece, 1))]
            early = early_gram(pieces[:n // 2])
            return pieces, early, pieces[n // 2:], same[-1]
        near = [swap(kept, 2), swap(kept, 4)]
        sibling = swap(kept, 1)
        near, sibling = lax.optimization_barrier((near, sibling))
        middle = kept.shape[1] // 2
        far = [swap(near[0][:, :middle], 4), swap(near[1][:, middle:], 2)]
        near_sibling = [swap(piece, 1) for piece in near]
        early = early_gram([kept, sibling, *near])
        far, early = lax.optimization_barrier((far, early))
        far_sibling = [swap(piece, 1) for piece in far]
        pieces = [kept, sibling, near[0], near_sibling[0], near[1], near_sibling[1], *far, *far_sibling]
        return pieces, early, [*near_sibling, *far, *far_sibling], far

    def on_device(tokens, orig_weight, keep_flags):
        features = tokens.shape[1]
        own = orig_weight.shape[0]
        rows = tokens.shape[0]
        kept = select_kept(tokens, keep_flags)
        panels = (kept.shape[0] - EXTRA) // PANEL
        begin = panels // 2
        middle = begin + 1
        tokens, kept = lax.optimization_barrier((tokens, kept))
        pieces, early, late, arrived = gather_kept(kept)
        orig_weight, arrived = lax.optimization_barrier((orig_weight, arrived))
        sibling = swap(tokens, 1)
        weights = [orig_weight] + [swap(orig_weight, k) for k in others]
        a, scale, factors, follow = first_part(*early, late, rows, features, begin)
        a, weights, sibling = lax.optimization_barrier((a, weights, sibling))
        chip = lax.axis_index("dp") // 2
        stacked = jnp.zeros((own * (n // 2), features), orig_weight.dtype)
        for k, part in enumerate(weights):
            stacked = lax.dynamic_update_slice(stacked, part, ((chip ^ k) * own, 0))
        projected = [
            lax.dot_general(stacked, part, NT, preferred_element_type=jnp.float32) for part in (tokens, sibling)
        ]
        projected, a = lax.optimization_barrier((jnp.concatenate(projected, axis=1), a))
        groups = [list(range(core, n, 2)) for core in range(2)]
        projected = lax.all_to_all(
            projected.reshape(n // 2, own, 2 * rows), "dp", 0, 0, axis_index_groups=groups
        )
        rest, more, follow = middle_part(a, factors, follow, begin, middle)
        begun = (scale, a, factors, rest, more, follow)
        mine = jnp.full((1,), chip, jnp.int32)
        return last_part(keep_flags, mine, projected, begun, pieces, features, begin, middle)

    in_specs = (P("dp", None), P(("section", "dp"), None), P())
    out_specs = P(("section", "dp"), None)
    return jax.shard_map(on_device, mesh=mesh, in_specs=in_specs, out_specs=out_specs, check_vma=False)
```

```python
import functools

import jax
import jax.numpy as jnp
from jax import lax
from jax.experimental import pallas as pl
from jax.experimental.pallas import tpu as pltpu
from jax.sharding import PartitionSpec as P

KEEP_BLK = 12
PANEL = 128
SUB = 8
EXTRA = 16
VMEM_LIMIT = 32 * 1024 * 1024
NT = (((1,), (1,)), ((), ()))
NN = (((1,), (0,)), ((), ()))


def split3(x):
    hi = x.astype(jnp.bfloat16)
    rest = x - hi.astype(jnp.float32)
    mid = rest.astype(jnp.bfloat16)
    low = (rest - mid.astype(jnp.float32)).astype(jnp.bfloat16)
    return hi, mid, low


def dot32(a, b, dims):
    return lax.dot_general(a, b, dims, preferred_element_type=jnp.float32)


def kept_blocks(flags_ref, index_ref):
    count = jnp.int32(0)
    for b in range(flags_ref.shape[0]):
        index_ref[count] = b
        count = count + flags_ref[b]


def select_kernel(side_ref, flags_in_ref, tokens_ref, out_ref, half_ref, *scratch):
    flags_ref, index_ref, held_ref, sem, flags_sem = scratch
    rows, features = tokens_ref.shape
    blocks = flags_ref.shape[0]
    width = features // blocks
    per_tile = 128 // width
    chunks = sem.shape[0]
    step = rows // chunks
    fetch = pltpu.make_async_copy(flags_in_ref, flags_ref, flags_sem)
    fetch.start()
    reads = []
    for c in range(chunks):
        part = pl.ds(c * step, step)
        reads.append(pltpu.make_async_copy(tokens_ref.at[part, :], held_ref.at[part, :], sem.at[c]))
        reads[-1].start()
    fetch.wait()
    kept_blocks(flags_ref, index_ref)
    row = lax.broadcasted_iota(jnp.int32, (width, 128), 0)
    lane = lax.broadcasted_iota(jnp.int32, (width, 128), 1)
    total = jnp.zeros((step, 128), jnp.float32)
    for c in range(chunks):
        reads[c].wait()
        part = slice(c * step, (c + 1) * step)
        for i in range(KEEP_BLK):
            b = index_ref[i]
            start = pl.multiple_of((b // per_tile) * 128, 128)
            pick = jnp.where(lane == row + (b % per_tile) * width, 1.0, 0.0).astype(jnp.bfloat16)
            picked = dot32(pick, held_ref[part, pl.ds(start, 128)], NT)
            out_ref[i * width:(i + 1) * width, part] = picked.astype(jnp.bfloat16)
        for f in range(features // 128):
            piece = held_ref[part, f * 128:(f + 1) * 128].astype(jnp.float32)
            total += piece * piece
    squares = jnp.sum(total)
    hi, mid, low = split3(jnp.full((EXTRA, rows), squares, jnp.float32))
    row = lax.broadcasted_iota(jnp.int32, (EXTRA, rows), 0)
    carried = jnp.where(
        row == 0,
        hi.astype(jnp.float32),
        jnp.where(row == 1, mid.astype(jnp.float32), jnp.where(row == 2, low.astype(jnp.float32), 0.0)),
    )
    kept = KEEP_BLK * width
    out_ref[kept:, :] = carried.astype(jnp.bfloat16)
    half = kept // 2
    half_ref[:half, :] = out_ref[pl.ds(pl.multiple_of(side_ref[0] * half, half), half), :]
    half_ref[half:, :] = carried.astype(jnp.bfloat16)


def select_kept(side, tokens, keep_flags):
    rows, features = tokens.shape
    blocks = keep_flags.shape[0]
    kept = KEEP_BLK * (features // blocks)
    chunks = rows // 128
    return pl.pallas_call(
        select_kernel,
        out_shape=[
            jax.ShapeDtypeStruct((kept + EXTRA, rows), jnp.bfloat16),
            jax.ShapeDtypeStruct((kept // 2 + EXTRA, rows), jnp.bfloat16),
        ],
        in_specs=[pl.BlockSpec(memory_space=pltpu.SMEM)] + [pl.BlockSpec(memory_space=pltpu.HBM)] * 2,
        out_specs=[pl.BlockSpec(memory_space=pltpu.VMEM)] * 2,
        scratch_shapes=[
            pltpu.SMEM((blocks,), jnp.int32),
            pltpu.SMEM((blocks + 1,), jnp.int32),
            pltpu.VMEM((rows, features), jnp.bfloat16),
            pltpu.SemaphoreType.DMA((chunks,)),
            pltpu.SemaphoreType.DMA,
        ],
        compiler_params=pltpu.CompilerParams(vmem_limit_bytes=VMEM_LIMIT),
        name="select_kept",
    )(side, keep_flags, tokens)


def lane_column(x, c):
    return jnp.broadcast_to(x[:, c:c + 1], (SUB, 128))


def sublane_row(x, t):
    return jnp.broadcast_to(x[t:t + 1, :], (SUB, 128))


def tree_sum(terms):
    while len(terms) > 1:
        pairs = [terms[i] + terms[i + 1] for i in range(0, len(terms) - 1, 2)]
        terms = pairs + terms[len(terms) - len(terms) % 2:]
    return terms[0]


def block_entries(block, base):
    entry = {}
    for j in range(SUB):
        column = lane_column(block, base + j)
        for i in range(j + 1):
            entry[i, j] = sublane_row(column, i)
    return entry


def solve_small(entry, rows, cross, ahead):
    entry, rows, cross, ahead = dict(entry), list(rows), list(cross), list(ahead)
    lower = {}
    for t in range(0, SUB, 2):
        u = t + 1
        a, b, c = entry[t, t], entry[t, u], entry[u, u]
        first = pl.reciprocal(a, approx=True)
        second = a * pl.reciprocal(a * c - b * b, approx=True)
        lower[u, t] = b * first
        later = range(u + 1, SUB)
        rest = {}
        for j in later:
            lower[j, t] = entry[t, j] * first
            rest[j] = entry[u, j] - b * lower[j, t]
        for j in later:
            for i in range(u + 1, j + 1):
                partial = entry[i, j] - entry[t, i] * lower[j, t]
                entry[i, j] = partial - (rest[i] * rest[j]) * second
        for j in later:
            lower[j, u] = rest[j] * second
        for part in (cross, rows):
            if part:
                part[u] = part[u] - lower[u, t] * part[t]
                for j in later:
                    part[j] = (part[j] - lower[j, t] * part[t]) - lower[j, u] * part[u]
        if cross:
            left, right = cross[t] * first, cross[u] * second
            for j in range(SUB):
                ahead[j] = (ahead[j] - left * sublane_row(cross[t], j)) - right * sublane_row(cross[u], j)
        rows[t] = rows[t] * first
        rows[u] = rows[u] * second
    following = {(i, j): sublane_row(ahead[j], i) for j in range(SUB) for i in range(j + 1) if cross}
    for t in reversed(range(SUB)):
        for j in range(t):
            rows[j] = rows[j] - lower[t, j] * rows[t]
    return rows, following


def factor_panel(block, beside=()):
    size = block.shape[0]
    count = size // SUB
    sub = lax.broadcasted_iota(jnp.int32, (SUB, 128), 0)
    lane = lax.broadcasted_iota(jnp.int32, (SUB, 128), 1)
    rows = [block[i * SUB:(i + 1) * SUB, :] for i in range(count)]
    entry = block_entries(rows[0], 0)
    lower, scaled = [], []
    done = 0
    for s in range(count):
        base = s * SUB
        inside = (lane >= base) & (lane < base + SUB)
        cross, ahead = [], []
        if s + 1 < count:
            cross = [lane_column(rows[s + 1], base + j) for j in range(SUB)]
            ahead = [lane_column(rows[s + 1], base + SUB + j) for j in range(SUB)]
        pivot_rows = jnp.where(inside, jnp.where(lane == sub + base, 1.0, 0.0), rows[s])
        spread, entry = solve_small(entry, [sublane_row(pivot_rows, j) for j in range(SUB)], cross, ahead)
        for i in range(s + 1, count):
            columns = cross if i == s + 1 else [lane_column(rows[i], base + j) for j in range(SUB)]
            change = tree_sum([columns[j] * spread[j] for j in range(SUB)])
            rows[i] = jnp.where(inside, 0.0, rows[i]) - change
        new = spread[SUB - 1]
        for j in range(SUB - 1):
            new = jnp.where(sub == j, spread[j], new)
        lower.append(jnp.where(lane < base + SUB, pivot_rows, 0.0))
        scaled.append(jnp.where(lane < base + SUB, new, 0.0))
        until = len(beside) * (s + 1) // count
        for task in beside[done:until]:
            task()
        done = until
    return jnp.concatenate(lower, axis=0), jnp.concatenate(scaled, axis=0)


def wide_left(x):
    hi, mid, low = split3(x)
    return jnp.concatenate([hi, hi, mid, hi, mid, low], axis=1)


def wide_right(x):
    hi, mid, low = split3(x)
    return jnp.concatenate([hi, mid, hi, low, mid, hi], axis=0)


def wide_across(x):
    hi, mid, low = split3(x)
    return jnp.concatenate([hi, mid, hi, low, mid, hi], axis=1)


def spans(low, high):
    first = low + (high - low) % 256
    starts = ([low] if first > low else []) + list(range(first, high, 256))
    return list(zip(starts, starts[1:] + [high]))


def settle_tasks(p, state, lower_ref, scaled_ref):
    a_ref, offset, _, w_ref, left_ref, right_ref = state
    kept = w_ref.shape[1]
    at = p * PANEL
    low = at + PANEL
    here = slice(at - offset, low - offset)
    rest = slice(low - offset, kept - offset)

    def make_w(c, d):
        value = dot32(wide_left(scaled_ref[...]), wide_right(a_ref[here, c - offset:d - offset]), NN)
        right_ref[:, c:d] = wide_right(value)

    def make_left():
        value = dot32(wide_left(a_ref[rest, here]), wide_across(lower_ref[...]), NT)
        left_ref[low:, :] = wide_left(value)

    def update(c, d):
        a_ref[rest, c - offset:d - offset] -= dot32(left_ref[low:, :], right_ref[:, c:d], NN)

    def place(c, d):
        a_ref[here, c - offset:d - offset] = dot32(wide_left(lower_ref[...].T), right_ref[:, c:d], NN)

    ranges = spans(low, kept)
    tasks = [functools.partial(make_w, c, d) for c, d in ranges] + [make_left]
    tasks += [functools.partial(update, c, d) for c, d in ranges]
    return tasks + [functools.partial(place, c, d) for c, d in ranges]


def panel(p, state, factors_ref, beside):
    a_ref, offset, next_ref = state[:3]
    at = p * PANEL - offset
    here, after = slice(at, at + PANEL), slice(at + PANEL, at + 2 * PANEL)
    lower, scaled = factor_panel(next_ref[...], beside)
    left = dot32(wide_left(a_ref[after, here]), wide_across(lower), NT)
    right = dot32(wide_left(scaled), wide_right(a_ref[here, after]), NN)
    next_ref[...] = a_ref[after, after] - dot32(wide_left(left), wide_right(right), NN)
    factors_ref[0] = lower
    factors_ref[1] = scaled


def factors_shape(count):
    return jax.ShapeDtypeStruct((count, 2, PANEL, PANEL), jnp.float32)


def work_scratch(kept):
    return [
        pltpu.VMEM((8, kept), jnp.float32),
        pltpu.VMEM((kept, 6 * PANEL), jnp.bfloat16),
        pltpu.VMEM((6 * PANEL, kept), jnp.bfloat16),
    ]


def flat(pieces):
    return [part for piece in pieces for part in (piece if isinstance(piece, tuple) else (piece,))]


def place_pieces(pieces, refs, side, all_ref, sem):
    refs = list(refs)
    moves = []
    at = 0
    for piece in pieces:
        if isinstance(piece, tuple):
            width = piece[0].shape[1]
            cols = pl.ds(at, width)
            half = piece[0].shape[0] - EXTRA
            mine, other = refs.pop(0), refs.pop(0)
            low = pl.multiple_of(side * half, half)
            high = pl.multiple_of((1 - side) * half, half)
            moves.append((mine.at[:half, :], all_ref.at[pl.ds(low, half), cols]))
            moves.append((other.at[:half, :], all_ref.at[pl.ds(high, half), cols]))
            moves.append((mine.at[half:, :], all_ref.at[pl.ds(2 * half, EXTRA), cols]))
        else:
            width = piece.shape[1]
            moves.append((refs.pop(0), all_ref.at[:, pl.ds(at, width)]))
        at += width
    copies = [pltpu.make_async_copy(a, b, sem.at[k]) for k, (a, b) in enumerate(moves)]
    for copy in copies:
        copy.start()
    return copies


def piece_scratch(pieces, kept):
    tokens = sum((piece[0] if isinstance(piece, tuple) else piece).shape[1] for piece in pieces)
    return pltpu.VMEM((kept + EXTRA, tokens), jnp.bfloat16), pltpu.SemaphoreType.DMA((3 * len(pieces),))


def gram_columns(all_ref, kept, at, tile):
    tokens = all_ref.shape[1]
    acc = None
    for c in range(0, tokens, 2048):
        d = min(c + 2048, tokens)
        part = dot32(all_ref[:kept, c:d], all_ref[at:at + tile, c:d], NT)
        acc = part if acc is None else acc + part
    return acc


def square_sum(all_ref, kept, rows):
    total = jnp.float32(0.0)
    for k in range(0, all_ref.shape[1], rows):
        total = total + jnp.sum(all_ref[kept:, k:k + 1].astype(jnp.float32))
    return total


def early_gram(pieces):
    kept_extra, rows = pieces[0].shape
    kept = kept_extra - EXTRA
    count = len(pieces)
    scratch = piece_scratch(pieces, kept)

    def body(*refs):
        out_ref, squares_ref, all_ref, sem = refs[count:]
        for copy in place_pieces(pieces, refs[:count], 0, all_ref, sem):
            copy.wait()
        squares_ref[...] = jnp.full(squares_ref.shape, square_sum(all_ref, kept, rows), jnp.float32)
        for at in range(0, kept, 256):
            out_ref[:, at:at + 256] = gram_columns(all_ref, kept, at, 256)

    return pl.pallas_call(
        body,
        out_shape=[
            jax.ShapeDtypeStruct((kept, kept), jnp.float32),
            jax.ShapeDtypeStruct((8, 128), jnp.float32),
        ],
        in_specs=[pl.BlockSpec(memory_space=pl.ANY)] * count,
        out_specs=[pl.BlockSpec(memory_space=pltpu.VMEM)] * 2,
        scratch_shapes=list(scratch),
        compiler_params=pltpu.CompilerParams(vmem_limit_bytes=VMEM_LIMIT),
        name="early_gram",
    )(*pieces)


def first_kernel(features, rows, last, early_ref, squares_ref, *refs):
    a_ref, scale_ref, factors_ref, next_ref, all_ref, w_ref, left_ref, right_ref = refs[-8:]
    kept = a_ref.shape[0]
    total = squares_ref[...] + square_sum(all_ref, kept, rows)
    scale_ref[...] = 1.0 / (0.01 * total / features)
    scale = scale_ref[0:1, 0:1]

    def gram(at, tile):
        row = lax.broadcasted_iota(jnp.int32, (kept, tile), 0)
        lane = lax.broadcasted_iota(jnp.int32, (kept, tile), 1)
        value = early_ref[:, at:at + tile] + gram_columns(all_ref, kept, at, tile)
        a_ref[:, at:at + tile] = value * scale + jnp.where(row == lane + at, 1.0, 0.0)

    gram(0, 256)
    next_ref[...] = a_ref[:PANEL, :PANEL]
    state = (a_ref, 0, next_ref, w_ref, left_ref, right_ref)
    for p in range(last):
        if p:
            tasks = settle_tasks(p - 1, state, factors_ref.at[p - 1, 0], factors_ref.at[p - 1, 1])
        else:
            tasks = [functools.partial(gram, at, 256) for at in range(256, kept, 256)]
        panel(p, state, factors_ref.at[p], tasks)


def first_part(side, early, squares, pieces, rows, features, last):
    kept = early.shape[0]
    count = len(flat(pieces))
    all_scratch, sem_scratch = piece_scratch(pieces, kept)
    vmem = pl.BlockSpec(memory_space=pltpu.VMEM)

    def body(*refs):
        side_ref, refs, sem = refs[0], refs[1:-1], refs[-1]
        for copy in place_pieces(pieces, refs[2:count + 2], side_ref[0], refs[count + 6], sem):
            copy.wait()
        first_kernel(float(features), rows, last, *refs)

    return pl.pallas_call(
        body,
        out_shape=[
            jax.ShapeDtypeStruct((kept, kept), jnp.float32),
            jax.ShapeDtypeStruct((8, 128), jnp.float32),
            factors_shape(last),
            jax.ShapeDtypeStruct((PANEL, PANEL), jnp.float32),
        ],
        in_specs=[pl.BlockSpec(memory_space=pltpu.SMEM)] + [vmem] * 2 + [pl.BlockSpec(memory_space=pl.ANY)] * count,
        out_specs=[vmem] * 4,
        scratch_shapes=[
            all_scratch,
            *work_scratch(kept),
            sem_scratch,
        ],
        compiler_params=pltpu.CompilerParams(vmem_limit_bytes=VMEM_LIMIT),
        name="gram_and_first_panels",
    )(side, early, squares, *flat(pieces))


def dot_small(x, y, dims=NN):
    rows = x.shape[0]
    hi, mid, low = split3(x)
    yhi, ymid, ylow = split3(y)
    first = dot32(jnp.concatenate([hi, mid, low], axis=0), yhi, dims)
    second = dot32(jnp.concatenate([hi, mid], axis=0), ymid, dims)
    third = dot32(hi, ylow, dims)
    small = first[2 * rows:] + second[rows:] + third
    return small + (first[rows:2 * rows] + second[:rows]) + first[:rows]


def middle_kernel(first, last, start_ref, early_ref, start_next_ref, a_ref, factors_ref, next_ref, *work):
    kept = start_ref.shape[0]
    offset = kept - a_ref.shape[0]
    a_ref[...] = start_ref[offset:, offset:]
    next_ref[...] = start_next_ref[...]
    state = (a_ref, offset, next_ref, *work)
    for p in range(first, last):
        source = early_ref.at[p - 1] if p == first else factors_ref.at[p - 1 - first]
        panel(p, state, factors_ref.at[p - first], settle_tasks(p - 1, state, source.at[0], source.at[1]))


def middle_part(a, factors, follow, first, last):
    kept = a.shape[0]
    left = kept - (first - 1) * PANEL
    vmem = pl.BlockSpec(memory_space=pltpu.VMEM)
    return pl.pallas_call(
        functools.partial(middle_kernel, first, last),
        out_shape=[
            jax.ShapeDtypeStruct((left, left), jnp.float32),
            factors_shape(last - first),
            jax.ShapeDtypeStruct((PANEL, PANEL), jnp.float32),
        ],
        in_specs=[vmem] * 3,
        out_specs=[vmem] * 3,
        scratch_shapes=work_scratch(kept),
        compiler_params=pltpu.CompilerParams(vmem_limit_bytes=VMEM_LIMIT),
        name="middle_panels",
    )(a, factors, follow)


def last_kernel(chips, begin, middle, copies, flags_ref, *refs):
    projected, refs = refs[:chips], refs[chips:]
    scale_ref, whole_ref, early_ref, start_ref, mid_ref, start_next_ref = refs[:6]
    out_ref, index_ref, wide_out_ref, all_ref, late_ref, a_ref, next_ref = refs[-10:-3]
    work = refs[-3:]
    own, features = out_ref.shape
    blocks = flags_ref.shape[0]
    width = features // blocks
    per_tile = 128 // width
    kept = whole_ref.shape[0]
    last = kept // PANEL - 1
    at = last * PANEL
    kept_blocks(flags_ref, index_ref)
    wide_out_ref[...] = jnp.zeros((own, features), jnp.float32)
    offset = kept - a_ref.shape[0]
    cut = start_ref.shape[0] - a_ref.shape[0]
    a_ref[...] = start_ref[cut:, cut:]
    next_ref[...] = start_next_ref[...]
    state = (a_ref, offset, next_ref, *work)
    held = {}

    def factor(p):
        source, skip = a_ref, offset
        if p < begin - 1:
            source, skip = whole_ref, 0
        elif p < middle - 1:
            source, skip = start_ref, kept - start_ref.shape[0]
        low = p * PANEL - skip
        return source[low:low + PANEL, low + PANEL:]

    def factors(p):
        if p < begin:
            return early_ref.at[p]
        return mid_ref.at[p - begin] if p < middle else late_ref.at[p - middle]

    def settle(p):
        return settle_tasks(p, state, factors(p).at[0], factors(p).at[1])

    def make_right():
        whole = jnp.concatenate([part[...] for part in projected], axis=1)
        right = dot32(jnp.concatenate(split3(whole), axis=0), all_ref[:kept, :], NT)
        held["right"] = right[:own] + right[own:2 * own] + right[2 * own:]

    def forward(p):
        right = held["right"]
        held["z", p] = right[:, :PANEL]
        held["right"] = right[:, PANEL:] - dot_small(right[:, :PANEL], factor(p))

    def scaled(p):
        held["zd", p] = dot_small(dot_small(held["z", p], factors(p)[0], NT), factors(p)[1])

    def backward(p):
        if p == last:
            row = lax.broadcasted_iota(jnp.int32, (own + PANEL, PANEL), 0)
            lane = lax.broadcasted_iota(jnp.int32, (own + PANEL, PANEL), 1)
            held["back"] = jnp.where(row == lane + own, 1.0, 0.0)
        else:
            base = jnp.concatenate([held["zd", p], jnp.zeros((PANEL, PANEL), jnp.float32)], axis=0)
            value = base - dot_small(held["back"], factor(p), NT)
            held["back"] = jnp.concatenate([value, held["back"]], axis=1)

    for copy in copies:
        copy.wait()
    for p in range(middle, last):
        tasks = settle(p - 1)
        if p == last - 1:
            tasks = [make_right] + [functools.partial(forward, q) for q in range(p - 1)] + tasks
            tasks += [functools.partial(forward, p - 1)] + [functools.partial(scaled, q) for q in range(p)]
        panel(p, state, late_ref.at[p - middle], tasks)
    tasks = settle(last - 1)
    tasks += [functools.partial(forward, last - 1), functools.partial(scaled, last - 1)]
    tasks += [functools.partial(backward, p) for p in reversed(range(last + 1))]
    lower, upper = factor_panel(next_ref[...], tasks)
    tail = dot_small(dot_small(held["right"], lower, NT), upper)
    scale = scale_ref[0:1, 0:1]
    front = held["back"][:own, :at] + dot_small(tail, held["back"][own:, :at])
    answer = [front[:, c:c + PANEL] * scale for c in range(0, at, PANEL)] + [tail * scale]
    place = lax.broadcasted_iota(jnp.int32, (own, 128), 1) // width
    for i in range(KEEP_BLK):
        b = index_ref[i]
        start = pl.multiple_of((b // per_tile) * 128, 128)
        inner = b % per_tile
        source = answer[i // per_tile]
        moved = pltpu.roll(source, width, 1)
        value = jnp.where(inner == i % per_tile, source, moved)
        old = wide_out_ref[:, pl.ds(start, 128)]
        wide_out_ref[:, pl.ds(start, 128)] = jnp.where(place == inner, value, old)
    out_ref[...] = wide_out_ref[...].astype(jnp.bfloat16)


def last_part(keep_flags, side, projected, begun, pieces, features, begin, middle):
    own = projected[0].shape[0]
    blocks = keep_flags.shape[0]
    chips = len(projected)
    kept = begun[1].shape[0]
    count = len(flat(pieces))
    all_scratch, sem_scratch = piece_scratch(pieces, kept)
    left = kept - (middle - 1) * PANEL
    vmem = pl.BlockSpec(memory_space=pltpu.VMEM)
    anywhere = pl.BlockSpec(memory_space=pl.ANY)

    def body(*refs):
        refs, sem = refs[:-1], refs[-1]
        side_ref, refs = refs[0], refs[1:]
        ins = 1 + chips + len(begun)
        copies = place_pieces(pieces, refs[ins:ins + count], side_ref[0], refs[ins + count + 3], sem)
        last_kernel(chips, begin, middle, copies, *refs)

    return pl.pallas_call(
        body,
        out_shape=jax.ShapeDtypeStruct((own, features), jnp.bfloat16),
        in_specs=[pl.BlockSpec(memory_space=pltpu.SMEM)] * 2 + [vmem] * (chips + len(begun)) + [anywhere] * count,
        out_specs=vmem,
        scratch_shapes=[
            pltpu.SMEM((blocks + 1,), jnp.int32),
            pltpu.VMEM((own, features), jnp.float32),
            all_scratch,
            pltpu.VMEM((kept // PANEL - 1 - middle, 2, PANEL, PANEL), jnp.float32),
            pltpu.VMEM((left, left), jnp.float32),
            pltpu.VMEM((PANEL, PANEL), jnp.float32),
            *work_scratch(kept),
            sem_scratch,
        ],
        compiler_params=pltpu.CompilerParams(vmem_limit_bytes=VMEM_LIMIT),
        name="last_panels_and_solution",
    )(side, keep_flags, *projected, *begun, *flat(pieces))


def solution(mesh):
    n = mesh.shape["dp"]
    others = range(2, n, 2)

    def swap(x, k):
        return lax.ppermute(x, "dp", [(d, d ^ k) for d in range(n)])

    def level(x):
        return lax.ppermute(x, "section", [(d, d ^ 1) for d in range(mesh.shape["section"])])

    def gather_kept(kept, half):
        if n != 8 or mesh.shape["section"] % 2:
            same = [kept] + [swap(kept, k) for k in others]
            pieces = [part for piece in same for part in (piece, swap(piece, 1))]
            return pieces, early_gram(pieces[:2]), same[-1]
        far = swap(half, 6)
        near = [swap(kept, 2), swap(kept, 4)]
        sibling = swap(kept, 1)
        other = level(far)
        far_sibling = swap(far, 1)
        early = early_gram([kept, sibling])
        near, early, far_sibling = lax.optimization_barrier((near, early, far_sibling))
        near_sibling = [swap(piece, 1) for piece in near]
        other_sibling = swap(other, 1)
        pieces = [kept, sibling, near[0], near_sibling[0], near[1], near_sibling[1]]
        return pieces + [(far, other), (far_sibling, other_sibling)], early, near

    def on_device(tokens, orig_weight, keep_flags):
        features = tokens.shape[1]
        own = orig_weight.shape[0]
        rows = tokens.shape[0]
        side = jnp.full((1,), lax.axis_index("section") % 2, jnp.int32)
        kept, half = select_kept(side, tokens, keep_flags)
        panels = (kept.shape[0] - EXTRA) // PANEL
        begin = panels // 2
        middle = begin + 1
        tokens, kept = lax.optimization_barrier((tokens, kept))
        pieces, early, arrived = gather_kept(kept, half)
        orig_weight, arrived = lax.optimization_barrier((orig_weight, arrived))
        sibling = swap(tokens, 1)
        weights = [orig_weight] + [swap(orig_weight, k) for k in others]
        a, scale, factors, follow = first_part(side, *early, pieces[2:], rows, features, begin)
        a, weights, sibling = lax.optimization_barrier((a, weights, sibling))
        stacked = jnp.concatenate(weights, axis=0)
        projected = [
            lax.dot_general(stacked, part, NT, preferred_element_type=jnp.float32) for part in (tokens, sibling)
        ]
        projected, a = lax.optimization_barrier((jnp.concatenate(projected, axis=1), a))
        parts = [projected[i * own:(i + 1) * own] for i in range(n // 2)]
        parts = [parts[0]] + [swap(part, k) for part, k in zip(parts[1:], others)]
        rest, more, follow = middle_part(a, factors, follow, begin, middle)
        begun = (scale, a, factors, rest, more, follow)
        return last_part(keep_flags, side, parts, begun, pieces, features, begin, middle)

    in_specs = (P("dp", None), P(("section", "dp"), None), P())
    out_specs = P(("section", "dp"), None)
    return jax.shard_map(on_device, mesh=mesh, in_specs=in_specs, out_specs=out_specs, check_vma=False)
```

```python
import functools

import jax
import jax.numpy as jnp
from jax import lax
from jax.experimental import pallas as pl
from jax.experimental.pallas import tpu as pltpu
from jax.sharding import PartitionSpec as P

KEEP_BLK = 12
PANEL = 128
SUB = 8
EXTRA = 16
VMEM_LIMIT = 32 * 1024 * 1024
NT = (((1,), (1,)), ((), ()))
NN = (((1,), (0,)), ((), ()))


def split3(x):
    hi = x.astype(jnp.bfloat16)
    rest = x - hi.astype(jnp.float32)
    mid = rest.astype(jnp.bfloat16)
    low = (rest - mid.astype(jnp.float32)).astype(jnp.bfloat16)
    return hi, mid, low


def dot32(a, b, dims):
    return lax.dot_general(a, b, dims, preferred_element_type=jnp.float32)


def kept_blocks(flags_ref, index_ref):
    count = jnp.int32(0)
    for b in range(flags_ref.shape[0]):
        index_ref[count] = b
        count = count + flags_ref[b]


def select_kernel(side_ref, flags_in_ref, tokens_ref, out_ref, half_ref, *scratch):
    flags_ref, index_ref, held_ref, sem, flags_sem = scratch
    rows, features = tokens_ref.shape
    blocks = flags_ref.shape[0]
    width = features // blocks
    per_tile = 128 // width
    chunks = sem.shape[0]
    step = rows // chunks
    fetch = pltpu.make_async_copy(flags_in_ref, flags_ref, flags_sem)
    fetch.start()
    reads = []
    for c in range(chunks):
        part = pl.ds(c * step, step)
        reads.append(pltpu.make_async_copy(tokens_ref.at[part, :], held_ref.at[part, :], sem.at[c]))
        reads[-1].start()
    fetch.wait()
    kept_blocks(flags_ref, index_ref)
    row = lax.broadcasted_iota(jnp.int32, (width, 128), 0)
    lane = lax.broadcasted_iota(jnp.int32, (width, 128), 1)
    total = jnp.zeros((step, 128), jnp.float32)
    for c in range(chunks):
        reads[c].wait()
        part = slice(c * step, (c + 1) * step)
        for i in range(KEEP_BLK):
            b = index_ref[i]
            start = pl.multiple_of((b // per_tile) * 128, 128)
            pick = jnp.where(lane == row + (b % per_tile) * width, 1.0, 0.0).astype(jnp.bfloat16)
            picked = dot32(pick, held_ref[part, pl.ds(start, 128)], NT)
            out_ref[i * width:(i + 1) * width, part] = picked.astype(jnp.bfloat16)
        for f in range(features // 128):
            piece = held_ref[part, f * 128:(f + 1) * 128].astype(jnp.float32)
            total += piece * piece
    squares = jnp.sum(total)
    hi, mid, low = split3(jnp.full((EXTRA, rows), squares, jnp.float32))
    row = lax.broadcasted_iota(jnp.int32, (EXTRA, rows), 0)
    carried = jnp.where(
        row == 0,
        hi.astype(jnp.float32),
        jnp.where(row == 1, mid.astype(jnp.float32), jnp.where(row == 2, low.astype(jnp.float32), 0.0)),
    )
    kept = KEEP_BLK * width
    out_ref[kept:, :] = carried.astype(jnp.bfloat16)
    half = kept // 2
    half_ref[:half, :] = out_ref[pl.ds(pl.multiple_of(side_ref[0] * half, half), half), :]
    half_ref[half:, :] = carried.astype(jnp.bfloat16)


def select_kept(side, tokens, keep_flags):
    rows, features = tokens.shape
    blocks = keep_flags.shape[0]
    kept = KEEP_BLK * (features // blocks)
    chunks = rows // 128
    return pl.pallas_call(
        select_kernel,
        out_shape=[
            jax.ShapeDtypeStruct((kept + EXTRA, rows), jnp.bfloat16),
            jax.ShapeDtypeStruct((kept // 2 + EXTRA, rows), jnp.bfloat16),
        ],
        in_specs=[pl.BlockSpec(memory_space=pltpu.SMEM)] + [pl.BlockSpec(memory_space=pltpu.HBM)] * 2,
        out_specs=[pl.BlockSpec(memory_space=pltpu.VMEM)] * 2,
        scratch_shapes=[
            pltpu.SMEM((blocks,), jnp.int32),
            pltpu.SMEM((blocks + 1,), jnp.int32),
            pltpu.VMEM((rows, features), jnp.bfloat16),
            pltpu.SemaphoreType.DMA((chunks,)),
            pltpu.SemaphoreType.DMA,
        ],
        compiler_params=pltpu.CompilerParams(vmem_limit_bytes=VMEM_LIMIT),
        name="select_kept",
    )(side, keep_flags, tokens)


def lane_column(x, c):
    return jnp.broadcast_to(x[:, c:c + 1], (SUB, 128))


def sublane_row(x, t):
    return jnp.broadcast_to(x[t:t + 1, :], (SUB, 128))


def tree_sum(terms):
    while len(terms) > 1:
        pairs = [terms[i] + terms[i + 1] for i in range(0, len(terms) - 1, 2)]
        terms = pairs + terms[len(terms) - len(terms) % 2:]
    return terms[0]


def block_entries(block, base):
    entry = {}
    for j in range(SUB):
        column = lane_column(block, base + j)
        for i in range(j + 1):
            entry[i, j] = sublane_row(column, i)
    return entry


def solve_small(entry, rows, cross, beyond, ahead):
    entry, rows, ahead = dict(entry), list(rows), list(ahead)
    cross, beyond = list(cross), list(beyond)
    lower = {}
    for t in range(0, SUB, 2):
        u = t + 1
        a, b, c = entry[t, t], entry[t, u], entry[u, u]
        first = pl.reciprocal(a, approx=True)
        second = a * pl.reciprocal(a * c - b * b, approx=True)
        lower[u, t] = b * first
        later = range(u + 1, SUB)
        rest = {}
        for j in later:
            lower[j, t] = entry[t, j] * first
            rest[j] = entry[u, j] - b * lower[j, t]
        for j in later:
            for i in range(u + 1, j + 1):
                partial = entry[i, j] - entry[t, i] * lower[j, t]
                entry[i, j] = partial - (rest[i] * rest[j]) * second
        for j in later:
            lower[j, u] = rest[j] * second
        for part in (cross, beyond, rows):
            if part:
                part[u] = part[u] - lower[u, t] * part[t]
                for j in later:
                    part[j] = (part[j] - lower[j, t] * part[t]) - lower[j, u] * part[u]
        if cross:
            left, right = cross[t] * first, cross[u] * second
            for j in range(SUB):
                ahead[j] = (ahead[j] - left * sublane_row(cross[t], j)) - right * sublane_row(cross[u], j)
        rows[t] = rows[t] * first
        rows[u] = rows[u] * second
    following = {(i, j): sublane_row(ahead[j], i) for j in range(SUB) for i in range(j + 1) if cross}
    forward = list(rows)
    for t in reversed(range(SUB)):
        for j in range(t):
            rows[j] = rows[j] - lower[t, j] * rows[t]
    return rows, forward, cross, beyond, following


def factor_panel(block, beside=()):
    size = block.shape[0]
    count = size // SUB
    sub = lax.broadcasted_iota(jnp.int32, (SUB, 128), 0)
    lane = lax.broadcasted_iota(jnp.int32, (SUB, 128), 1)
    rows = [block[i * SUB:(i + 1) * SUB, :] for i in range(count)]
    entry = block_entries(rows[0], 0)
    lower, scaled = [], []
    done = 0
    for s in range(count):
        base = s * SUB
        inside = (lane >= base) & (lane < base + SUB)
        cross, beyond, ahead = [], [], []
        if s + 2 < count:
            beyond = [lane_column(rows[s + 2], base + j) for j in range(SUB)]
        if s + 1 < count:
            cross = [lane_column(rows[s + 1], base + j) for j in range(SUB)]
            ahead = [lane_column(rows[s + 1], base + SUB + j) for j in range(SUB)]
        pivot_rows = jnp.where(inside, jnp.where(lane == sub + base, 1.0, 0.0), rows[s])
        spread_in = [sublane_row(pivot_rows, j) for j in range(SUB)]
        spread, forward, cross, beyond, entry = solve_small(entry, spread_in, cross, beyond, ahead)
        for i in range(s + 1, count):
            if i <= s + 2:
                columns, lines = (cross if i == s + 1 else beyond), forward
            else:
                columns, lines = [lane_column(rows[i], base + j) for j in range(SUB)], spread
            change = tree_sum([columns[j] * lines[j] for j in range(SUB)])
            rows[i] = jnp.where(inside, 0.0, rows[i]) - change
        new = spread[SUB - 1]
        for j in range(SUB - 1):
            new = jnp.where(sub == j, spread[j], new)
        lower.append(jnp.where(lane < base + SUB, pivot_rows, 0.0))
        scaled.append(jnp.where(lane < base + SUB, new, 0.0))
        until = len(beside) * (s + 1) // count
        for task in beside[done:until]:
            task()
        done = until
    return jnp.concatenate(lower, axis=0), jnp.concatenate(scaled, axis=0)


def wide_left(x):
    hi, mid, low = split3(x)
    return jnp.concatenate([hi, hi, mid, hi, mid, low], axis=1)


def wide_right(x):
    hi, mid, low = split3(x)
    return jnp.concatenate([hi, mid, hi, low, mid, hi], axis=0)


def wide_across(x):
    hi, mid, low = split3(x)
    return jnp.concatenate([hi, mid, hi, low, mid, hi], axis=1)


def spans(low, high):
    first = low + (high - low) % 256
    starts = ([low] if first > low else []) + list(range(first, high, 256))
    return list(zip(starts, starts[1:] + [high]))


def settle_tasks(p, state, lower_ref, scaled_ref):
    a_ref, offset, _, w_ref, left_ref, right_ref = state
    kept = w_ref.shape[1]
    at = p * PANEL
    low = at + PANEL
    here = slice(at - offset, low - offset)
    rest = slice(low - offset, kept - offset)

    def make_w(c, d):
        value = dot32(wide_left(scaled_ref[...]), wide_right(a_ref[here, c - offset:d - offset]), NN)
        right_ref[:, c:d] = wide_right(value)

    def make_left():
        value = dot32(wide_left(a_ref[rest, here]), wide_across(lower_ref[...]), NT)
        left_ref[low:, :] = wide_left(value)

    def update(c, d):
        a_ref[rest, c - offset:d - offset] -= dot32(left_ref[low:, :], right_ref[:, c:d], NN)

    def place(c, d):
        a_ref[here, c - offset:d - offset] = dot32(wide_left(lower_ref[...].T), right_ref[:, c:d], NN)

    ranges = spans(low, kept)
    tasks = [functools.partial(make_w, c, d) for c, d in ranges] + [make_left]
    tasks += [functools.partial(update, c, d) for c, d in ranges]
    return tasks + [functools.partial(place, c, d) for c, d in ranges]


def panel(p, state, factors_ref, beside):
    a_ref, offset, next_ref = state[:3]
    at = p * PANEL - offset
    here, after = slice(at, at + PANEL), slice(at + PANEL, at + 2 * PANEL)
    lower, scaled = factor_panel(next_ref[...], beside)
    left = dot32(wide_left(a_ref[after, here]), wide_across(lower), NT)
    right = dot32(wide_left(scaled), wide_right(a_ref[here, after]), NN)
    next_ref[...] = a_ref[after, after] - dot32(wide_left(left), wide_right(right), NN)
    factors_ref[0] = lower
    factors_ref[1] = scaled


def factors_shape(count):
    return jax.ShapeDtypeStruct((count, 2, PANEL, PANEL), jnp.float32)


def work_scratch(kept):
    return [
        pltpu.VMEM((8, kept), jnp.float32),
        pltpu.VMEM((kept, 6 * PANEL), jnp.bfloat16),
        pltpu.VMEM((6 * PANEL, kept), jnp.bfloat16),
    ]


def flat(pieces):
    return [part for piece in pieces for part in (piece if isinstance(piece, tuple) else (piece,))]


def place_pieces(pieces, refs, side, all_ref, sem):
    refs = list(refs)
    moves = []
    at = 0
    for piece in pieces:
        if isinstance(piece, tuple):
            width = piece[0].shape[1]
            cols = pl.ds(at, width)
            half = piece[0].shape[0] - EXTRA
            mine, other = refs.pop(0), refs.pop(0)
            low = pl.multiple_of(side * half, half)
            high = pl.multiple_of((1 - side) * half, half)
            moves.append((mine.at[:half, :], all_ref.at[pl.ds(low, half), cols]))
            moves.append((other.at[:half, :], all_ref.at[pl.ds(high, half), cols]))
            moves.append((mine.at[half:, :], all_ref.at[pl.ds(2 * half, EXTRA), cols]))
        else:
            width = piece.shape[1]
            moves.append((refs.pop(0), all_ref.at[:, pl.ds(at, width)]))
        at += width
    copies = [pltpu.make_async_copy(a, b, sem.at[k]) for k, (a, b) in enumerate(moves)]
    for copy in copies:
        copy.start()
    return copies


def piece_scratch(pieces, kept):
    tokens = sum((piece[0] if isinstance(piece, tuple) else piece).shape[1] for piece in pieces)
    return pltpu.VMEM((kept + EXTRA, tokens), jnp.bfloat16), pltpu.SemaphoreType.DMA((3 * len(pieces),))


def gram_columns(all_ref, kept, at, tile):
    tokens = all_ref.shape[1]
    acc = None
    for c in range(0, tokens, 2048):
        d = min(c + 2048, tokens)
        part = dot32(all_ref[:kept, c:d], all_ref[at:at + tile, c:d], NT)
        acc = part if acc is None else acc + part
    return acc


def square_sum(all_ref, kept, rows):
    total = jnp.float32(0.0)
    for k in range(0, all_ref.shape[1], rows):
        total = total + jnp.sum(all_ref[kept:, k:k + 1].astype(jnp.float32))
    return total


def early_gram(pieces, source):
    kept_extra, rows = pieces[0].shape
    kept = kept_extra - EXTRA
    count = len(pieces)
    scratch = piece_scratch(pieces, kept)

    def body(*refs):
        source_ref, out_ref, squares_ref, held_ref, all_ref, sem, held_sem = refs[count:]
        copies = place_pieces(pieces, refs[:count], 0, all_ref, sem)
        fetch = pltpu.make_async_copy(source_ref, held_ref, held_sem)
        fetch.start()
        for copy in copies:
            copy.wait()
        squares_ref[...] = jnp.full(squares_ref.shape, square_sum(all_ref, kept, rows), jnp.float32)
        for at in range(0, kept, 256):
            out_ref[:, at:at + 256] = gram_columns(all_ref, kept, at, 256)
        fetch.wait()

    return pl.pallas_call(
        body,
        out_shape=[
            jax.ShapeDtypeStruct((kept, kept), jnp.float32),
            jax.ShapeDtypeStruct((8, 128), jnp.float32),
            jax.ShapeDtypeStruct(source.shape, source.dtype),
        ],
        in_specs=[pl.BlockSpec(memory_space=pl.ANY)] * (count + 1),
        out_specs=[pl.BlockSpec(memory_space=pltpu.VMEM)] * 3,
        scratch_shapes=[*scratch, pltpu.SemaphoreType.DMA],
        compiler_params=pltpu.CompilerParams(vmem_limit_bytes=VMEM_LIMIT),
        name="early_gram",
    )(*pieces, source)


def first_kernel(features, rows, last, early_ref, squares_ref, *refs):
    a_ref, scale_ref, factors_ref, next_ref, all_ref, w_ref, left_ref, right_ref = refs[-8:]
    kept = a_ref.shape[0]
    total = squares_ref[...] + square_sum(all_ref, kept, rows)
    scale_ref[...] = 1.0 / (0.01 * total / features)
    scale = scale_ref[0:1, 0:1]

    def gram(at, tile):
        row = lax.broadcasted_iota(jnp.int32, (kept, tile), 0)
        lane = lax.broadcasted_iota(jnp.int32, (kept, tile), 1)
        value = early_ref[:, at:at + tile] + gram_columns(all_ref, kept, at, tile)
        a_ref[:, at:at + tile] = value * scale + jnp.where(row == lane + at, 1.0, 0.0)

    block = slice(0, PANEL)
    corner = early_ref[block, block] + dot32(all_ref[block, :], all_ref[block, :], NT)
    row = lax.broadcasted_iota(jnp.int32, (PANEL, PANEL), 0)
    lane = lax.broadcasted_iota(jnp.int32, (PANEL, PANEL), 1)
    next_ref[...] = corner * scale + jnp.where(row == lane, 1.0, 0.0)
    state = (a_ref, 0, next_ref, w_ref, left_ref, right_ref)
    for p in range(last):
        if p:
            tasks = settle_tasks(p - 1, state, factors_ref.at[p - 1, 0], factors_ref.at[p - 1, 1])
        else:
            tasks = [functools.partial(gram, at, 256) for at in range(0, kept, 256)]
        panel(p, state, factors_ref.at[p], tasks)


def first_part(side, early, squares, pieces, rows, features, last):
    kept = early.shape[0]
    count = len(flat(pieces))
    all_scratch, sem_scratch = piece_scratch(pieces, kept)
    vmem = pl.BlockSpec(memory_space=pltpu.VMEM)

    def body(*refs):
        side_ref, refs, sem = refs[0], refs[1:-1], refs[-1]
        for copy in place_pieces(pieces, refs[2:count + 2], side_ref[0], refs[count + 6], sem):
            copy.wait()
        first_kernel(float(features), rows, last, *refs)

    return pl.pallas_call(
        body,
        out_shape=[
            jax.ShapeDtypeStruct((kept, kept), jnp.float32),
            jax.ShapeDtypeStruct((8, 128), jnp.float32),
            factors_shape(last),
            jax.ShapeDtypeStruct((PANEL, PANEL), jnp.float32),
        ],
        in_specs=[pl.BlockSpec(memory_space=pltpu.SMEM)] + [vmem] * 2 + [pl.BlockSpec(memory_space=pl.ANY)] * count,
        out_specs=[vmem] * 4,
        scratch_shapes=[
            all_scratch,
            *work_scratch(kept),
            sem_scratch,
        ],
        compiler_params=pltpu.CompilerParams(vmem_limit_bytes=VMEM_LIMIT),
        name="gram_and_first_panels",
    )(side, early, squares, *flat(pieces))


def dot_small(x, y, dims=NN):
    rows = x.shape[0]
    hi, mid, low = split3(x)
    yhi, ymid, ylow = split3(y)
    first = dot32(jnp.concatenate([hi, mid, low], axis=0), yhi, dims)
    second = dot32(jnp.concatenate([hi, mid], axis=0), ymid, dims)
    third = dot32(hi, ylow, dims)
    small = first[2 * rows:] + second[rows:] + third
    return small + (first[rows:2 * rows] + second[:rows]) + first[:rows]


def middle_kernel(first, last, start_ref, early_ref, start_next_ref, a_ref, factors_ref, next_ref, *work):
    kept = start_ref.shape[0]
    offset = kept - a_ref.shape[0]
    a_ref[...] = start_ref[offset:, offset:]
    next_ref[...] = start_next_ref[...]
    state = (a_ref, offset, next_ref, *work)
    for p in range(first, last):
        source = early_ref.at[p - 1] if p == first else factors_ref.at[p - 1 - first]
        panel(p, state, factors_ref.at[p - first], settle_tasks(p - 1, state, source.at[0], source.at[1]))


def middle_part(a, factors, follow, first, last):
    kept = a.shape[0]
    left = kept - (first - 1) * PANEL
    vmem = pl.BlockSpec(memory_space=pltpu.VMEM)
    return pl.pallas_call(
        functools.partial(middle_kernel, first, last),
        out_shape=[
            jax.ShapeDtypeStruct((left, left), jnp.float32),
            factors_shape(last - first),
            jax.ShapeDtypeStruct((PANEL, PANEL), jnp.float32),
        ],
        in_specs=[vmem] * 3,
        out_specs=[vmem] * 3,
        scratch_shapes=work_scratch(kept),
        compiler_params=pltpu.CompilerParams(vmem_limit_bytes=VMEM_LIMIT),
        name="middle_panels",
    )(a, factors, follow)


def last_kernel(chips, begin, middle, copies, flags_ref, *refs):
    projected, refs = refs[:chips], refs[chips:]
    scale_ref, whole_ref, early_ref, start_ref, mid_ref, start_next_ref = refs[:6]
    out_ref, index_ref, wide_out_ref, all_ref, late_ref, a_ref, next_ref = refs[-10:-3]
    work = refs[-3:]
    own, features = out_ref.shape
    blocks = flags_ref.shape[0]
    width = features // blocks
    per_tile = 128 // width
    kept = whole_ref.shape[0]
    last = kept // PANEL - 1
    at = last * PANEL
    kept_blocks(flags_ref, index_ref)
    wide_out_ref[...] = jnp.zeros((own, features), jnp.float32)
    offset = kept - a_ref.shape[0]
    cut = start_ref.shape[0] - a_ref.shape[0]
    a_ref[...] = start_ref[cut:, cut:]
    next_ref[...] = start_next_ref[...]
    state = (a_ref, offset, next_ref, *work)
    held = {}

    def factor(p):
        source, skip = a_ref, offset
        if p < begin - 1:
            source, skip = whole_ref, 0
        elif p < middle - 1:
            source, skip = start_ref, kept - start_ref.shape[0]
        low = p * PANEL - skip
        return source[low:low + PANEL, low + PANEL:]

    def factors(p):
        if p < begin:
            return early_ref.at[p]
        return mid_ref.at[p - begin] if p < middle else late_ref.at[p - middle]

    def settle(p):
        return settle_tasks(p, state, factors(p).at[0], factors(p).at[1])

    def make_right():
        whole = jnp.concatenate([part[...] for part in projected], axis=1)
        right = dot32(jnp.concatenate(split3(whole), axis=0), all_ref[:kept, :], NT)
        held["right"] = right[:own] + right[own:2 * own] + right[2 * own:]

    def forward(p):
        right = held["right"]
        held["z", p] = right[:, :PANEL]
        held["right"] = right[:, PANEL:] - dot_small(right[:, :PANEL], factor(p))

    def scaled(p):
        held["zd", p] = dot_small(dot_small(held["z", p], factors(p)[0], NT), factors(p)[1])

    def backward(p):
        if p == last:
            row = lax.broadcasted_iota(jnp.int32, (own + PANEL, PANEL), 0)
            lane = lax.broadcasted_iota(jnp.int32, (own + PANEL, PANEL), 1)
            held["back"] = jnp.where(row == lane + own, 1.0, 0.0)
        else:
            base = jnp.concatenate([held["zd", p], jnp.zeros((PANEL, PANEL), jnp.float32)], axis=0)
            value = base - dot_small(held["back"], factor(p), NT)
            held["back"] = jnp.concatenate([value, held["back"]], axis=1)

    def await_pieces():
        for copy in copies:
            copy.wait()

    for p in range(middle, last):
        tasks = settle(p - 1)
        if p == last - 1:
            tasks += [await_pieces, make_right] + [functools.partial(forward, q) for q in range(p)]
            tasks += [functools.partial(scaled, q) for q in range(p)]
        panel(p, state, late_ref.at[p - middle], tasks)
    tasks = settle(last - 1)
    tasks += [functools.partial(forward, last - 1), functools.partial(scaled, last - 1)]
    tasks += [functools.partial(backward, p) for p in reversed(range(last + 1))]
    lower, upper = factor_panel(next_ref[...], tasks)
    tail = dot_small(dot_small(held["right"], lower, NT), upper)
    scale = scale_ref[0:1, 0:1]
    front = held["back"][:own, :at] + dot_small(tail, held["back"][own:, :at])
    answer = [front[:, c:c + PANEL] * scale for c in range(0, at, PANEL)] + [tail * scale]
    place = lax.broadcasted_iota(jnp.int32, (own, 128), 1) // width
    for i in range(KEEP_BLK):
        b = index_ref[i]
        start = pl.multiple_of((b // per_tile) * 128, 128)
        inner = b % per_tile
        source = answer[i // per_tile]
        moved = pltpu.roll(source, width, 1)
        value = jnp.where(inner == i % per_tile, source, moved)
        old = wide_out_ref[:, pl.ds(start, 128)]
        wide_out_ref[:, pl.ds(start, 128)] = jnp.where(place == inner, value, old)
    out_ref[...] = wide_out_ref[...].astype(jnp.bfloat16)


def last_part(keep_flags, side, projected, begun, pieces, features, begin, middle):
    own = projected[0].shape[0]
    blocks = keep_flags.shape[0]
    chips = len(projected)
    kept = begun[1].shape[0]
    count = len(flat(pieces))
    all_scratch, sem_scratch = piece_scratch(pieces, kept)
    left = kept - (middle - 1) * PANEL
    vmem = pl.BlockSpec(memory_space=pltpu.VMEM)
    anywhere = pl.BlockSpec(memory_space=pl.ANY)

    def body(*refs):
        refs, sem = refs[:-1], refs[-1]
        side_ref, refs = refs[0], refs[1:]
        ins = 1 + chips + len(begun)
        copies = place_pieces(pieces, refs[ins:ins + count], side_ref[0], refs[ins + count + 3], sem)
        last_kernel(chips, begin, middle, copies, *refs)

    return pl.pallas_call(
        body,
        out_shape=jax.ShapeDtypeStruct((own, features), jnp.bfloat16),
        in_specs=[pl.BlockSpec(memory_space=pltpu.SMEM)] * 2 + [vmem] * (chips + len(begun)) + [anywhere] * count,
        out_specs=vmem,
        scratch_shapes=[
            pltpu.SMEM((blocks + 1,), jnp.int32),
            pltpu.VMEM((own, features), jnp.float32),
            all_scratch,
            pltpu.VMEM((kept // PANEL - 1 - middle, 2, PANEL, PANEL), jnp.float32),
            pltpu.VMEM((left, left), jnp.float32),
            pltpu.VMEM((PANEL, PANEL), jnp.float32),
            *work_scratch(kept),
            sem_scratch,
        ],
        compiler_params=pltpu.CompilerParams(vmem_limit_bytes=VMEM_LIMIT),
        name="last_panels_and_solution",
    )(side, keep_flags, *projected, *begun, *flat(pieces))


def solution(mesh):
    n = mesh.shape["dp"]
    others = range(2, n, 2)

    def swap(x, k):
        return lax.ppermute(x, "dp", [(d, d ^ k) for d in range(n)])

    def level(x):
        return lax.ppermute(x, "section", [(d, d ^ 1) for d in range(mesh.shape["section"])])

    def gather_kept(kept, half, tokens):
        if n != 8 or mesh.shape["section"] % 2:
            same = [kept] + [swap(kept, k) for k in others]
            pieces = [part for piece in same for part in (piece, swap(piece, 1))]
            *early, held = early_gram(pieces[:2], tokens)
            return pieces, early, same[-1], held, swap(tokens, 1)
        far = swap(half, 6)
        near = [swap(kept, 2), swap(kept, 4)]
        sibling = swap(kept, 1)
        other = level(far)
        far_sibling = swap(far, 1)
        tokens_sibling = swap(tokens, 1)
        *early, held = early_gram([kept, sibling], tokens)
        near, early, far_sibling = lax.optimization_barrier((near, early, far_sibling))
        near_sibling = [swap(piece, 1) for piece in near]
        other_sibling = swap(other, 1)
        pieces = [kept, sibling, near[0], near_sibling[0], near[1], near_sibling[1]]
        pieces += [(far, other), (far_sibling, other_sibling)]
        return pieces, early, near, held, tokens_sibling

    def on_device(tokens, orig_weight, keep_flags):
        features = tokens.shape[1]
        own = orig_weight.shape[0]
        rows = tokens.shape[0]
        side = jnp.full((1,), lax.axis_index("section") % 2, jnp.int32)
        kept, half = select_kept(side, tokens, keep_flags)
        panels = (kept.shape[0] - EXTRA) // PANEL
        begin = panels // 2
        middle = begin + 1
        tokens, kept = lax.optimization_barrier((tokens, kept))
        pieces, early, arrived, tokens, sibling = gather_kept(kept, half, tokens)
        orig_weight, arrived = lax.optimization_barrier((orig_weight, arrived))
        weights = [orig_weight] + [swap(orig_weight, k) for k in others]
        a, scale, factors, follow = first_part(side, *early, pieces[2:], rows, features, begin)
        a, weights, sibling = lax.optimization_barrier((a, weights, sibling))
        stacked = jnp.concatenate(weights, axis=0)
        projected = [
            lax.dot_general(stacked, part, NT, preferred_element_type=jnp.float32) for part in (tokens, sibling)
        ]
        projected, a = lax.optimization_barrier((jnp.concatenate(projected, axis=1), a))
        parts = [projected[i * own:(i + 1) * own] for i in range(n // 2)]
        parts = [parts[0]] + [swap(part, k) for part, k in zip(parts[1:], others)]
        rest, more, follow = middle_part(a, factors, follow, begin, middle)
        begun = (scale, a, factors, rest, more, follow)
        return last_part(keep_flags, side, parts, begun, pieces, features, begin, middle)

    in_specs = (P("dp", None), P(("section", "dp"), None), P())
    out_specs = P(("section", "dp"), None)
    return jax.shard_map(on_device, mesh=mesh, in_specs=in_specs, out_specs=out_specs, check_vma=False)
```

```python
import functools

import jax
import jax.numpy as jnp
from jax import lax
from jax.experimental import pallas as pl
from jax.experimental.pallas import tpu as pltpu
from jax.sharding import PartitionSpec as P

KEEP_BLK = 12
PANEL = 128
SUB = 8
EXTRA = 16
VMEM_LIMIT = 32 * 1024 * 1024
NT = (((1,), (1,)), ((), ()))
NN = (((1,), (0,)), ((), ()))


def split3(x):
    hi = x.astype(jnp.bfloat16)
    rest = x - hi.astype(jnp.float32)
    mid = rest.astype(jnp.bfloat16)
    low = (rest - mid.astype(jnp.float32)).astype(jnp.bfloat16)
    return hi, mid, low


def dot32(a, b, dims):
    return lax.dot_general(a, b, dims, preferred_element_type=jnp.float32)


def kept_blocks(flags_ref, index_ref):
    count = jnp.int32(0)
    for b in range(flags_ref.shape[0]):
        index_ref[count] = b
        count = count + flags_ref[b]


def select_kernel(side_ref, flags_in_ref, tokens_ref, out_ref, half_ref, *scratch):
    flags_ref, index_ref, held_ref, sem, flags_sem = scratch
    rows, features = tokens_ref.shape
    blocks = flags_ref.shape[0]
    width = features // blocks
    per_tile = 128 // width
    chunks = sem.shape[0]
    step = rows // chunks
    fetch = pltpu.make_async_copy(flags_in_ref, flags_ref, flags_sem)
    fetch.start()
    reads = []
    for c in range(chunks):
        part = pl.ds(c * step, step)
        reads.append(pltpu.make_async_copy(tokens_ref.at[part, :], held_ref.at[part, :], sem.at[c]))
        reads[-1].start()
    fetch.wait()
    kept_blocks(flags_ref, index_ref)
    row = lax.broadcasted_iota(jnp.int32, (width, 128), 0)
    lane = lax.broadcasted_iota(jnp.int32, (width, 128), 1)
    total = jnp.zeros((step, 128), jnp.float32)
    for c in range(chunks):
        reads[c].wait()
        part = slice(c * step, (c + 1) * step)
        for i in range(KEEP_BLK):
            b = index_ref[i]
            start = pl.multiple_of((b // per_tile) * 128, 128)
            pick = jnp.where(lane == row + (b % per_tile) * width, 1.0, 0.0).astype(jnp.bfloat16)
            picked = dot32(pick, held_ref[part, pl.ds(start, 128)], NT)
            out_ref[i * width:(i + 1) * width, part] = picked.astype(jnp.bfloat16)
        for f in range(features // 128):
            piece = held_ref[part, f * 128:(f + 1) * 128].astype(jnp.float32)
            total += piece * piece
    squares = jnp.sum(total)
    hi, mid, low = split3(jnp.full((EXTRA, rows), squares, jnp.float32))
    row = lax.broadcasted_iota(jnp.int32, (EXTRA, rows), 0)
    carried = jnp.where(
        row == 0,
        hi.astype(jnp.float32),
        jnp.where(row == 1, mid.astype(jnp.float32), jnp.where(row == 2, low.astype(jnp.float32), 0.0)),
    )
    kept = KEEP_BLK * width
    out_ref[kept:, :] = carried.astype(jnp.bfloat16)
    half = kept // 2
    half_ref[:half, :] = out_ref[pl.ds(pl.multiple_of(side_ref[0] * half, half), half), :]
    half_ref[half:, :] = carried.astype(jnp.bfloat16)


def select_kept(side, tokens, keep_flags):
    rows, features = tokens.shape
    blocks = keep_flags.shape[0]
    kept = KEEP_BLK * (features // blocks)
    chunks = rows // 128
    return pl.pallas_call(
        select_kernel,
        out_shape=[
            jax.ShapeDtypeStruct((kept + EXTRA, rows), jnp.bfloat16),
            jax.ShapeDtypeStruct((kept // 2 + EXTRA, rows), jnp.bfloat16),
        ],
        in_specs=[pl.BlockSpec(memory_space=pltpu.SMEM)] + [pl.BlockSpec(memory_space=pltpu.HBM)] * 2,
        out_specs=[pl.BlockSpec(memory_space=pltpu.VMEM)] * 2,
        scratch_shapes=[
            pltpu.SMEM((blocks,), jnp.int32),
            pltpu.SMEM((blocks + 1,), jnp.int32),
            pltpu.VMEM((rows, features), jnp.bfloat16),
            pltpu.SemaphoreType.DMA((chunks,)),
            pltpu.SemaphoreType.DMA,
        ],
        compiler_params=pltpu.CompilerParams(vmem_limit_bytes=VMEM_LIMIT),
        name="select_kept",
    )(side, keep_flags, tokens)


def lane_column(x, c):
    return jnp.broadcast_to(x[:, c:c + 1], (SUB, 128))


def sublane_row(x, t):
    return jnp.broadcast_to(x[t:t + 1, :], (SUB, 128))


def tree_sum(terms):
    while len(terms) > 1:
        pairs = [terms[i] + terms[i + 1] for i in range(0, len(terms) - 1, 2)]
        terms = pairs + terms[len(terms) - len(terms) % 2:]
    return terms[0]


def block_entries(block, base):
    entry = {}
    for j in range(SUB):
        column = lane_column(block, base + j)
        for i in range(j + 1):
            entry[i, j] = sublane_row(column, i)
    return entry


def solve_small(entry, rows, cross, beyond, ahead):
    entry, rows, ahead = dict(entry), list(rows), list(ahead)
    cross, beyond = list(cross), list(beyond)
    lower = {}
    for t in range(0, SUB, 2):
        u = t + 1
        a, b, c = entry[t, t], entry[t, u], entry[u, u]
        first = pl.reciprocal(a, approx=True)
        second = a * pl.reciprocal(a * c - b * b, approx=True)
        lower[u, t] = b * first
        later = range(u + 1, SUB)
        rest = {}
        for j in later:
            lower[j, t] = entry[t, j] * first
            rest[j] = entry[u, j] - b * lower[j, t]
        for j in later:
            for i in range(u + 1, j + 1):
                partial = entry[i, j] - entry[t, i] * lower[j, t]
                entry[i, j] = partial - (rest[i] * rest[j]) * second
        for j in later:
            lower[j, u] = rest[j] * second
        for part in (cross, beyond, rows):
            if part:
                part[u] = part[u] - lower[u, t] * part[t]
                for j in later:
                    part[j] = (part[j] - lower[j, t] * part[t]) - lower[j, u] * part[u]
        if cross:
            left, right = cross[t] * first, cross[u] * second
            for j in range(SUB):
                ahead[j] = (ahead[j] - left * sublane_row(cross[t], j)) - right * sublane_row(cross[u], j)
        rows[t] = rows[t] * first
        rows[u] = rows[u] * second
    following = {(i, j): sublane_row(ahead[j], i) for j in range(SUB) for i in range(j + 1) if cross}
    forward = list(rows)
    for t in reversed(range(SUB)):
        for j in range(t):
            rows[j] = rows[j] - lower[t, j] * rows[t]
    return rows, forward, cross, beyond, following


def factor_panel(block, beside=()):
    size = block.shape[0]
    count = size // SUB
    sub = lax.broadcasted_iota(jnp.int32, (SUB, 128), 0)
    lane = lax.broadcasted_iota(jnp.int32, (SUB, 128), 1)
    rows = [block[i * SUB:(i + 1) * SUB, :] for i in range(count)]
    entry = block_entries(rows[0], 0)
    lower, scaled = [], []
    done = 0
    for s in range(count):
        base = s * SUB
        inside = (lane >= base) & (lane < base + SUB)
        cross, beyond, ahead = [], [], []
        if s + 2 < count:
            beyond = [lane_column(rows[s + 2], base + j) for j in range(SUB)]
        if s + 1 < count:
            cross = [lane_column(rows[s + 1], base + j) for j in range(SUB)]
            ahead = [lane_column(rows[s + 1], base + SUB + j) for j in range(SUB)]
        pivot_rows = jnp.where(inside, jnp.where(lane == sub + base, 1.0, 0.0), rows[s])
        spread_in = [sublane_row(pivot_rows, j) for j in range(SUB)]
        spread, forward, cross, beyond, entry = solve_small(entry, spread_in, cross, beyond, ahead)
        for i in range(s + 1, count):
            if i <= s + 2:
                columns, lines = (cross if i == s + 1 else beyond), forward
            else:
                columns, lines = [lane_column(rows[i], base + j) for j in range(SUB)], spread
            change = tree_sum([columns[j] * lines[j] for j in range(SUB)])
            rows[i] = jnp.where(inside, 0.0, rows[i]) - change
        new = spread[SUB - 1]
        for j in range(SUB - 1):
            new = jnp.where(sub == j, spread[j], new)
        lower.append(jnp.where(lane < base + SUB, pivot_rows, 0.0))
        scaled.append(jnp.where(lane < base + SUB, new, 0.0))
        until = len(beside) * (s + 1) // count
        for task in beside[done:until]:
            task()
        done = until
    return jnp.concatenate(lower, axis=0), jnp.concatenate(scaled, axis=0)


def wide_left(x):
    hi, mid, low = split3(x)
    return jnp.concatenate([hi, hi, mid, hi, mid, low], axis=1)


def wide_right(x):
    hi, mid, low = split3(x)
    return jnp.concatenate([hi, mid, hi, low, mid, hi], axis=0)


def wide_across(x):
    hi, mid, low = split3(x)
    return jnp.concatenate([hi, mid, hi, low, mid, hi], axis=1)


def spans(low, high):
    first = low + (high - low) % 256
    starts = ([low] if first > low else []) + list(range(first, high, 256))
    return list(zip(starts, starts[1:] + [high]))


def settle_tasks(p, state, lower_ref, scaled_ref):
    a_ref, offset, _, w_ref, left_ref, right_ref = state
    kept = w_ref.shape[1]
    at = p * PANEL
    low = at + PANEL
    here = slice(at - offset, low - offset)
    rest = slice(low - offset, kept - offset)

    def make_w(c, d):
        value = dot32(wide_left(scaled_ref[...]), wide_right(a_ref[here, c - offset:d - offset]), NN)
        right_ref[:, c:d] = wide_right(value)

    def make_left():
        value = dot32(wide_left(a_ref[rest, here]), wide_across(lower_ref[...]), NT)
        left_ref[low:, :] = wide_left(value)

    def update(c, d):
        a_ref[rest, c - offset:d - offset] -= dot32(left_ref[low:, :], right_ref[:, c:d], NN)

    def place(c, d):
        a_ref[here, c - offset:d - offset] = dot32(wide_left(lower_ref[...].T), right_ref[:, c:d], NN)

    ranges = spans(low, kept)
    tasks = [functools.partial(make_w, c, d) for c, d in ranges] + [make_left]
    tasks += [functools.partial(update, c, d) for c, d in ranges]
    return tasks + [functools.partial(place, c, d) for c, d in ranges]


def panel(p, state, factors_ref, beside):
    a_ref, offset, next_ref = state[:3]
    at = p * PANEL - offset
    here, after = slice(at, at + PANEL), slice(at + PANEL, at + 2 * PANEL)
    lower, scaled = factor_panel(next_ref[...], beside)
    left = dot32(wide_left(a_ref[after, here]), wide_across(lower), NT)
    right = dot32(wide_left(scaled), wide_right(a_ref[here, after]), NN)
    next_ref[...] = a_ref[after, after] - dot32(wide_left(left), wide_right(right), NN)
    factors_ref[0] = lower
    factors_ref[1] = scaled


def factors_shape(count):
    return jax.ShapeDtypeStruct((count, 2, PANEL, PANEL), jnp.float32)


def work_scratch(kept):
    return [
        pltpu.VMEM((8, kept), jnp.float32),
        pltpu.VMEM((kept, 6 * PANEL), jnp.bfloat16),
        pltpu.VMEM((6 * PANEL, kept), jnp.bfloat16),
    ]


def flat(pieces):
    return [part for piece in pieces for part in (piece if isinstance(piece, tuple) else (piece,))]


def place_pieces(pieces, refs, side, all_ref, sem):
    refs = list(refs)
    moves = []
    at = 0
    for piece in pieces:
        if isinstance(piece, tuple):
            width = piece[0].shape[1]
            cols = pl.ds(at, width)
            half = piece[0].shape[0] - EXTRA
            mine, other = refs.pop(0), refs.pop(0)
            low = pl.multiple_of(side * half, half)
            high = pl.multiple_of((1 - side) * half, half)
            moves.append((mine.at[:half, :], all_ref.at[pl.ds(low, half), cols]))
            moves.append((other.at[:half, :], all_ref.at[pl.ds(high, half), cols]))
            moves.append((mine.at[half:, :], all_ref.at[pl.ds(2 * half, EXTRA), cols]))
        else:
            width = piece.shape[1]
            moves.append((refs.pop(0), all_ref.at[:, pl.ds(at, width)]))
        at += width
    copies = [pltpu.make_async_copy(a, b, sem.at[k]) for k, (a, b) in enumerate(moves)]
    for copy in copies:
        copy.start()
    return copies


def piece_scratch(pieces, kept):
    tokens = sum((piece[0] if isinstance(piece, tuple) else piece).shape[1] for piece in pieces)
    return pltpu.VMEM((kept + EXTRA, tokens), jnp.bfloat16), pltpu.SemaphoreType.DMA((3 * len(pieces),))


def gram_columns(all_ref, kept, at, tile):
    tokens = all_ref.shape[1]
    acc = None
    for c in range(0, tokens, 2048):
        d = min(c + 2048, tokens)
        part = dot32(all_ref[:kept, c:d], all_ref[at:at + tile, c:d], NT)
        acc = part if acc is None else acc + part
    return acc


def square_sum(all_ref, kept, rows):
    total = jnp.float32(0.0)
    for k in range(0, all_ref.shape[1], rows):
        total = total + jnp.sum(all_ref[kept:, k:k + 1].astype(jnp.float32))
    return total


def early_gram(pieces, source):
    kept_extra, rows = pieces[0].shape
    kept = kept_extra - EXTRA
    count = len(pieces)
    scratch = piece_scratch(pieces, kept)

    def body(*refs):
        source_ref, out_ref, squares_ref, held_ref, all_ref, sem, held_sem = refs[count:]
        copies = place_pieces(pieces, refs[:count], 0, all_ref, sem)
        fetch = pltpu.make_async_copy(source_ref, held_ref, held_sem)
        fetch.start()
        for copy in copies:
            copy.wait()
        squares_ref[...] = jnp.full(squares_ref.shape, square_sum(all_ref, kept, rows), jnp.float32)
        for at in range(0, kept, 256):
            out_ref[:, at:at + 256] = gram_columns(all_ref, kept, at, 256)
        fetch.wait()

    return pl.pallas_call(
        body,
        out_shape=[
            jax.ShapeDtypeStruct((kept, kept), jnp.float32),
            jax.ShapeDtypeStruct((8, 128), jnp.float32),
            jax.ShapeDtypeStruct(source.shape, source.dtype),
        ],
        in_specs=[pl.BlockSpec(memory_space=pl.ANY)] * (count + 1),
        out_specs=[pl.BlockSpec(memory_space=pltpu.VMEM)] * 3,
        scratch_shapes=[*scratch, pltpu.SemaphoreType.DMA],
        compiler_params=pltpu.CompilerParams(vmem_limit_bytes=VMEM_LIMIT),
        name="early_gram",
    )(*pieces, source)


def first_kernel(features, rows, last, fetch, squares_ref, *refs):
    a_ref, scale_ref, factors_ref, next_ref, all_ref, corner_ref, w_ref, left_ref, right_ref = refs[-9:]
    kept = a_ref.shape[0]
    total = squares_ref[...] + square_sum(all_ref, kept, rows)
    scale_ref[...] = 1.0 / (0.01 * total / features)
    scale = scale_ref[0:1, 0:1]

    def gram(at, tile):
        row = lax.broadcasted_iota(jnp.int32, (kept, tile), 0)
        lane = lax.broadcasted_iota(jnp.int32, (kept, tile), 1)
        value = a_ref[:, at:at + tile] + gram_columns(all_ref, kept, at, tile)
        a_ref[:, at:at + tile] = value * scale + jnp.where(row == lane + at, 1.0, 0.0)

    block = slice(0, PANEL)
    corner = corner_ref[...] + dot32(all_ref[block, :], all_ref[block, :], NT)
    row = lax.broadcasted_iota(jnp.int32, (PANEL, PANEL), 0)
    lane = lax.broadcasted_iota(jnp.int32, (PANEL, PANEL), 1)
    next_ref[...] = corner * scale + jnp.where(row == lane, 1.0, 0.0)
    state = (a_ref, 0, next_ref, w_ref, left_ref, right_ref)
    for p in range(last):
        if p:
            tasks = settle_tasks(p - 1, state, factors_ref.at[p - 1, 0], factors_ref.at[p - 1, 1])
        else:
            tasks = [fetch.wait] + [functools.partial(gram, at, 256) for at in range(0, kept, 256)]
        panel(p, state, factors_ref.at[p], tasks)


def first_part(side, early, squares, pieces, rows, features, last):
    kept = early.shape[0]
    count = len(flat(pieces))
    all_scratch, sem_scratch = piece_scratch(pieces, kept)
    vmem = pl.BlockSpec(memory_space=pltpu.VMEM)
    anywhere = pl.BlockSpec(memory_space=pl.ANY)

    def body(*refs):
        side_ref, early_ref, refs, sem, early_sem = refs[0], refs[1], refs[2:-2], refs[-2], refs[-1]
        a_ref, all_ref, corner_ref = refs[count + 1], refs[count + 5], refs[count + 6]
        block = pl.ds(0, PANEL)
        corner = pltpu.make_async_copy(early_ref.at[block, block], corner_ref, early_sem.at[0])
        corner.start()
        copies = place_pieces(pieces, refs[1:count + 1], side_ref[0], all_ref, sem)
        fetch = pltpu.make_async_copy(early_ref, a_ref, early_sem.at[1])
        fetch.start()
        for copy in [corner, *copies]:
            copy.wait()
        first_kernel(float(features), rows, last, fetch, *refs)

    return pl.pallas_call(
        body,
        out_shape=[
            jax.ShapeDtypeStruct((kept, kept), jnp.float32),
            jax.ShapeDtypeStruct((8, 128), jnp.float32),
            factors_shape(last),
            jax.ShapeDtypeStruct((PANEL, PANEL), jnp.float32),
        ],
        in_specs=[pl.BlockSpec(memory_space=pltpu.SMEM), anywhere, vmem] + [anywhere] * count,
        out_specs=[vmem] * 4,
        scratch_shapes=[
            all_scratch,
            pltpu.VMEM((PANEL, PANEL), jnp.float32),
            *work_scratch(kept),
            sem_scratch,
            pltpu.SemaphoreType.DMA((2,)),
        ],
        compiler_params=pltpu.CompilerParams(vmem_limit_bytes=VMEM_LIMIT),
        name="gram_and_first_panels",
    )(side, early, squares, *flat(pieces))


def dot_small(x, y, dims=NN):
    rows = x.shape[0]
    hi, mid, low = split3(x)
    yhi, ymid, ylow = split3(y)
    first = dot32(jnp.concatenate([hi, mid, low], axis=0), yhi, dims)
    second = dot32(jnp.concatenate([hi, mid], axis=0), ymid, dims)
    third = dot32(hi, ylow, dims)
    small = first[2 * rows:] + second[rows:] + third
    return small + (first[rows:2 * rows] + second[:rows]) + first[:rows]


def middle_kernel(first, last, start_ref, early_ref, start_next_ref, a_ref, factors_ref, next_ref, *work):
    *work, sem = work
    kept = start_ref.shape[0]
    offset = kept - a_ref.shape[0]
    live = pl.ds(offset, kept - offset)
    fetch = pltpu.make_async_copy(start_ref.at[live, live], a_ref, sem)
    fetch.start()
    fetch.wait()
    next_ref[...] = start_next_ref[...]
    state = (a_ref, offset, next_ref, *work)
    for p in range(first, last):
        source = early_ref.at[p - 1] if p == first else factors_ref.at[p - 1 - first]
        panel(p, state, factors_ref.at[p - first], settle_tasks(p - 1, state, source.at[0], source.at[1]))


def middle_part(a, factors, follow, first, last):
    kept = a.shape[0]
    left = kept - (first - 1) * PANEL
    vmem = pl.BlockSpec(memory_space=pltpu.VMEM)
    return pl.pallas_call(
        functools.partial(middle_kernel, first, last),
        out_shape=[
            jax.ShapeDtypeStruct((left, left), jnp.float32),
            factors_shape(last - first),
            jax.ShapeDtypeStruct((PANEL, PANEL), jnp.float32),
        ],
        in_specs=[pl.BlockSpec(memory_space=pl.ANY)] + [vmem] * 2,
        out_specs=[vmem] * 3,
        scratch_shapes=[*work_scratch(kept), pltpu.SemaphoreType.DMA],
        compiler_params=pltpu.CompilerParams(vmem_limit_bytes=VMEM_LIMIT),
        name="middle_panels",
    )(a, factors, follow)


def last_kernel(chips, begin, middle, copies, flags_ref, *refs):
    projected, refs = refs[:chips], refs[chips:]
    scale_ref, whole_ref, early_ref, start_ref, mid_ref, start_next_ref = refs[:6]
    out_ref, index_ref, wide_out_ref, all_ref, late_ref, a_ref, next_ref = refs[-13:-6]
    top_ref, mid_rows_ref, *work = refs[-6:-1]
    sem = refs[-1]
    own, features = out_ref.shape
    blocks = flags_ref.shape[0]
    width = features // blocks
    per_tile = 128 // width
    kept = whole_ref.shape[0]
    last = kept // PANEL - 1
    at = last * PANEL
    kept_blocks(flags_ref, index_ref)
    wide_out_ref[...] = jnp.zeros((own, features), jnp.float32)
    offset = kept - a_ref.shape[0]
    cut = start_ref.shape[0] - a_ref.shape[0]
    live = pl.ds(cut, a_ref.shape[0])
    fetches = [
        pltpu.make_async_copy(start_ref.at[live, live], a_ref, sem.at[0]),
        pltpu.make_async_copy(start_ref.at[pl.ds(0, cut), :], mid_rows_ref, sem.at[1]),
        pltpu.make_async_copy(whole_ref.at[pl.ds(0, top_ref.shape[0]), :], top_ref, sem.at[2]),
    ]
    for fetch in fetches:
        fetch.start()
    next_ref[...] = start_next_ref[...]
    state = (a_ref, offset, next_ref, *work)
    held = {}

    def factor(p):
        source, skip = a_ref, offset
        if p < begin - 1:
            source, skip = top_ref, 0
        elif p < middle - 1:
            source, skip = mid_rows_ref, kept - start_ref.shape[0]
        low = p * PANEL - skip
        return source[low:low + PANEL, low + PANEL:]

    def factors(p):
        if p < begin:
            return early_ref.at[p]
        return mid_ref.at[p - begin] if p < middle else late_ref.at[p - middle]

    def settle(p):
        return settle_tasks(p, state, factors(p).at[0], factors(p).at[1])

    def make_right():
        whole = jnp.concatenate([part[...] for part in projected], axis=1)
        right = dot32(jnp.concatenate(split3(whole), axis=0), all_ref[:kept, :], NT)
        held["right"] = right[:own] + right[own:2 * own] + right[2 * own:]

    def forward(p):
        right = held["right"]
        held["z", p] = right[:, :PANEL]
        held["right"] = right[:, PANEL:] - dot_small(right[:, :PANEL], factor(p))

    def scaled(p):
        held["zd", p] = dot_small(dot_small(held["z", p], factors(p)[0], NT), factors(p)[1])

    def backward(p):
        if p == last:
            row = lax.broadcasted_iota(jnp.int32, (own + PANEL, PANEL), 0)
            lane = lax.broadcasted_iota(jnp.int32, (own + PANEL, PANEL), 1)
            held["back"] = jnp.where(row == lane + own, 1.0, 0.0)
        else:
            base = jnp.concatenate([held["zd", p], jnp.zeros((PANEL, PANEL), jnp.float32)], axis=0)
            value = base - dot_small(held["back"], factor(p), NT)
            held["back"] = jnp.concatenate([value, held["back"]], axis=1)

    for copy in fetches + copies:
        copy.wait()
    for p in range(middle, last):
        tasks = settle(p - 1)
        if p == last - 1:
            tasks = [make_right] + [functools.partial(forward, q) for q in range(p - 1)] + tasks
            tasks += [functools.partial(forward, p - 1)] + [functools.partial(scaled, q) for q in range(p)]
        panel(p, state, late_ref.at[p - middle], tasks)
    tasks = settle(last - 1)
    tasks += [functools.partial(forward, last - 1), functools.partial(scaled, last - 1)]
    tasks += [functools.partial(backward, p) for p in reversed(range(last + 1))]
    lower, upper = factor_panel(next_ref[...], tasks)
    tail = dot_small(dot_small(held["right"], lower, NT), upper)
    scale = scale_ref[0:1, 0:1]
    front = held["back"][:own, :at] + dot_small(tail, held["back"][own:, :at])
    answer = [front[:, c:c + PANEL] * scale for c in range(0, at, PANEL)] + [tail * scale]
    place = lax.broadcasted_iota(jnp.int32, (own, 128), 1) // width
    for i in range(KEEP_BLK):
        b = index_ref[i]
        start = pl.multiple_of((b // per_tile) * 128, 128)
        inner = b % per_tile
        source = answer[i // per_tile]
        moved = pltpu.roll(source, width, 1)
        value = jnp.where(inner == i % per_tile, source, moved)
        old = wide_out_ref[:, pl.ds(start, 128)]
        wide_out_ref[:, pl.ds(start, 128)] = jnp.where(place == inner, value, old)
    out_ref[...] = wide_out_ref[...].astype(jnp.bfloat16)


def last_part(keep_flags, side, projected, begun, pieces, features, begin, middle):
    own = projected[0].shape[0]
    blocks = keep_flags.shape[0]
    chips = len(projected)
    kept = begun[1].shape[0]
    count = len(flat(pieces))
    all_scratch, sem_scratch = piece_scratch(pieces, kept)
    left = kept - (middle - 1) * PANEL
    vmem = pl.BlockSpec(memory_space=pltpu.VMEM)
    anywhere = pl.BlockSpec(memory_space=pl.ANY)

    def body(*refs):
        refs, sem = refs[:-1], refs[-1]
        side_ref, refs = refs[0], refs[1:]
        ins = 1 + chips + len(begun)
        copies = place_pieces(pieces, refs[ins:ins + count], side_ref[0], refs[ins + count + 3], sem)
        last_kernel(chips, begin, middle, copies, *refs)

    return pl.pallas_call(
        body,
        out_shape=jax.ShapeDtypeStruct((own, features), jnp.bfloat16),
        in_specs=[pl.BlockSpec(memory_space=pltpu.SMEM)] * 2
        + [vmem] * (chips + 1)
        + [anywhere, vmem, anywhere, vmem, vmem]
        + [anywhere] * count,
        out_specs=vmem,
        scratch_shapes=[
            pltpu.SMEM((blocks + 1,), jnp.int32),
            pltpu.VMEM((own, features), jnp.float32),
            all_scratch,
            pltpu.VMEM((kept // PANEL - 1 - middle, 2, PANEL, PANEL), jnp.float32),
            pltpu.VMEM((left, left), jnp.float32),
            pltpu.VMEM((PANEL, PANEL), jnp.float32),
            pltpu.VMEM(((begin - 1) * PANEL, kept), jnp.float32),
            pltpu.VMEM(((middle - begin) * PANEL, kept - (begin - 1) * PANEL), jnp.float32),
            *work_scratch(kept),
            pltpu.SemaphoreType.DMA((3,)),
            sem_scratch,
        ],
        compiler_params=pltpu.CompilerParams(vmem_limit_bytes=VMEM_LIMIT),
        name="last_panels_and_solution",
    )(side, keep_flags, *projected, *begun, *flat(pieces))


def solution(mesh):
    n = mesh.shape["dp"]
    others = range(2, n, 2)

    def swap(x, k):
        return lax.ppermute(x, "dp", [(d, d ^ k) for d in range(n)])

    def level(x):
        return lax.ppermute(x, "section", [(d, d ^ 1) for d in range(mesh.shape["section"])])

    def gather_kept(kept, half, tokens):
        if n != 8 or mesh.shape["section"] % 2:
            same = [kept] + [swap(kept, k) for k in others]
            pieces = [part for piece in same for part in (piece, swap(piece, 1))]
            *early, held = early_gram(pieces[:2], tokens)
            return pieces, early, same[-1], held, swap(tokens, 1)
        far = swap(half, 6)
        near = [swap(kept, 2), swap(kept, 4)]
        sibling = swap(kept, 1)
        other = level(far)
        far_sibling = swap(far, 1)
        tokens_sibling = swap(tokens, 1)
        *early, held = early_gram([kept, sibling], tokens)
        near, early, far_sibling = lax.optimization_barrier((near, early, far_sibling))
        near_sibling = [swap(piece, 1) for piece in near]
        other_sibling = swap(other, 1)
        pieces = [kept, sibling, near[0], near_sibling[0], near[1], near_sibling[1]]
        pieces += [(far, other), (far_sibling, other_sibling)]
        return pieces, early, near, held, tokens_sibling

    def on_device(tokens, orig_weight, keep_flags):
        features = tokens.shape[1]
        own = orig_weight.shape[0]
        rows = tokens.shape[0]
        side = jnp.full((1,), lax.axis_index("section") % 2, jnp.int32)
        kept, half = select_kept(side, tokens, keep_flags)
        panels = (kept.shape[0] - EXTRA) // PANEL
        begin = panels // 2
        middle = begin + 1
        tokens, kept = lax.optimization_barrier((tokens, kept))
        pieces, early, arrived, tokens, sibling = gather_kept(kept, half, tokens)
        orig_weight, arrived = lax.optimization_barrier((orig_weight, arrived))
        weights = [orig_weight] + [swap(orig_weight, k) for k in others]
        a, scale, factors, follow = first_part(side, *early, pieces[2:], rows, features, begin)
        a, weights, sibling = lax.optimization_barrier((a, weights, sibling))
        stacked = jnp.concatenate(weights, axis=0)
        projected = [
            lax.dot_general(stacked, part, NT, preferred_element_type=jnp.float32) for part in (tokens, sibling)
        ]
        projected, a = lax.optimization_barrier((jnp.concatenate(projected, axis=1), a))
        parts = [projected[i * own:(i + 1) * own] for i in range(n // 2)]
        parts = [parts[0]] + [swap(part, k) for part, k in zip(parts[1:], others)]
        rest, more, follow = middle_part(a, factors, follow, begin, middle)
        begun = (scale, a, factors, rest, more, follow)
        return last_part(keep_flags, side, parts, begun, pieces, features, begin, middle)

    in_specs = (P("dp", None), P(("section", "dp"), None), P())
    out_specs = P(("section", "dp"), None)
    return jax.shard_map(on_device, mesh=mesh, in_specs=in_specs, out_specs=out_specs, check_vma=False)
```

```python
import functools

import jax
import jax.numpy as jnp
from jax import lax
from jax.experimental import pallas as pl
from jax.experimental.pallas import tpu as pltpu
from jax.sharding import PartitionSpec as P

KEEP_BLK = 12
PANEL = 128
SUB = 8
EXTRA = 16
VMEM_LIMIT = 32 * 1024 * 1024
NT = (((1,), (1,)), ((), ()))
NN = (((1,), (0,)), ((), ()))


def split3(x):
    hi = x.astype(jnp.bfloat16)
    rest = x - hi.astype(jnp.float32)
    mid = rest.astype(jnp.bfloat16)
    low = (rest - mid.astype(jnp.float32)).astype(jnp.bfloat16)
    return hi, mid, low


def dot32(a, b, dims):
    return lax.dot_general(a, b, dims, preferred_element_type=jnp.float32)


def kept_blocks(flags_ref, index_ref):
    count = jnp.int32(0)
    for b in range(flags_ref.shape[0]):
        index_ref[count] = b
        count = count + flags_ref[b]


def select_kernel(side_ref, flags_in_ref, tokens_ref, out_ref, half_ref, *scratch):
    flags_ref, index_ref, held_ref, sem, flags_sem = scratch
    rows, features = tokens_ref.shape
    blocks = flags_ref.shape[0]
    width = features // blocks
    per_tile = 128 // width
    chunks = sem.shape[0]
    step = rows // chunks
    fetch = pltpu.make_async_copy(flags_in_ref, flags_ref, flags_sem)
    fetch.start()
    reads = []
    for c in range(chunks):
        part = pl.ds(c * step, step)
        reads.append(pltpu.make_async_copy(tokens_ref.at[part, :], held_ref.at[part, :], sem.at[c]))
        reads[-1].start()
    fetch.wait()
    kept_blocks(flags_ref, index_ref)
    row = lax.broadcasted_iota(jnp.int32, (width, 128), 0)
    lane = lax.broadcasted_iota(jnp.int32, (width, 128), 1)
    total = jnp.zeros((step, 128), jnp.float32)
    for c in range(chunks):
        reads[c].wait()
        part = slice(c * step, (c + 1) * step)
        for i in range(KEEP_BLK):
            b = index_ref[i]
            start = pl.multiple_of((b // per_tile) * 128, 128)
            pick = jnp.where(lane == row + (b % per_tile) * width, 1.0, 0.0).astype(jnp.bfloat16)
            picked = dot32(pick, held_ref[part, pl.ds(start, 128)], NT)
            out_ref[i * width:(i + 1) * width, part] = picked.astype(jnp.bfloat16)
        for f in range(features // 128):
            piece = held_ref[part, f * 128:(f + 1) * 128].astype(jnp.float32)
            total += piece * piece
    squares = jnp.sum(total)
    hi, mid, low = split3(jnp.full((EXTRA, rows), squares, jnp.float32))
    row = lax.broadcasted_iota(jnp.int32, (EXTRA, rows), 0)
    carried = jnp.where(
        row == 0,
        hi.astype(jnp.float32),
        jnp.where(row == 1, mid.astype(jnp.float32), jnp.where(row == 2, low.astype(jnp.float32), 0.0)),
    )
    kept = KEEP_BLK * width
    out_ref[kept:, :] = carried.astype(jnp.bfloat16)
    half = kept // 2
    half_ref[:half, :] = out_ref[pl.ds(pl.multiple_of(side_ref[0] * half, half), half), :]
    half_ref[half:, :] = carried.astype(jnp.bfloat16)


def select_kept(side, tokens, keep_flags):
    rows, features = tokens.shape
    blocks = keep_flags.shape[0]
    kept = KEEP_BLK * (features // blocks)
    chunks = rows // 128
    return pl.pallas_call(
        select_kernel,
        out_shape=[
            jax.ShapeDtypeStruct((kept + EXTRA, rows), jnp.bfloat16),
            jax.ShapeDtypeStruct((kept // 2 + EXTRA, rows), jnp.bfloat16),
        ],
        in_specs=[pl.BlockSpec(memory_space=pltpu.SMEM)] + [pl.BlockSpec(memory_space=pltpu.HBM)] * 2,
        out_specs=[pl.BlockSpec(memory_space=pltpu.VMEM)] * 2,
        scratch_shapes=[
            pltpu.SMEM((blocks,), jnp.int32),
            pltpu.SMEM((blocks + 1,), jnp.int32),
            pltpu.VMEM((rows, features), jnp.bfloat16),
            pltpu.SemaphoreType.DMA((chunks,)),
            pltpu.SemaphoreType.DMA,
        ],
        compiler_params=pltpu.CompilerParams(vmem_limit_bytes=VMEM_LIMIT),
        name="select_kept",
    )(side, keep_flags, tokens)


def lane_column(x, c):
    return jnp.broadcast_to(x[:, c:c + 1], (SUB, 128))


def sublane_row(x, t):
    return jnp.broadcast_to(x[t:t + 1, :], (SUB, 128))


def tree_sum(terms):
    while len(terms) > 1:
        pairs = [terms[i] + terms[i + 1] for i in range(0, len(terms) - 1, 2)]
        terms = pairs + terms[len(terms) - len(terms) % 2:]
    return terms[0]


def block_entries(block, base):
    entry = {}
    for j in range(SUB):
        column = lane_column(block, base + j)
        for i in range(j + 1):
            entry[i, j] = sublane_row(column, i)
    return entry


def solve_small(entry, rows, cross, beyond, ahead):
    entry, rows, ahead = dict(entry), list(rows), list(ahead)
    cross, beyond = list(cross), list(beyond)
    lower = {}
    for t in range(0, SUB, 2):
        u = t + 1
        a, b, c = entry[t, t], entry[t, u], entry[u, u]
        first = pl.reciprocal(a, approx=True)
        second = a * pl.reciprocal(a * c - b * b, approx=True)
        lower[u, t] = b * first
        later = range(u + 1, SUB)
        rest = {}
        for j in later:
            lower[j, t] = entry[t, j] * first
            rest[j] = entry[u, j] - b * lower[j, t]
        for j in later:
            for i in range(u + 1, j + 1):
                partial = entry[i, j] - entry[t, i] * lower[j, t]
                entry[i, j] = partial - (rest[i] * rest[j]) * second
        for j in later:
            lower[j, u] = rest[j] * second
        for part in (cross, beyond, rows):
            if part:
                part[u] = part[u] - lower[u, t] * part[t]
                for j in later:
                    part[j] = (part[j] - lower[j, t] * part[t]) - lower[j, u] * part[u]
        if cross:
            left, right = cross[t] * first, cross[u] * second
            for j in range(SUB):
                ahead[j] = (ahead[j] - left * sublane_row(cross[t], j)) - right * sublane_row(cross[u], j)
        rows[t] = rows[t] * first
        rows[u] = rows[u] * second
    following = {(i, j): sublane_row(ahead[j], i) for j in range(SUB) for i in range(j + 1) if cross}
    forward = list(rows)
    for t in reversed(range(SUB)):
        for j in range(t):
            rows[j] = rows[j] - lower[t, j] * rows[t]
    return rows, forward, cross, beyond, following


def factor_panel(block, beside=()):
    size = block.shape[0]
    count = size // SUB
    sub = lax.broadcasted_iota(jnp.int32, (SUB, 128), 0)
    lane = lax.broadcasted_iota(jnp.int32, (SUB, 128), 1)
    rows = [block[i * SUB:(i + 1) * SUB, :] for i in range(count)]
    entry = block_entries(rows[0], 0)
    lower, scaled = [], []
    done = 0
    for s in range(count):
        base = s * SUB
        inside = (lane >= base) & (lane < base + SUB)
        cross, beyond, ahead = [], [], []
        if s + 2 < count:
            beyond = [lane_column(rows[s + 2], base + j) for j in range(SUB)]
        if s + 1 < count:
            cross = [lane_column(rows[s + 1], base + j) for j in range(SUB)]
            ahead = [lane_column(rows[s + 1], base + SUB + j) for j in range(SUB)]
        pivot_rows = jnp.where(inside, jnp.where(lane == sub + base, 1.0, 0.0), rows[s])
        spread_in = [sublane_row(pivot_rows, j) for j in range(SUB)]
        spread, forward, cross, beyond, entry = solve_small(entry, spread_in, cross, beyond, ahead)
        for i in range(s + 1, count):
            if i <= s + 2:
                columns, lines = (cross if i == s + 1 else beyond), forward
            else:
                columns, lines = [lane_column(rows[i], base + j) for j in range(SUB)], spread
            change = tree_sum([columns[j] * lines[j] for j in range(SUB)])
            rows[i] = jnp.where(inside, 0.0, rows[i]) - change
        new = spread[SUB - 1]
        for j in range(SUB - 1):
            new = jnp.where(sub == j, spread[j], new)
        lower.append(jnp.where(lane < base + SUB, pivot_rows, 0.0))
        scaled.append(jnp.where(lane < base + SUB, new, 0.0))
        until = len(beside) * (s + 1) // count
        for task in beside[done:until]:
            task()
        done = until
    return jnp.concatenate(lower, axis=0), jnp.concatenate(scaled, axis=0)


def wide_left(x):
    hi, mid, low = split3(x)
    return jnp.concatenate([hi, hi, mid, hi, mid, low], axis=1)


def wide_right(x):
    hi, mid, low = split3(x)
    return jnp.concatenate([hi, mid, hi, low, mid, hi], axis=0)


def wide_across(x):
    hi, mid, low = split3(x)
    return jnp.concatenate([hi, mid, hi, low, mid, hi], axis=1)


def spans(low, high):
    first = low + (high - low) % 256
    starts = ([low] if first > low else []) + list(range(first, high, 256))
    return list(zip(starts, starts[1:] + [high]))


def settle_tasks(p, state, lower_ref, scaled_ref):
    a_ref, offset, _, w_ref, left_ref, right_ref = state
    kept = w_ref.shape[1]
    at = p * PANEL
    low = at + PANEL
    here = slice(at - offset, low - offset)
    rest = slice(low - offset, kept - offset)

    def make_w(c, d):
        value = dot32(wide_left(scaled_ref[...]), wide_right(a_ref[here, c - offset:d - offset]), NN)
        right_ref[:, c:d] = wide_right(value)

    def make_left():
        value = dot32(wide_left(a_ref[rest, here]), wide_across(lower_ref[...]), NT)
        left_ref[low:, :] = wide_left(value)

    def update(c, d):
        a_ref[rest, c - offset:d - offset] -= dot32(left_ref[low:, :], right_ref[:, c:d], NN)

    def place(c, d):
        a_ref[here, c - offset:d - offset] = dot32(wide_left(lower_ref[...].T), right_ref[:, c:d], NN)

    ranges = spans(low, kept)
    tasks = [functools.partial(make_w, c, d) for c, d in ranges] + [make_left]
    tasks += [functools.partial(update, c, d) for c, d in ranges]
    return tasks + [functools.partial(place, c, d) for c, d in ranges]


def panel(p, state, factors_ref, beside):
    a_ref, offset, next_ref = state[:3]
    at = p * PANEL - offset
    here, after = slice(at, at + PANEL), slice(at + PANEL, at + 2 * PANEL)
    lower, scaled = factor_panel(next_ref[...], beside)
    left = dot32(wide_left(a_ref[after, here]), wide_across(lower), NT)
    right = dot32(wide_left(scaled), wide_right(a_ref[here, after]), NN)
    next_ref[...] = a_ref[after, after] - dot32(wide_left(left), wide_right(right), NN)
    factors_ref[0] = lower
    factors_ref[1] = scaled


def factors_shape(count):
    return jax.ShapeDtypeStruct((count, 2, PANEL, PANEL), jnp.float32)


def work_scratch(kept):
    return [
        pltpu.VMEM((8, kept), jnp.float32),
        pltpu.VMEM((kept, 6 * PANEL), jnp.bfloat16),
        pltpu.VMEM((6 * PANEL, kept), jnp.bfloat16),
    ]


def flat(pieces):
    return [part for piece in pieces for part in (piece if isinstance(piece, tuple) else (piece,))]


def place_pieces(pieces, refs, side, all_ref, sem):
    refs = list(refs)
    moves = []
    at = 0
    for piece in pieces:
        if isinstance(piece, tuple):
            width = piece[0].shape[1]
            cols = pl.ds(at, width)
            half = piece[0].shape[0] - EXTRA
            mine, other = refs.pop(0), refs.pop(0)
            low = pl.multiple_of(side * half, half)
            high = pl.multiple_of((1 - side) * half, half)
            moves.append((mine.at[:half, :], all_ref.at[pl.ds(low, half), cols]))
            moves.append((other.at[:half, :], all_ref.at[pl.ds(high, half), cols]))
            moves.append((mine.at[half:, :], all_ref.at[pl.ds(2 * half, EXTRA), cols]))
        else:
            width = piece.shape[1]
            moves.append((refs.pop(0), all_ref.at[:, pl.ds(at, width)]))
        at += width
    copies = [pltpu.make_async_copy(a, b, sem.at[k]) for k, (a, b) in enumerate(moves)]
    for copy in copies:
        copy.start()
    return copies


def halves(pieces):
    return [piece for piece in pieces if isinstance(piece, tuple)]


def piece_scratch(pieces, kept):
    tokens = sum((piece[0] if isinstance(piece, tuple) else piece).shape[1] for piece in pieces)
    return pltpu.VMEM((kept + EXTRA, max(tokens, 128)), jnp.bfloat16), pltpu.SemaphoreType.DMA((3 * len(pieces) + 1,))


def piece_specs(pieces):
    specs = []
    for piece in pieces:
        if isinstance(piece, tuple):
            specs += [pl.BlockSpec(memory_space=pl.ANY)] * len(piece)
        else:
            specs.append(pl.BlockSpec(memory_space=pltpu.VMEM))
    return specs


def join_pieces(pieces, refs, side, all_ref, sem):
    whole = sum(not isinstance(piece, tuple) for piece in pieces)
    copies = place_pieces(pieces[whole:], refs[whole:], side, all_ref, sem)
    return copies, list(refs[:whole]) + [all_ref] * (whole < len(pieces))


def gram_columns(parts, low, high, at, tile):
    acc = None
    for part in parts:
        value = dot32(part[low:high, :], part[at:at + tile, :], NT)
        acc = value if acc is None else acc + value
    return acc


def square_sum(parts, kept, rows):
    total = jnp.float32(0.0)
    for part in parts:
        for k in range(0, part.shape[1], rows):
            total = total + jnp.sum(part[kept:, k:k + 1].astype(jnp.float32))
    return total


def early_gram(pieces, source):
    kept_extra, rows = pieces[0].shape
    kept = kept_extra - EXTRA
    count = len(pieces)
    scratch = piece_scratch(pieces, kept)

    def body(*refs):
        source_ref, out_ref, squares_ref, held_ref, all_ref, sem, held_sem = refs[count:]
        copies = place_pieces(pieces, refs[:count], 0, all_ref, sem)
        fetch = pltpu.make_async_copy(source_ref, held_ref, held_sem)
        fetch.start()
        for copy in copies:
            copy.wait()
        squares_ref[...] = jnp.full(squares_ref.shape, square_sum([all_ref], kept, rows), jnp.float32)
        for at in range(0, kept, 256):
            out_ref[:, at:at + 256] = gram_columns([all_ref], 0, kept, at, 256)
        fetch.wait()

    return pl.pallas_call(
        body,
        out_shape=[
            jax.ShapeDtypeStruct((kept, kept), jnp.float32),
            jax.ShapeDtypeStruct((8, 128), jnp.float32),
            jax.ShapeDtypeStruct(source.shape, source.dtype),
        ],
        in_specs=[pl.BlockSpec(memory_space=pl.ANY)] * (count + 1),
        out_specs=[pl.BlockSpec(memory_space=pltpu.VMEM)] * 3,
        scratch_shapes=[*scratch, pltpu.SemaphoreType.DMA],
        compiler_params=pltpu.CompilerParams(vmem_limit_bytes=VMEM_LIMIT),
        name="early_gram",
    )(*pieces, source)


def first_kernel(features, rows, last, parts, early_ref, squares_ref, *refs):
    a_ref, scale_ref, factors_ref, next_ref, _, w_ref, left_ref, right_ref = refs[-8:]
    kept = a_ref.shape[0]
    total = squares_ref[...] + square_sum(parts, kept, rows)
    scale_ref[...] = 1.0 / (0.01 * total / features)
    scale = scale_ref[0:1, 0:1]

    def gram(at, tile):
        row = lax.broadcasted_iota(jnp.int32, (kept, tile), 0)
        lane = lax.broadcasted_iota(jnp.int32, (kept, tile), 1)
        value = early_ref[:, at:at + tile] + gram_columns(parts, 0, kept, at, tile)
        a_ref[:, at:at + tile] = value * scale + jnp.where(row == lane + at, 1.0, 0.0)

    block = slice(0, PANEL)
    corner = early_ref[block, block] + gram_columns(parts, 0, PANEL, 0, PANEL)
    row = lax.broadcasted_iota(jnp.int32, (PANEL, PANEL), 0)
    lane = lax.broadcasted_iota(jnp.int32, (PANEL, PANEL), 1)
    next_ref[...] = corner * scale + jnp.where(row == lane, 1.0, 0.0)
    state = (a_ref, 0, next_ref, w_ref, left_ref, right_ref)
    for p in range(last):
        if p:
            tasks = settle_tasks(p - 1, state, factors_ref.at[p - 1, 0], factors_ref.at[p - 1, 1])
        else:
            tasks = [functools.partial(gram, at, 256) for at in range(0, kept, 256)]
        panel(p, state, factors_ref.at[p], tasks)


def first_part(side, early, squares, pieces, rows, features, last):
    kept = early.shape[0]
    count = len(flat(pieces))
    all_scratch, sem_scratch = piece_scratch(halves(pieces), kept)
    vmem = pl.BlockSpec(memory_space=pltpu.VMEM)

    def body(*refs):
        side_ref, refs, sem = refs[0], refs[1:-1], refs[-1]
        copies, parts = join_pieces(pieces, refs[2:count + 2], side_ref[0], refs[count + 6], sem)
        for copy in copies:
            copy.wait()
        first_kernel(float(features), rows, last, parts, *refs)

    return pl.pallas_call(
        body,
        out_shape=[
            jax.ShapeDtypeStruct((kept, kept), jnp.float32),
            jax.ShapeDtypeStruct((8, 128), jnp.float32),
            factors_shape(last),
            jax.ShapeDtypeStruct((PANEL, PANEL), jnp.float32),
        ],
        in_specs=[pl.BlockSpec(memory_space=pltpu.SMEM)] + [vmem] * 2 + piece_specs(pieces),
        out_specs=[vmem] * 4,
        scratch_shapes=[
            all_scratch,
            *work_scratch(kept),
            sem_scratch,
        ],
        compiler_params=pltpu.CompilerParams(vmem_limit_bytes=VMEM_LIMIT),
        name="gram_and_first_panels",
    )(side, early, squares, *flat(pieces))


def dot_small(x, y, dims=NN):
    rows = x.shape[0]
    hi, mid, low = split3(x)
    yhi, ymid, ylow = split3(y)
    first = dot32(jnp.concatenate([hi, mid, low], axis=0), yhi, dims)
    second = dot32(jnp.concatenate([hi, mid], axis=0), ymid, dims)
    third = dot32(hi, ylow, dims)
    small = first[2 * rows:] + second[rows:] + third
    return small + (first[rows:2 * rows] + second[:rows]) + first[:rows]


def middle_kernel(first, last, start_ref, early_ref, start_next_ref, a_ref, factors_ref, next_ref, *work):
    kept = start_ref.shape[0]
    offset = kept - a_ref.shape[0]
    a_ref[...] = start_ref[offset:, offset:]
    next_ref[...] = start_next_ref[...]
    state = (a_ref, offset, next_ref, *work)
    for p in range(first, last):
        source = early_ref.at[p - 1] if p == first else factors_ref.at[p - 1 - first]
        panel(p, state, factors_ref.at[p - first], settle_tasks(p - 1, state, source.at[0], source.at[1]))


def middle_part(a, factors, follow, first, last):
    kept = a.shape[0]
    left = kept - (first - 1) * PANEL
    vmem = pl.BlockSpec(memory_space=pltpu.VMEM)
    return pl.pallas_call(
        functools.partial(middle_kernel, first, last),
        out_shape=[
            jax.ShapeDtypeStruct((left, left), jnp.float32),
            factors_shape(last - first),
            jax.ShapeDtypeStruct((PANEL, PANEL), jnp.float32),
        ],
        in_specs=[vmem] * 3,
        out_specs=[vmem] * 3,
        scratch_shapes=work_scratch(kept),
        compiler_params=pltpu.CompilerParams(vmem_limit_bytes=VMEM_LIMIT),
        name="middle_panels",
    )(a, factors, follow)


def last_kernel(chips, begin, middle, copies, parts, flags_ref, *refs):
    projected, refs = refs[:chips], refs[chips:]
    scale_ref, whole_ref, early_ref, start_ref, mid_ref, start_next_ref = refs[:6]
    out_ref, index_ref, wide_out_ref, _, late_ref, a_ref, next_ref = refs[-10:-3]
    work = refs[-3:]
    own, features = out_ref.shape
    blocks = flags_ref.shape[0]
    width = features // blocks
    per_tile = 128 // width
    kept = whole_ref.shape[0]
    last = kept // PANEL - 1
    at = last * PANEL
    kept_blocks(flags_ref, index_ref)
    wide_out_ref[...] = jnp.zeros((own, features), jnp.float32)
    offset = kept - a_ref.shape[0]
    cut = start_ref.shape[0] - a_ref.shape[0]
    a_ref[...] = start_ref[cut:, cut:]
    next_ref[...] = start_next_ref[...]
    state = (a_ref, offset, next_ref, *work)
    held = {}

    def factor(p):
        source, skip = a_ref, offset
        if p < begin - 1:
            source, skip = whole_ref, 0
        elif p < middle - 1:
            source, skip = start_ref, kept - start_ref.shape[0]
        low = p * PANEL - skip
        return source[low:low + PANEL, low + PANEL:]

    def factors(p):
        if p < begin:
            return early_ref.at[p]
        return mid_ref.at[p - begin] if p < middle else late_ref.at[p - middle]

    def settle(p):
        return settle_tasks(p, state, factors(p).at[0], factors(p).at[1])

    def make_right():
        whole = jnp.concatenate([part[...] for part in projected], axis=1)
        stacked = jnp.concatenate(split3(whole), axis=0)
        right, low = None, 0
        for part in parts:
            high = low + part.shape[1]
            value = dot32(stacked[:, low:high], part[:kept, :], NT)
            right, low = value if right is None else right + value, high
        held["right"] = right[:own] + right[own:2 * own] + right[2 * own:]

    def forward(p):
        right = held["right"]
        held["z", p] = right[:, :PANEL]
        held["right"] = right[:, PANEL:] - dot_small(right[:, :PANEL], factor(p))

    def scaled(p):
        held["zd", p] = dot_small(dot_small(held["z", p], factors(p)[0], NT), factors(p)[1])

    def backward(p):
        if p == last:
            row = lax.broadcasted_iota(jnp.int32, (own + PANEL, PANEL), 0)
            lane = lax.broadcasted_iota(jnp.int32, (own + PANEL, PANEL), 1)
            held["back"] = jnp.where(row == lane + own, 1.0, 0.0)
        else:
            base = jnp.concatenate([held["zd", p], jnp.zeros((PANEL, PANEL), jnp.float32)], axis=0)
            value = base - dot_small(held["back"], factor(p), NT)
            held["back"] = jnp.concatenate([value, held["back"]], axis=1)

    for copy in copies:
        copy.wait()
    for p in range(middle, last):
        tasks = settle(p - 1)
        if p == last - 1:
            tasks = [make_right] + [functools.partial(forward, q) for q in range(p - 1)] + tasks
            tasks += [functools.partial(forward, p - 1)] + [functools.partial(scaled, q) for q in range(p)]
        panel(p, state, late_ref.at[p - middle], tasks)
    tasks = settle(last - 1)
    tasks += [functools.partial(forward, last - 1), functools.partial(scaled, last - 1)]
    tasks += [functools.partial(backward, p) for p in reversed(range(last + 1))]
    lower, upper = factor_panel(next_ref[...], tasks)
    tail = dot_small(dot_small(held["right"], lower, NT), upper)
    scale = scale_ref[0:1, 0:1]
    front = held["back"][:own, :at] + dot_small(tail, held["back"][own:, :at])
    answer = [front[:, c:c + PANEL] * scale for c in range(0, at, PANEL)] + [tail * scale]
    place = lax.broadcasted_iota(jnp.int32, (own, 128), 1) // width
    for i in range(KEEP_BLK):
        b = index_ref[i]
        start = pl.multiple_of((b // per_tile) * 128, 128)
        inner = b % per_tile
        source = answer[i // per_tile]
        moved = pltpu.roll(source, width, 1)
        value = jnp.where(inner == i % per_tile, source, moved)
        old = wide_out_ref[:, pl.ds(start, 128)]
        wide_out_ref[:, pl.ds(start, 128)] = jnp.where(place == inner, value, old)
    out_ref[...] = wide_out_ref[...].astype(jnp.bfloat16)


def last_part(keep_flags, side, projected, begun, pieces, features, begin, middle):
    own = projected[0].shape[0]
    blocks = keep_flags.shape[0]
    chips = len(projected)
    kept = begun[1].shape[0]
    count = len(flat(pieces))
    all_scratch, sem_scratch = piece_scratch(halves(pieces), kept)
    left = kept - (middle - 1) * PANEL
    vmem = pl.BlockSpec(memory_space=pltpu.VMEM)

    def body(*refs):
        refs, sem = refs[:-1], refs[-1]
        side_ref, refs = refs[0], refs[1:]
        ins = 1 + chips + len(begun)
        copies, parts = join_pieces(pieces, refs[ins:ins + count], side_ref[0], refs[ins + count + 3], sem)
        last_kernel(chips, begin, middle, copies, parts, *refs)

    return pl.pallas_call(
        body,
        out_shape=jax.ShapeDtypeStruct((own, features), jnp.bfloat16),
        in_specs=[pl.BlockSpec(memory_space=pltpu.SMEM)] * 2
        + [vmem] * (chips + len(begun))
        + piece_specs(pieces),
        out_specs=vmem,
        scratch_shapes=[
            pltpu.SMEM((blocks + 1,), jnp.int32),
            pltpu.VMEM((own, features), jnp.float32),
            all_scratch,
            pltpu.VMEM((kept // PANEL - 1 - middle, 2, PANEL, PANEL), jnp.float32),
            pltpu.VMEM((left, left), jnp.float32),
            pltpu.VMEM((PANEL, PANEL), jnp.float32),
            *work_scratch(kept),
            sem_scratch,
        ],
        compiler_params=pltpu.CompilerParams(vmem_limit_bytes=VMEM_LIMIT),
        name="last_panels_and_solution",
    )(side, keep_flags, *projected, *begun, *flat(pieces))


def solution(mesh):
    n = mesh.shape["dp"]
    others = range(2, n, 2)

    def swap(x, k):
        return lax.ppermute(x, "dp", [(d, d ^ k) for d in range(n)])

    def level(x):
        return lax.ppermute(x, "section", [(d, d ^ 1) for d in range(mesh.shape["section"])])

    def gather_kept(kept, half, tokens):
        if n != 8 or mesh.shape["section"] % 2:
            same = [kept] + [swap(kept, k) for k in others]
            pieces = [part for piece in same for part in (piece, swap(piece, 1))]
            *early, held = early_gram(pieces[:2], tokens)
            return pieces, early, same[-1], held, swap(tokens, 1)
        far = swap(half, 6)
        near = [swap(kept, 2), swap(kept, 4)]
        sibling = swap(kept, 1)
        other = level(far)
        far_sibling = swap(far, 1)
        tokens_sibling = swap(tokens, 1)
        *early, held = early_gram([kept, sibling], tokens)
        near, early, far_sibling = lax.optimization_barrier((near, early, far_sibling))
        near_sibling = [swap(piece, 1) for piece in near]
        other_sibling = swap(other, 1)
        pieces = [kept, sibling, near[0], near_sibling[0], near[1], near_sibling[1]]
        pieces += [(far, other), (far_sibling, other_sibling)]
        return pieces, early, near, held, tokens_sibling

    def on_device(tokens, orig_weight, keep_flags):
        features = tokens.shape[1]
        own = orig_weight.shape[0]
        rows = tokens.shape[0]
        side = jnp.full((1,), lax.axis_index("section") % 2, jnp.int32)
        kept, half = select_kept(side, tokens, keep_flags)
        panels = (kept.shape[0] - EXTRA) // PANEL
        begin = panels // 2
        middle = begin + 1
        tokens, kept = lax.optimization_barrier((tokens, kept))
        pieces, early, arrived, tokens, sibling = gather_kept(kept, half, tokens)
        orig_weight, arrived = lax.optimization_barrier((orig_weight, arrived))
        weights = [orig_weight] + [swap(orig_weight, k) for k in others]
        a, scale, factors, follow = first_part(side, *early, pieces[2:], rows, features, begin)
        a, weights, sibling = lax.optimization_barrier((a, weights, sibling))
        stacked = jnp.concatenate(weights, axis=0)
        projected = [
            lax.dot_general(stacked, part, NT, preferred_element_type=jnp.float32) for part in (tokens, sibling)
        ]
        projected, a = lax.optimization_barrier((jnp.concatenate(projected, axis=1), a))
        parts = [projected[i * own:(i + 1) * own] for i in range(n // 2)]
        parts = [parts[0]] + [swap(part, k) for part, k in zip(parts[1:], others)]
        rest, more, follow = middle_part(a, factors, follow, begin, middle)
        begun = (scale, a, factors, rest, more, follow)
        return last_part(keep_flags, side, parts, begun, pieces, features, begin, middle)

    in_specs = (P("dp", None), P(("section", "dp"), None), P())
    out_specs = P(("section", "dp"), None)
    return jax.shard_map(on_device, mesh=mesh, in_specs=in_specs, out_specs=out_specs, check_vma=False)
```

```python
import functools

import jax
import jax.numpy as jnp
from jax import lax
from jax.experimental import pallas as pl
from jax.experimental.pallas import tpu as pltpu
from jax.sharding import PartitionSpec as P

KEEP_BLK = 12
PANEL = 128
SUB = 8
EXTRA = 16
VMEM_LIMIT = 32 * 1024 * 1024
NT = (((1,), (1,)), ((), ()))
NN = (((1,), (0,)), ((), ()))


def split3(x):
    hi = x.astype(jnp.bfloat16)
    rest = x - hi.astype(jnp.float32)
    mid = rest.astype(jnp.bfloat16)
    low = (rest - mid.astype(jnp.float32)).astype(jnp.bfloat16)
    return hi, mid, low


def dot32(a, b, dims):
    return lax.dot_general(a, b, dims, preferred_element_type=jnp.float32)


def kept_blocks(flags_ref, index_ref):
    count = jnp.int32(0)
    for b in range(flags_ref.shape[0]):
        index_ref[count] = b
        count = count + flags_ref[b]


def select_kernel(side_ref, flags_in_ref, tokens_ref, out_ref, half_ref, *scratch):
    flags_ref, index_ref, held_ref, sem, flags_sem = scratch
    rows, features = tokens_ref.shape
    blocks = flags_ref.shape[0]
    width = features // blocks
    per_tile = 128 // width
    chunks = sem.shape[0]
    step = rows // chunks
    fetch = pltpu.make_async_copy(flags_in_ref, flags_ref, flags_sem)
    fetch.start()
    reads = []
    for c in range(chunks):
        part = pl.ds(c * step, step)
        reads.append(pltpu.make_async_copy(tokens_ref.at[part, :], held_ref.at[part, :], sem.at[c]))
        reads[-1].start()
    fetch.wait()
    kept_blocks(flags_ref, index_ref)
    row = lax.broadcasted_iota(jnp.int32, (width, 128), 0)
    lane = lax.broadcasted_iota(jnp.int32, (width, 128), 1)
    total = jnp.zeros((step, 128), jnp.float32)
    for c in range(chunks):
        reads[c].wait()
        part = slice(c * step, (c + 1) * step)
        for i in range(KEEP_BLK):
            b = index_ref[i]
            start = pl.multiple_of((b // per_tile) * 128, 128)
            pick = jnp.where(lane == row + (b % per_tile) * width, 1.0, 0.0).astype(jnp.bfloat16)
            picked = dot32(pick, held_ref[part, pl.ds(start, 128)], NT)
            out_ref[i * width:(i + 1) * width, part] = picked.astype(jnp.bfloat16)
        for f in range(features // 128):
            piece = held_ref[part, f * 128:(f + 1) * 128].astype(jnp.float32)
            total += piece * piece
    squares = jnp.sum(total)
    hi, mid, low = split3(jnp.full((EXTRA, rows), squares, jnp.float32))
    row = lax.broadcasted_iota(jnp.int32, (EXTRA, rows), 0)
    carried = jnp.where(
        row == 0,
        hi.astype(jnp.float32),
        jnp.where(row == 1, mid.astype(jnp.float32), jnp.where(row == 2, low.astype(jnp.float32), 0.0)),
    )
    kept = KEEP_BLK * width
    out_ref[kept:, :] = carried.astype(jnp.bfloat16)
    half = kept // 2
    half_ref[:half, :] = out_ref[pl.ds(pl.multiple_of(side_ref[0] * half, half), half), :]
    half_ref[half:, :] = carried.astype(jnp.bfloat16)


def select_kept(side, tokens, keep_flags):
    rows, features = tokens.shape
    blocks = keep_flags.shape[0]
    kept = KEEP_BLK * (features // blocks)
    chunks = rows // 128
    return pl.pallas_call(
        select_kernel,
        out_shape=[
            jax.ShapeDtypeStruct((kept + EXTRA, rows), jnp.bfloat16),
            jax.ShapeDtypeStruct((kept // 2 + EXTRA, rows), jnp.bfloat16),
        ],
        in_specs=[pl.BlockSpec(memory_space=pltpu.SMEM)] + [pl.BlockSpec(memory_space=pltpu.HBM)] * 2,
        out_specs=[pl.BlockSpec(memory_space=pltpu.VMEM)] * 2,
        scratch_shapes=[
            pltpu.SMEM((blocks,), jnp.int32),
            pltpu.SMEM((blocks + 1,), jnp.int32),
            pltpu.VMEM((rows, features), jnp.bfloat16),
            pltpu.SemaphoreType.DMA((chunks,)),
            pltpu.SemaphoreType.DMA,
        ],
        compiler_params=pltpu.CompilerParams(vmem_limit_bytes=VMEM_LIMIT),
        name="select_kept",
    )(side, keep_flags, tokens)


def lane_column(x, c):
    return jnp.broadcast_to(x[:, c:c + 1], (SUB, 128))


def sublane_row(x, t):
    return jnp.broadcast_to(x[t:t + 1, :], (SUB, 128))


def tree_sum(terms):
    while len(terms) > 1:
        pairs = [terms[i] + terms[i + 1] for i in range(0, len(terms) - 1, 2)]
        terms = pairs + terms[len(terms) - len(terms) % 2:]
    return terms[0]


def block_entries(block, base):
    entry = {}
    for j in range(SUB):
        column = lane_column(block, base + j)
        for i in range(j + 1):
            entry[i, j] = sublane_row(column, i)
    return entry


def solve_small(entry, rows, cross, beyond, ahead):
    entry, rows, ahead = dict(entry), list(rows), list(ahead)
    cross, beyond = list(cross), list(beyond)
    lower = {}
    for t in range(0, SUB, 2):
        u = t + 1
        a, b, c = entry[t, t], entry[t, u], entry[u, u]
        first = pl.reciprocal(a, approx=True)
        second = a * pl.reciprocal(a * c - b * b, approx=True)
        lower[u, t] = b * first
        later = range(u + 1, SUB)
        rest = {}
        for j in later:
            lower[j, t] = entry[t, j] * first
            rest[j] = entry[u, j] - b * lower[j, t]
        for j in later:
            for i in range(u + 1, j + 1):
                partial = entry[i, j] - entry[t, i] * lower[j, t]
                entry[i, j] = partial - (rest[i] * rest[j]) * second
        for j in later:
            lower[j, u] = rest[j] * second
        for part in (cross, beyond, rows):
            if part:
                part[u] = part[u] - lower[u, t] * part[t]
                for j in later:
                    part[j] = (part[j] - lower[j, t] * part[t]) - lower[j, u] * part[u]
        if cross:
            left, right = cross[t] * first, cross[u] * second
            for j in range(SUB):
                ahead[j] = (ahead[j] - left * sublane_row(cross[t], j)) - right * sublane_row(cross[u], j)
        rows[t] = rows[t] * first
        rows[u] = rows[u] * second
    following = {(i, j): sublane_row(ahead[j], i) for j in range(SUB) for i in range(j + 1) if cross}
    forward = list(rows)
    for t in reversed(range(SUB)):
        for j in range(t):
            rows[j] = rows[j] - lower[t, j] * rows[t]
    return rows, forward, cross, beyond, following


def factor_panel(block, beside=()):
    size = block.shape[0]
    count = size // SUB
    sub = lax.broadcasted_iota(jnp.int32, (SUB, 128), 0)
    lane = lax.broadcasted_iota(jnp.int32, (SUB, 128), 1)
    rows = [block[i * SUB:(i + 1) * SUB, :] for i in range(count)]
    entry = block_entries(rows[0], 0)
    lower, scaled = [], []
    done = 0
    for s in range(count):
        base = s * SUB
        inside = (lane >= base) & (lane < base + SUB)
        cross, beyond, ahead = [], [], []
        if s + 2 < count:
            beyond = [lane_column(rows[s + 2], base + j) for j in range(SUB)]
        if s + 1 < count:
            cross = [lane_column(rows[s + 1], base + j) for j in range(SUB)]
            ahead = [lane_column(rows[s + 1], base + SUB + j) for j in range(SUB)]
        pivot_rows = jnp.where(inside, jnp.where(lane == sub + base, 1.0, 0.0), rows[s])
        spread_in = [sublane_row(pivot_rows, j) for j in range(SUB)]
        spread, forward, cross, beyond, entry = solve_small(entry, spread_in, cross, beyond, ahead)
        for i in range(s + 1, count):
            if i <= s + 2:
                columns, lines = (cross if i == s + 1 else beyond), forward
            else:
                columns, lines = [lane_column(rows[i], base + j) for j in range(SUB)], spread
            change = tree_sum([columns[j] * lines[j] for j in range(SUB)])
            rows[i] = jnp.where(inside, 0.0, rows[i]) - change
        new = spread[SUB - 1]
        for j in range(SUB - 1):
            new = jnp.where(sub == j, spread[j], new)
        lower.append(jnp.where(lane < base + SUB, pivot_rows, 0.0))
        scaled.append(jnp.where(lane < base + SUB, new, 0.0))
        until = len(beside) * (s + 1) // count
        for task in beside[done:until]:
            task()
        done = until
    return jnp.concatenate(lower, axis=0), jnp.concatenate(scaled, axis=0)


def wide_left(x):
    hi, mid, low = split3(x)
    return jnp.concatenate([hi, hi, mid, hi, mid, low], axis=1)


def wide_right(x):
    hi, mid, low = split3(x)
    return jnp.concatenate([hi, mid, hi, low, mid, hi], axis=0)


def wide_across(x):
    hi, mid, low = split3(x)
    return jnp.concatenate([hi, mid, hi, low, mid, hi], axis=1)


def spans(low, high):
    first = low + (high - low) % 256
    starts = ([low] if first > low else []) + list(range(first, high, 256))
    return list(zip(starts, starts[1:] + [high]))


def settle_tasks(p, state, lower_ref, scaled_ref):
    a_ref, offset, _, w_ref, left_ref, right_ref = state
    kept = w_ref.shape[1]
    at = p * PANEL
    low = at + PANEL
    here = slice(at - offset, low - offset)
    rest = slice(low - offset, kept - offset)

    def make_w(c, d):
        value = dot32(wide_left(scaled_ref[...]), wide_right(a_ref[here, c - offset:d - offset]), NN)
        right_ref[:, c:d] = wide_right(value)

    def make_left():
        value = dot32(wide_left(a_ref[rest, here]), wide_across(lower_ref[...]), NT)
        left_ref[low:, :] = wide_left(value)

    def update(c, d):
        a_ref[rest, c - offset:d - offset] -= dot32(left_ref[low:, :], right_ref[:, c:d], NN)

    def place(c, d):
        a_ref[here, c - offset:d - offset] = dot32(wide_left(lower_ref[...].T), right_ref[:, c:d], NN)

    ranges = spans(low, kept)
    tasks = [functools.partial(make_w, c, d) for c, d in ranges] + [make_left]
    tasks += [functools.partial(update, c, d) for c, d in ranges]
    return tasks + [functools.partial(place, c, d) for c, d in ranges]


def panel(p, state, factors_ref, beside):
    a_ref, offset, next_ref = state[:3]
    at = p * PANEL - offset
    here, after = slice(at, at + PANEL), slice(at + PANEL, at + 2 * PANEL)
    lower, scaled = factor_panel(next_ref[...], beside)
    left = dot32(wide_left(a_ref[after, here]), wide_across(lower), NT)
    right = dot32(wide_left(scaled), wide_right(a_ref[here, after]), NN)
    next_ref[...] = a_ref[after, after] - dot32(wide_left(left), wide_right(right), NN)
    factors_ref[0] = lower
    factors_ref[1] = scaled


def factors_shape(count):
    return jax.ShapeDtypeStruct((count, 2, PANEL, PANEL), jnp.float32)


def work_scratch(kept):
    return [
        pltpu.VMEM((8, kept), jnp.float32),
        pltpu.VMEM((kept, 6 * PANEL), jnp.bfloat16),
        pltpu.VMEM((6 * PANEL, kept), jnp.bfloat16),
    ]


def flat(pieces):
    return [part for piece in pieces for part in (piece if isinstance(piece, tuple) else (piece,))]


def place_pieces(pieces, refs, side, all_ref, sem):
    refs = list(refs)
    moves = []
    at = 0
    for piece in pieces:
        if isinstance(piece, tuple):
            width = piece[0].shape[1]
            cols = pl.ds(at, width)
            half = piece[0].shape[0] - EXTRA
            mine, other = refs.pop(0), refs.pop(0)
            low = pl.multiple_of(side * half, half)
            high = pl.multiple_of((1 - side) * half, half)
            moves.append((mine.at[:half, :], all_ref.at[pl.ds(low, half), cols]))
            moves.append((other.at[:half, :], all_ref.at[pl.ds(high, half), cols]))
            moves.append((mine.at[half:, :], all_ref.at[pl.ds(2 * half, EXTRA), cols]))
        else:
            width = piece.shape[1]
            moves.append((refs.pop(0), all_ref.at[:, pl.ds(at, width)]))
        at += width
    copies = [pltpu.make_async_copy(a, b, sem.at[k]) for k, (a, b) in enumerate(moves)]
    for copy in copies:
        copy.start()
    return copies


def halves(pieces):
    return [piece for piece in pieces if isinstance(piece, tuple)]


def piece_scratch(pieces, kept):
    tokens = sum((piece[0] if isinstance(piece, tuple) else piece).shape[1] for piece in pieces)
    return pltpu.VMEM((kept + EXTRA, max(tokens, 128)), jnp.bfloat16), pltpu.SemaphoreType.DMA((3 * len(pieces) + 1,))


def piece_specs(pieces):
    specs = []
    for piece in pieces:
        if isinstance(piece, tuple):
            specs += [pl.BlockSpec(memory_space=pl.ANY)] * len(piece)
        else:
            specs.append(pl.BlockSpec(memory_space=pltpu.VMEM))
    return specs


def join_pieces(pieces, refs, side, all_ref, sem):
    whole = sum(not isinstance(piece, tuple) for piece in pieces)
    copies = place_pieces(pieces[whole:], refs[whole:], side, all_ref, sem)
    return copies, list(refs[:whole]) + [all_ref] * (whole < len(pieces))


def gram_columns(parts, low, high, at, tile):
    acc = None
    for part in parts:
        value = dot32(part[low:high, :], part[at:at + tile, :], NT)
        acc = value if acc is None else acc + value
    return acc


def square_sum(parts, kept, rows):
    total = jnp.zeros((EXTRA, 128), jnp.float32)
    for part in parts:
        for k in range(0, part.shape[1], rows):
            total = total + part[kept:, k:k + 128].astype(jnp.float32)
    return jnp.broadcast_to(jnp.sum(total, axis=0, keepdims=True), (8, 128))


def early_gram(pieces, source):
    kept_extra, rows = pieces[0].shape
    kept = kept_extra - EXTRA
    count = len(pieces)
    scratch = piece_scratch(pieces, kept)

    def body(*refs):
        source_ref, out_ref, squares_ref, held_ref, all_ref, sem, held_sem = refs[count:]
        copies = place_pieces(pieces, refs[:count], 0, all_ref, sem)
        fetch = pltpu.make_async_copy(source_ref, held_ref, held_sem)
        fetch.start()
        for copy in copies:
            copy.wait()
        squares_ref[...] = square_sum([all_ref], kept, rows)
        for at in range(0, kept, 256):
            out_ref[:, at:at + 256] = gram_columns([all_ref], 0, kept, at, 256)
        fetch.wait()

    return pl.pallas_call(
        body,
        out_shape=[
            jax.ShapeDtypeStruct((kept, kept), jnp.float32),
            jax.ShapeDtypeStruct((8, 128), jnp.float32),
            jax.ShapeDtypeStruct(source.shape, source.dtype),
        ],
        in_specs=[pl.BlockSpec(memory_space=pl.ANY)] * (count + 1),
        out_specs=[pl.BlockSpec(memory_space=pltpu.VMEM)] * 3,
        scratch_shapes=[*scratch, pltpu.SemaphoreType.DMA],
        compiler_params=pltpu.CompilerParams(vmem_limit_bytes=VMEM_LIMIT),
        name="early_gram",
    )(*pieces, source)


def first_kernel(features, rows, last, parts, early_ref, squares_ref, *refs):
    a_ref, scale_ref, factors_ref, next_ref, _, w_ref, left_ref, right_ref = refs[-8:]
    kept = a_ref.shape[0]
    total = squares_ref[...] + square_sum(parts, kept, rows)
    scale_ref[...] = 1.0 / (0.01 * total / features)
    scale = scale_ref[0:1, 0:1]

    def gram(at, tile):
        row = lax.broadcasted_iota(jnp.int32, (kept, tile), 0)
        lane = lax.broadcasted_iota(jnp.int32, (kept, tile), 1)
        value = early_ref[:, at:at + tile] + gram_columns(parts, 0, kept, at, tile)
        a_ref[:, at:at + tile] = value * scale + jnp.where(row == lane + at, 1.0, 0.0)

    block = slice(0, PANEL)
    corner = early_ref[block, block] + gram_columns(parts, 0, PANEL, 0, PANEL)
    row = lax.broadcasted_iota(jnp.int32, (PANEL, PANEL), 0)
    lane = lax.broadcasted_iota(jnp.int32, (PANEL, PANEL), 1)
    next_ref[...] = corner * scale + jnp.where(row == lane, 1.0, 0.0)
    state = (a_ref, 0, next_ref, w_ref, left_ref, right_ref)
    for p in range(last):
        if p:
            tasks = settle_tasks(p - 1, state, factors_ref.at[p - 1, 0], factors_ref.at[p - 1, 1])
        else:
            tasks = [functools.partial(gram, at, 256) for at in range(0, kept, 256)]
        panel(p, state, factors_ref.at[p], tasks)


def first_part(side, early, squares, pieces, rows, features, last):
    kept = early.shape[0]
    count = len(flat(pieces))
    all_scratch, sem_scratch = piece_scratch(halves(pieces), kept)
    vmem = pl.BlockSpec(memory_space=pltpu.VMEM)

    def body(*refs):
        side_ref, refs, sem = refs[0], refs[1:-1], refs[-1]
        copies, parts = join_pieces(pieces, refs[2:count + 2], side_ref[0], refs[count + 6], sem)
        for copy in copies:
            copy.wait()
        first_kernel(float(features), rows, last, parts, *refs)

    return pl.pallas_call(
        body,
        out_shape=[
            jax.ShapeDtypeStruct((kept, kept), jnp.float32),
            jax.ShapeDtypeStruct((8, 128), jnp.float32),
            factors_shape(last),
            jax.ShapeDtypeStruct((PANEL, PANEL), jnp.float32),
        ],
        in_specs=[pl.BlockSpec(memory_space=pltpu.SMEM)] + [vmem] * 2 + piece_specs(pieces),
        out_specs=[vmem] * 4,
        scratch_shapes=[
            all_scratch,
            *work_scratch(kept),
            sem_scratch,
        ],
        compiler_params=pltpu.CompilerParams(vmem_limit_bytes=VMEM_LIMIT),
        name="gram_and_first_panels",
    )(side, early, squares, *flat(pieces))


def dot_small(x, y, dims=NN):
    rows = x.shape[0]
    hi, mid, low = split3(x)
    yhi, ymid, ylow = split3(y)
    first = dot32(jnp.concatenate([hi, mid, low], axis=0), yhi, dims)
    second = dot32(jnp.concatenate([hi, mid], axis=0), ymid, dims)
    third = dot32(hi, ylow, dims)
    small = first[2 * rows:] + second[rows:] + third
    return small + (first[rows:2 * rows] + second[:rows]) + first[:rows]


def middle_kernel(first, last, start_ref, early_ref, start_next_ref, a_ref, factors_ref, next_ref, *work):
    kept = start_ref.shape[0]
    offset = kept - a_ref.shape[0]
    a_ref[...] = start_ref[offset:, offset:]
    next_ref[...] = start_next_ref[...]
    state = (a_ref, offset, next_ref, *work)
    for p in range(first, last):
        source = early_ref.at[p - 1] if p == first else factors_ref.at[p - 1 - first]
        panel(p, state, factors_ref.at[p - first], settle_tasks(p - 1, state, source.at[0], source.at[1]))


def middle_part(a, factors, follow, first, last):
    kept = a.shape[0]
    left = kept - (first - 1) * PANEL
    vmem = pl.BlockSpec(memory_space=pltpu.VMEM)
    return pl.pallas_call(
        functools.partial(middle_kernel, first, last),
        out_shape=[
            jax.ShapeDtypeStruct((left, left), jnp.float32),
            factors_shape(last - first),
            jax.ShapeDtypeStruct((PANEL, PANEL), jnp.float32),
        ],
        in_specs=[vmem] * 3,
        out_specs=[vmem] * 3,
        scratch_shapes=work_scratch(kept),
        compiler_params=pltpu.CompilerParams(vmem_limit_bytes=VMEM_LIMIT),
        name="middle_panels",
    )(a, factors, follow)


def last_kernel(chips, begin, middle, copies, parts, flags_ref, *refs):
    projected, refs = refs[:chips], refs[chips:]
    scale_ref, whole_ref, early_ref, start_ref, mid_ref, start_next_ref = refs[:6]
    out_ref, index_ref, wide_out_ref, _, late_ref, a_ref, next_ref = refs[-10:-3]
    work = refs[-3:]
    own, features = out_ref.shape
    blocks = flags_ref.shape[0]
    width = features // blocks
    per_tile = 128 // width
    kept = whole_ref.shape[0]
    last = kept // PANEL - 1
    at = last * PANEL
    kept_blocks(flags_ref, index_ref)
    wide_out_ref[...] = jnp.zeros((own, features), jnp.float32)
    offset = kept - a_ref.shape[0]
    cut = start_ref.shape[0] - a_ref.shape[0]
    a_ref[...] = start_ref[cut:, cut:]
    next_ref[...] = start_next_ref[...]
    state = (a_ref, offset, next_ref, *work)
    held = {}

    def factor(p):
        source, skip = a_ref, offset
        if p < begin - 1:
            source, skip = whole_ref, 0
        elif p < middle - 1:
            source, skip = start_ref, kept - start_ref.shape[0]
        low = p * PANEL - skip
        return source[low:low + PANEL, low + PANEL:]

    def factors(p):
        if p < begin:
            return early_ref.at[p]
        return mid_ref.at[p - begin] if p < middle else late_ref.at[p - middle]

    def settle(p):
        return settle_tasks(p, state, factors(p).at[0], factors(p).at[1])

    def make_right():
        whole = jnp.concatenate([part[...] for part in projected], axis=1)
        stacked = jnp.concatenate(split3(whole), axis=0)
        right, low = None, 0
        for part in parts:
            high = low + part.shape[1]
            value = dot32(stacked[:, low:high], part[:kept, :], NT)
            right, low = value if right is None else right + value, high
        held["right"] = right[:own] + right[own:2 * own] + right[2 * own:]

    def forward(p):
        right = held["right"]
        held["z", p] = right[:, :PANEL]
        held["right"] = right[:, PANEL:] - dot_small(right[:, :PANEL], factor(p))

    def scaled(p):
        held["zd", p] = dot_small(dot_small(held["z", p], factors(p)[0], NT), factors(p)[1])

    def backward(p):
        if p == last:
            row = lax.broadcasted_iota(jnp.int32, (own + PANEL, PANEL), 0)
            lane = lax.broadcasted_iota(jnp.int32, (own + PANEL, PANEL), 1)
            held["back"] = jnp.where(row == lane + own, 1.0, 0.0)
        else:
            base = jnp.concatenate([held["zd", p], jnp.zeros((PANEL, PANEL), jnp.float32)], axis=0)
            value = base - dot_small(held["back"], factor(p), NT)
            held["back"] = jnp.concatenate([value, held["back"]], axis=1)

    for copy in copies:
        copy.wait()
    for p in range(middle, last):
        tasks = settle(p - 1)
        if p == last - 1:
            tasks = [make_right] + [functools.partial(forward, q) for q in range(p - 1)] + tasks
            tasks += [functools.partial(forward, p - 1)] + [functools.partial(scaled, q) for q in range(p)]
        panel(p, state, late_ref.at[p - middle], tasks)
    tasks = settle(last - 1)
    tasks += [functools.partial(forward, last - 1), functools.partial(scaled, last - 1)]
    tasks += [functools.partial(backward, p) for p in reversed(range(last + 1))]
    lower, upper = factor_panel(next_ref[...], tasks)
    lifted = dot_small(upper, held["back"][own:, :at])
    inner_part = dot_small(held["right"], lower, NT)
    tail = dot_small(inner_part, upper)
    scale = scale_ref[0:1, 0:1]
    front = held["back"][:own, :at] + dot_small(inner_part, lifted)
    answer = [front[:, c:c + PANEL] * scale for c in range(0, at, PANEL)] + [tail * scale]
    place = lax.broadcasted_iota(jnp.int32, (own, 128), 1) // width
    for i in range(KEEP_BLK):
        b = index_ref[i]
        start = pl.multiple_of((b // per_tile) * 128, 128)
        inner = b % per_tile
        source = answer[i // per_tile]
        moved = pltpu.roll(source, width, 1)
        value = jnp.where(inner == i % per_tile, source, moved)
        old = wide_out_ref[:, pl.ds(start, 128)]
        wide_out_ref[:, pl.ds(start, 128)] = jnp.where(place == inner, value, old)
    out_ref[...] = wide_out_ref[...].astype(jnp.bfloat16)


def last_part(keep_flags, side, projected, begun, pieces, features, begin, middle):
    own = projected[0].shape[0]
    blocks = keep_flags.shape[0]
    chips = len(projected)
    kept = begun[1].shape[0]
    count = len(flat(pieces))
    all_scratch, sem_scratch = piece_scratch(halves(pieces), kept)
    left = kept - (middle - 1) * PANEL
    vmem = pl.BlockSpec(memory_space=pltpu.VMEM)

    def body(*refs):
        refs, sem = refs[:-1], refs[-1]
        side_ref, refs = refs[0], refs[1:]
        ins = 1 + chips + len(begun)
        copies, parts = join_pieces(pieces, refs[ins:ins + count], side_ref[0], refs[ins + count + 3], sem)
        last_kernel(chips, begin, middle, copies, parts, *refs)

    return pl.pallas_call(
        body,
        out_shape=jax.ShapeDtypeStruct((own, features), jnp.bfloat16),
        in_specs=[pl.BlockSpec(memory_space=pltpu.SMEM)] * 2
        + [vmem] * (chips + len(begun))
        + piece_specs(pieces),
        out_specs=vmem,
        scratch_shapes=[
            pltpu.SMEM((blocks + 1,), jnp.int32),
            pltpu.VMEM((own, features), jnp.float32),
            all_scratch,
            pltpu.VMEM((kept // PANEL - 1 - middle, 2, PANEL, PANEL), jnp.float32),
            pltpu.VMEM((left, left), jnp.float32),
            pltpu.VMEM((PANEL, PANEL), jnp.float32),
            *work_scratch(kept),
            sem_scratch,
        ],
        compiler_params=pltpu.CompilerParams(vmem_limit_bytes=VMEM_LIMIT),
        name="last_panels_and_solution",
    )(side, keep_flags, *projected, *begun, *flat(pieces))


def solution(mesh):
    n = mesh.shape["dp"]
    others = range(2, n, 2)

    def swap(x, k):
        return lax.ppermute(x, "dp", [(d, d ^ k) for d in range(n)])

    def level(x):
        return lax.ppermute(x, "section", [(d, d ^ 1) for d in range(mesh.shape["section"])])

    def gather_kept(kept, half, tokens):
        if n != 8 or mesh.shape["section"] % 2:
            same = [kept] + [swap(kept, k) for k in others]
            pieces = [part for piece in same for part in (piece, swap(piece, 1))]
            *early, held = early_gram(pieces[:2], tokens)
            return pieces, early, same[-1], held, swap(tokens, 1)
        far = swap(half, 6)
        near = [swap(kept, 2), swap(kept, 4)]
        sibling = swap(kept, 1)
        other = level(far)
        far_sibling = swap(far, 1)
        tokens_sibling = swap(tokens, 1)
        *early, held = early_gram([kept, sibling], tokens)
        near, early, far_sibling = lax.optimization_barrier((near, early, far_sibling))
        near_sibling = [swap(piece, 1) for piece in near]
        other_sibling = swap(other, 1)
        pieces = [kept, sibling, near[0], near_sibling[0], near[1], near_sibling[1]]
        pieces += [(far, other), (far_sibling, other_sibling)]
        return pieces, early, near, held, tokens_sibling

    def on_device(tokens, orig_weight, keep_flags):
        features = tokens.shape[1]
        own = orig_weight.shape[0]
        rows = tokens.shape[0]
        side = jnp.full((1,), lax.axis_index("section") % 2, jnp.int32)
        kept, half = select_kept(side, tokens, keep_flags)
        panels = (kept.shape[0] - EXTRA) // PANEL
        begin = panels // 2
        middle = begin + 1
        tokens, kept = lax.optimization_barrier((tokens, kept))
        pieces, early, arrived, tokens, sibling = gather_kept(kept, half, tokens)
        orig_weight, arrived = lax.optimization_barrier((orig_weight, arrived))
        weights = [orig_weight] + [swap(orig_weight, k) for k in others]
        a, scale, factors, follow = first_part(side, *early, pieces[2:], rows, features, begin)
        a, weights, sibling = lax.optimization_barrier((a, weights, sibling))
        stacked = jnp.concatenate(weights, axis=0)
        projected = [
            lax.dot_general(stacked, part, NT, preferred_element_type=jnp.float32) for part in (tokens, sibling)
        ]
        projected, a = lax.optimization_barrier((jnp.concatenate(projected, axis=1), a))
        parts = [projected[i * own:(i + 1) * own] for i in range(n // 2)]
        parts = [parts[0]] + [swap(part, k) for part, k in zip(parts[1:], others)]
        rest, more, follow = middle_part(a, factors, follow, begin, middle)
        begun = (scale, a, factors, rest, more, follow)
        return last_part(keep_flags, side, parts, begun, pieces, features, begin, middle)

    in_specs = (P("dp", None), P(("section", "dp"), None), P())
    out_specs = P(("section", "dp"), None)
    return jax.shard_map(on_device, mesh=mesh, in_specs=in_specs, out_specs=out_specs, check_vma=False)
```

```python
import functools

import jax
import jax.numpy as jnp
from jax import lax
from jax.experimental import pallas as pl
from jax.experimental.pallas import tpu as pltpu
from jax.sharding import PartitionSpec as P

KEEP_BLK = 12
PANEL = 128
SUB = 8
EXTRA = 16
VMEM_LIMIT = 32 * 1024 * 1024
NT = (((1,), (1,)), ((), ()))
NN = (((1,), (0,)), ((), ()))


def split3(x):
    hi = x.astype(jnp.bfloat16)
    rest = x - hi.astype(jnp.float32)
    mid = rest.astype(jnp.bfloat16)
    low = (rest - mid.astype(jnp.float32)).astype(jnp.bfloat16)
    return hi, mid, low


def dot32(a, b, dims):
    return lax.dot_general(a, b, dims, preferred_element_type=jnp.float32)


def kept_blocks(flags_ref, index_ref):
    count = jnp.int32(0)
    for b in range(flags_ref.shape[0]):
        index_ref[count] = b
        count = count + flags_ref[b]


def select_kernel(side_ref, flags_in_ref, tokens_ref, out_ref, half_ref, *scratch):
    flags_ref, index_ref, held_ref, sem, flags_sem = scratch
    rows, features = tokens_ref.shape
    blocks = flags_ref.shape[0]
    width = features // blocks
    per_tile = 128 // width
    chunks = sem.shape[0]
    step = rows // chunks
    fetch = pltpu.make_async_copy(flags_in_ref, flags_ref, flags_sem)
    fetch.start()
    reads = []
    for c in range(chunks):
        part = pl.ds(c * step, step)
        reads.append(pltpu.make_async_copy(tokens_ref.at[part, :], held_ref.at[part, :], sem.at[c]))
        reads[-1].start()
    fetch.wait()
    kept_blocks(flags_ref, index_ref)
    row = lax.broadcasted_iota(jnp.int32, (width, 128), 0)
    lane = lax.broadcasted_iota(jnp.int32, (width, 128), 1)
    total = jnp.zeros((step, 128), jnp.float32)
    for c in range(chunks):
        reads[c].wait()
        part = slice(c * step, (c + 1) * step)
        for i in range(KEEP_BLK):
            b = index_ref[i]
            start = pl.multiple_of((b // per_tile) * 128, 128)
            pick = jnp.where(lane == row + (b % per_tile) * width, 1.0, 0.0).astype(jnp.bfloat16)
            picked = dot32(pick, held_ref[part, pl.ds(start, 128)], NT)
            out_ref[i * width:(i + 1) * width, part] = picked.astype(jnp.bfloat16)
        for f in range(features // 128):
            piece = held_ref[part, f * 128:(f + 1) * 128].astype(jnp.float32)
            total += piece * piece
    squares = jnp.sum(total)
    hi, mid, low = split3(jnp.full((EXTRA, rows), squares, jnp.float32))
    row = lax.broadcasted_iota(jnp.int32, (EXTRA, rows), 0)
    carried = jnp.where(
        row == 0,
        hi.astype(jnp.float32),
        jnp.where(row == 1, mid.astype(jnp.float32), jnp.where(row == 2, low.astype(jnp.float32), 0.0)),
    )
    kept = KEEP_BLK * width
    out_ref[kept:, :] = carried.astype(jnp.bfloat16)
    half = kept // 2
    half_ref[:half, :] = out_ref[pl.ds(pl.multiple_of(side_ref[0] * half, half), half), :]
    half_ref[half:, :] = carried.astype(jnp.bfloat16)


def select_kept(side, tokens, keep_flags):
    rows, features = tokens.shape
    blocks = keep_flags.shape[0]
    kept = KEEP_BLK * (features // blocks)
    chunks = rows // 128
    return pl.pallas_call(
        select_kernel,
        out_shape=[
            jax.ShapeDtypeStruct((kept + EXTRA, rows), jnp.bfloat16),
            jax.ShapeDtypeStruct((kept // 2 + EXTRA, rows), jnp.bfloat16),
        ],
        in_specs=[pl.BlockSpec(memory_space=pltpu.SMEM)] + [pl.BlockSpec(memory_space=pltpu.HBM)] * 2,
        out_specs=[pl.BlockSpec(memory_space=pltpu.VMEM)] * 2,
        scratch_shapes=[
            pltpu.SMEM((blocks,), jnp.int32),
            pltpu.SMEM((blocks + 1,), jnp.int32),
            pltpu.VMEM((rows, features), jnp.bfloat16),
            pltpu.SemaphoreType.DMA((chunks,)),
            pltpu.SemaphoreType.DMA,
        ],
        compiler_params=pltpu.CompilerParams(vmem_limit_bytes=VMEM_LIMIT),
        name="select_kept",
    )(side, keep_flags, tokens)


def lane_column(x, c):
    return jnp.broadcast_to(x[:, c:c + 1], (SUB, 128))


def sublane_row(x, t):
    return jnp.broadcast_to(x[t:t + 1, :], (SUB, 128))


def tree_sum(terms):
    while len(terms) > 1:
        pairs = [terms[i] + terms[i + 1] for i in range(0, len(terms) - 1, 2)]
        terms = pairs + terms[len(terms) - len(terms) % 2:]
    return terms[0]


def block_entries(block, base):
    entry = {}
    for j in range(SUB):
        column = lane_column(block, base + j)
        for i in range(j + 1):
            entry[i, j] = sublane_row(column, i)
    return entry


def solve_small(entry, rows, cross, beyond, ahead):
    entry, rows, ahead = dict(entry), list(rows), list(ahead)
    cross, beyond = list(cross), list(beyond)
    lower = {}
    for t in range(0, SUB, 2):
        u = t + 1
        a, b, c = entry[t, t], entry[t, u], entry[u, u]
        first = pl.reciprocal(a, approx=True)
        second = a * pl.reciprocal(a * c - b * b, approx=True)
        lower[u, t] = b * first
        later = range(u + 1, SUB)
        rest = {}
        for j in later:
            lower[j, t] = entry[t, j] * first
            rest[j] = entry[u, j] - b * lower[j, t]
        for j in later:
            for i in range(u + 1, j + 1):
                partial = entry[i, j] - entry[t, i] * lower[j, t]
                entry[i, j] = partial - (rest[i] * rest[j]) * second
        for j in later:
            lower[j, u] = rest[j] * second
        for part in (cross, beyond, rows):
            if part:
                part[u] = part[u] - lower[u, t] * part[t]
                for j in later:
                    part[j] = (part[j] - lower[j, t] * part[t]) - lower[j, u] * part[u]
        if cross:
            left, right = cross[t] * first, cross[u] * second
            for j in range(SUB):
                ahead[j] = (ahead[j] - left * sublane_row(cross[t], j)) - right * sublane_row(cross[u], j)
        rows[t] = rows[t] * first
        rows[u] = rows[u] * second
    following = {(i, j): sublane_row(ahead[j], i) for j in range(SUB) for i in range(j + 1) if cross}
    forward = list(rows)
    for t in reversed(range(SUB)):
        for j in range(t):
            rows[j] = rows[j] - lower[t, j] * rows[t]
    return rows, forward, cross, beyond, following


def factor_panel(block, beside=()):
    size = block.shape[0]
    count = size // SUB
    sub = lax.broadcasted_iota(jnp.int32, (SUB, 128), 0)
    lane = lax.broadcasted_iota(jnp.int32, (SUB, 128), 1)
    rows = [block[i * SUB:(i + 1) * SUB, :] for i in range(count)]
    entry = block_entries(rows[0], 0)
    lower, scaled = [], []
    done = 0
    for s in range(count):
        base = s * SUB
        inside = (lane >= base) & (lane < base + SUB)
        cross, beyond, ahead = [], [], []
        if s + 2 < count:
            beyond = [lane_column(rows[s + 2], base + j) for j in range(SUB)]
        if s + 1 < count:
            cross = [lane_column(rows[s + 1], base + j) for j in range(SUB)]
            ahead = [lane_column(rows[s + 1], base + SUB + j) for j in range(SUB)]
        pivot_rows = jnp.where(inside, jnp.where(lane == sub + base, 1.0, 0.0), rows[s])
        spread_in = [sublane_row(pivot_rows, j) for j in range(SUB)]
        spread, forward, cross, beyond, entry = solve_small(entry, spread_in, cross, beyond, ahead)
        for i in range(s + 1, count):
            value = jnp.where(inside, 0.0, rows[i])
            if i <= s + 2:
                columns = cross if i == s + 1 else beyond
                value = value - tree_sum([columns[j] * forward[j] for j in range(SUB)])
            else:
                for j in range(SUB):
                    value = value - lane_column(rows[i], base + j) * spread[j]
            rows[i] = value
        new = spread[SUB - 1]
        for j in range(SUB - 1):
            new = jnp.where(sub == j, spread[j], new)
        lower.append(jnp.where(lane < base + SUB, pivot_rows, 0.0))
        scaled.append(jnp.where(lane < base + SUB, new, 0.0))
        until = len(beside) * (s + 1) // count
        for task in beside[done:until]:
            task()
        done = until
    return jnp.concatenate(lower, axis=0), jnp.concatenate(scaled, axis=0)


def wide_left(x):
    hi, mid, low = split3(x)
    return jnp.concatenate([hi, hi, mid, hi, mid, low], axis=1)


def wide_right(x):
    hi, mid, low = split3(x)
    return jnp.concatenate([hi, mid, hi, low, mid, hi], axis=0)


def wide_across(x):
    hi, mid, low = split3(x)
    return jnp.concatenate([hi, mid, hi, low, mid, hi], axis=1)


def spans(low, high):
    first = low + (high - low) % 256
    starts = ([low] if first > low else []) + list(range(first, high, 256))
    return list(zip(starts, starts[1:] + [high]))


def settle_tasks(p, state, lower_ref, scaled_ref):
    a_ref, offset, _, w_ref, left_ref, right_ref = state
    kept = w_ref.shape[1]
    at = p * PANEL
    low = at + PANEL
    here = slice(at - offset, low - offset)
    rest = slice(low - offset, kept - offset)

    def make_w(c, d):
        value = dot32(wide_left(scaled_ref[...]), wide_right(a_ref[here, c - offset:d - offset]), NN)
        right_ref[:, c:d] = wide_right(value)

    def make_left():
        value = dot32(wide_left(a_ref[rest, here]), wide_across(lower_ref[...]), NT)
        left_ref[low:, :] = wide_left(value)

    def update(c, d):
        a_ref[rest, c - offset:d - offset] -= dot32(left_ref[low:, :], right_ref[:, c:d], NN)

    def place(c, d):
        a_ref[here, c - offset:d - offset] = dot32(wide_left(lower_ref[...].T), right_ref[:, c:d], NN)

    ranges = spans(low, kept)
    tasks = [functools.partial(make_w, c, d) for c, d in ranges] + [make_left]
    tasks += [functools.partial(update, c, d) for c, d in ranges]
    return tasks + [functools.partial(place, c, d) for c, d in ranges]


def panel(p, state, factors_ref, beside):
    a_ref, offset, next_ref = state[:3]
    at = p * PANEL - offset
    here, after = slice(at, at + PANEL), slice(at + PANEL, at + 2 * PANEL)
    lower, scaled = factor_panel(next_ref[...], beside)
    left = dot32(wide_left(a_ref[after, here]), wide_across(lower), NT)
    right = dot32(wide_left(scaled), wide_right(a_ref[here, after]), NN)
    next_ref[...] = a_ref[after, after] - dot32(wide_left(left), wide_right(right), NN)
    factors_ref[0] = lower
    factors_ref[1] = scaled


def factors_shape(count):
    return jax.ShapeDtypeStruct((count, 2, PANEL, PANEL), jnp.float32)


def work_scratch(kept):
    return [
        pltpu.VMEM((8, kept), jnp.float32),
        pltpu.VMEM((kept, 6 * PANEL), jnp.bfloat16),
        pltpu.VMEM((6 * PANEL, kept), jnp.bfloat16),
    ]


def flat(pieces):
    return [part for piece in pieces for part in (piece if isinstance(piece, tuple) else (piece,))]


def place_pieces(pieces, refs, side, all_ref, sem):
    refs = list(refs)
    moves = []
    at = 0
    for piece in pieces:
        if isinstance(piece, tuple):
            width = piece[0].shape[1]
            cols = pl.ds(at, width)
            half = piece[0].shape[0] - EXTRA
            mine, other = refs.pop(0), refs.pop(0)
            low = pl.multiple_of(side * half, half)
            high = pl.multiple_of((1 - side) * half, half)
            moves.append((mine.at[:half, :], all_ref.at[pl.ds(low, half), cols]))
            moves.append((other.at[:half, :], all_ref.at[pl.ds(high, half), cols]))
            moves.append((mine.at[half:, :], all_ref.at[pl.ds(2 * half, EXTRA), cols]))
        else:
            width = piece.shape[1]
            moves.append((refs.pop(0), all_ref.at[:, pl.ds(at, width)]))
        at += width
    copies = [pltpu.make_async_copy(a, b, sem.at[k]) for k, (a, b) in enumerate(moves)]
    for copy in copies:
        copy.start()
    return copies


def halves(pieces):
    return [piece for piece in pieces if isinstance(piece, tuple)]


def piece_scratch(pieces, kept):
    tokens = sum((piece[0] if isinstance(piece, tuple) else piece).shape[1] for piece in pieces)
    return pltpu.VMEM((kept + EXTRA, max(tokens, 128)), jnp.bfloat16), pltpu.SemaphoreType.DMA((3 * len(pieces) + 1,))


def piece_specs(pieces):
    specs = []
    for piece in pieces:
        if isinstance(piece, tuple):
            specs += [pl.BlockSpec(memory_space=pl.ANY)] * len(piece)
        else:
            specs.append(pl.BlockSpec(memory_space=pltpu.VMEM))
    return specs


def join_pieces(pieces, refs, side, all_ref, sem):
    whole = sum(not isinstance(piece, tuple) for piece in pieces)
    copies = place_pieces(pieces[whole:], refs[whole:], side, all_ref, sem)
    return copies, list(refs[:whole]) + [all_ref] * (whole < len(pieces))


def gram_columns(parts, low, high, at, tile):
    acc = None
    for part in parts:
        value = dot32(part[low:high, :], part[at:at + tile, :], NT)
        acc = value if acc is None else acc + value
    return acc


def square_sum(parts, kept, rows):
    total = jnp.float32(0.0)
    for part in parts:
        for k in range(0, part.shape[1], rows):
            total = total + jnp.sum(part[kept:, k:k + 1].astype(jnp.float32))
    return total


def early_gram(pieces, source):
    kept_extra, rows = pieces[0].shape
    kept = kept_extra - EXTRA
    count = len(pieces)
    scratch = piece_scratch(pieces, kept)

    def body(*refs):
        source_ref, out_ref, squares_ref, held_ref, all_ref, sem, held_sem = refs[count:]
        copies = place_pieces(pieces, refs[:count], 0, all_ref, sem)
        fetch = pltpu.make_async_copy(source_ref, held_ref, held_sem)
        fetch.start()
        for copy in copies:
            copy.wait()
        squares_ref[...] = jnp.full(squares_ref.shape, square_sum([all_ref], kept, rows), jnp.float32)
        for at in range(0, kept, 256):
            out_ref[:, at:at + 256] = gram_columns([all_ref], 0, kept, at, 256)
        fetch.wait()

    return pl.pallas_call(
        body,
        out_shape=[
            jax.ShapeDtypeStruct((kept, kept), jnp.float32),
            jax.ShapeDtypeStruct((8, 128), jnp.float32),
            jax.ShapeDtypeStruct(source.shape, source.dtype),
        ],
        in_specs=[pl.BlockSpec(memory_space=pl.ANY)] * (count + 1),
        out_specs=[pl.BlockSpec(memory_space=pltpu.VMEM)] * 3,
        scratch_shapes=[*scratch, pltpu.SemaphoreType.DMA],
        compiler_params=pltpu.CompilerParams(vmem_limit_bytes=VMEM_LIMIT),
        name="early_gram",
    )(*pieces, source)


def first_kernel(features, rows, last, parts, early_ref, squares_ref, *refs):
    a_ref, scale_ref, factors_ref, next_ref, _, w_ref, left_ref, right_ref = refs[-8:]
    kept = a_ref.shape[0]
    total = squares_ref[...] + square_sum(parts, kept, rows)
    scale_ref[...] = 1.0 / (0.01 * total / features)
    scale = scale_ref[0:1, 0:1]

    def gram(at, tile):
        row = lax.broadcasted_iota(jnp.int32, (kept, tile), 0)
        lane = lax.broadcasted_iota(jnp.int32, (kept, tile), 1)
        value = early_ref[:, at:at + tile] + gram_columns(parts, 0, kept, at, tile)
        a_ref[:, at:at + tile] = value * scale + jnp.where(row == lane + at, 1.0, 0.0)

    block = slice(0, PANEL)
    corner = early_ref[block, block] + gram_columns(parts, 0, PANEL, 0, PANEL)
    row = lax.broadcasted_iota(jnp.int32, (PANEL, PANEL), 0)
    lane = lax.broadcasted_iota(jnp.int32, (PANEL, PANEL), 1)
    next_ref[...] = corner * scale + jnp.where(row == lane, 1.0, 0.0)
    state = (a_ref, 0, next_ref, w_ref, left_ref, right_ref)
    for p in range(last):
        if p:
            tasks = settle_tasks(p - 1, state, factors_ref.at[p - 1, 0], factors_ref.at[p - 1, 1])
        else:
            tasks = [functools.partial(gram, at, 256) for at in range(0, kept, 256)]
        panel(p, state, factors_ref.at[p], tasks)


def first_part(side, early, squares, pieces, rows, features, last):
    kept = early.shape[0]
    count = len(flat(pieces))
    all_scratch, sem_scratch = piece_scratch(halves(pieces), kept)
    vmem = pl.BlockSpec(memory_space=pltpu.VMEM)

    def body(*refs):
        side_ref, refs, sem = refs[0], refs[1:-1], refs[-1]
        copies, parts = join_pieces(pieces, refs[2:count + 2], side_ref[0], refs[count + 6], sem)
        for copy in copies:
            copy.wait()
        first_kernel(float(features), rows, last, parts, *refs)

    return pl.pallas_call(
        body,
        out_shape=[
            jax.ShapeDtypeStruct((kept, kept), jnp.float32),
            jax.ShapeDtypeStruct((8, 128), jnp.float32),
            factors_shape(last),
            jax.ShapeDtypeStruct((PANEL, PANEL), jnp.float32),
        ],
        in_specs=[pl.BlockSpec(memory_space=pltpu.SMEM)] + [vmem] * 2 + piece_specs(pieces),
        out_specs=[vmem] * 4,
        scratch_shapes=[
            all_scratch,
            *work_scratch(kept),
            sem_scratch,
        ],
        compiler_params=pltpu.CompilerParams(vmem_limit_bytes=VMEM_LIMIT),
        name="gram_and_first_panels",
    )(side, early, squares, *flat(pieces))


def dot_small(x, y, dims=NN):
    rows = x.shape[0]
    hi, mid, low = split3(x)
    yhi, ymid, ylow = split3(y)
    first = dot32(jnp.concatenate([hi, mid, low], axis=0), yhi, dims)
    second = dot32(jnp.concatenate([hi, mid], axis=0), ymid, dims)
    third = dot32(hi, ylow, dims)
    small = first[2 * rows:] + second[rows:] + third
    return small + (first[rows:2 * rows] + second[:rows]) + first[:rows]


def middle_kernel(first, last, start_ref, early_ref, start_next_ref, a_ref, factors_ref, next_ref, *work):
    kept = start_ref.shape[0]
    offset = kept - a_ref.shape[0]
    a_ref[...] = start_ref[offset:, offset:]
    next_ref[...] = start_next_ref[...]
    state = (a_ref, offset, next_ref, *work)
    for p in range(first, last):
        source = early_ref.at[p - 1] if p == first else factors_ref.at[p - 1 - first]
        panel(p, state, factors_ref.at[p - first], settle_tasks(p - 1, state, source.at[0], source.at[1]))


def middle_part(a, factors, follow, first, last):
    kept = a.shape[0]
    left = kept - (first - 1) * PANEL
    vmem = pl.BlockSpec(memory_space=pltpu.VMEM)
    return pl.pallas_call(
        functools.partial(middle_kernel, first, last),
        out_shape=[
            jax.ShapeDtypeStruct((left, left), jnp.float32),
            factors_shape(last - first),
            jax.ShapeDtypeStruct((PANEL, PANEL), jnp.float32),
        ],
        in_specs=[vmem] * 3,
        out_specs=[vmem] * 3,
        scratch_shapes=work_scratch(kept),
        compiler_params=pltpu.CompilerParams(vmem_limit_bytes=VMEM_LIMIT),
        name="middle_panels",
    )(a, factors, follow)


def last_kernel(chips, begin, middle, copies, parts, flags_ref, *refs):
    projected, refs = refs[:chips], refs[chips:]
    scale_ref, whole_ref, early_ref, start_ref, mid_ref, start_next_ref = refs[:6]
    out_ref, index_ref, wide_out_ref, _, late_ref, a_ref, next_ref = refs[-10:-3]
    work = refs[-3:]
    own, features = out_ref.shape
    blocks = flags_ref.shape[0]
    width = features // blocks
    per_tile = 128 // width
    kept = whole_ref.shape[0]
    last = kept // PANEL - 1
    at = last * PANEL
    kept_blocks(flags_ref, index_ref)
    wide_out_ref[...] = jnp.zeros((own, features), jnp.float32)
    offset = kept - a_ref.shape[0]
    cut = start_ref.shape[0] - a_ref.shape[0]
    a_ref[...] = start_ref[cut:, cut:]
    next_ref[...] = start_next_ref[...]
    state = (a_ref, offset, next_ref, *work)
    held = {}

    def factor(p):
        source, skip = a_ref, offset
        if p < begin - 1:
            source, skip = whole_ref, 0
        elif p < middle - 1:
            source, skip = start_ref, kept - start_ref.shape[0]
        low = p * PANEL - skip
        return source[low:low + PANEL, low + PANEL:]

    def factors(p):
        if p < begin:
            return early_ref.at[p]
        return mid_ref.at[p - begin] if p < middle else late_ref.at[p - middle]

    def settle(p):
        return settle_tasks(p, state, factors(p).at[0], factors(p).at[1])

    def make_right():
        whole = jnp.concatenate([part[...] for part in projected], axis=1)
        stacked = jnp.concatenate(split3(whole), axis=0)
        right, low = None, 0
        for part in parts:
            high = low + part.shape[1]
            value = dot32(stacked[:, low:high], part[:kept, :], NT)
            right, low = value if right is None else right + value, high
        held["right"] = right[:own] + right[own:2 * own] + right[2 * own:]

    def forward(p):
        right = held["right"]
        held["z", p] = right[:, :PANEL]
        held["right"] = right[:, PANEL:] - dot_small(right[:, :PANEL], factor(p))

    def scaled(p):
        held["zd", p] = dot_small(dot_small(held["z", p], factors(p)[0], NT), factors(p)[1])

    def backward(p):
        if p == last:
            row = lax.broadcasted_iota(jnp.int32, (own + PANEL, PANEL), 0)
            lane = lax.broadcasted_iota(jnp.int32, (own + PANEL, PANEL), 1)
            held["back"] = jnp.where(row == lane + own, 1.0, 0.0)
        else:
            base = jnp.concatenate([held["zd", p], jnp.zeros((PANEL, PANEL), jnp.float32)], axis=0)
            value = base - dot_small(held["back"], factor(p), NT)
            held["back"] = jnp.concatenate([value, held["back"]], axis=1)

    for copy in copies:
        copy.wait()
    for p in range(middle, last):
        tasks = settle(p - 1)
        if p == last - 1:
            tasks = [make_right] + [functools.partial(forward, q) for q in range(p - 1)] + tasks
            tasks += [functools.partial(forward, p - 1)] + [functools.partial(scaled, q) for q in range(p)]
        panel(p, state, late_ref.at[p - middle], tasks)
    tasks = settle(last - 1)
    tasks += [functools.partial(forward, last - 1), functools.partial(scaled, last - 1)]
    tasks += [functools.partial(backward, p) for p in reversed(range(last + 1))]
    lower, upper = factor_panel(next_ref[...], tasks)
    tail = dot_small(dot_small(held["right"], lower, NT), upper)
    scale = scale_ref[0:1, 0:1]
    front = held["back"][:own, :at] + dot_small(tail, held["back"][own:, :at])
    answer = [front[:, c:c + PANEL] * scale for c in range(0, at, PANEL)] + [tail * scale]
    place = lax.broadcasted_iota(jnp.int32, (own, 128), 1) // width
    for i in range(KEEP_BLK):
        b = index_ref[i]
        start = pl.multiple_of((b // per_tile) * 128, 128)
        inner = b % per_tile
        source = answer[i // per_tile]
        moved = pltpu.roll(source, width, 1)
        value = jnp.where(inner == i % per_tile, source, moved)
        old = wide_out_ref[:, pl.ds(start, 128)]
        wide_out_ref[:, pl.ds(start, 128)] = jnp.where(place == inner, value, old)
    out_ref[...] = wide_out_ref[...].astype(jnp.bfloat16)


def last_part(keep_flags, side, projected, begun, pieces, features, begin, middle):
    own = projected[0].shape[0]
    blocks = keep_flags.shape[0]
    chips = len(projected)
    kept = begun[1].shape[0]
    count = len(flat(pieces))
    all_scratch, sem_scratch = piece_scratch(halves(pieces), kept)
    left = kept - (middle - 1) * PANEL
    vmem = pl.BlockSpec(memory_space=pltpu.VMEM)

    def body(*refs):
        refs, sem = refs[:-1], refs[-1]
        side_ref, refs = refs[0], refs[1:]
        ins = 1 + chips + len(begun)
        copies, parts = join_pieces(pieces, refs[ins:ins + count], side_ref[0], refs[ins + count + 3], sem)
        last_kernel(chips, begin, middle, copies, parts, *refs)

    return pl.pallas_call(
        body,
        out_shape=jax.ShapeDtypeStruct((own, features), jnp.bfloat16),
        in_specs=[pl.BlockSpec(memory_space=pltpu.SMEM)] * 2
        + [vmem] * (chips + len(begun))
        + piece_specs(pieces),
        out_specs=vmem,
        scratch_shapes=[
            pltpu.SMEM((blocks + 1,), jnp.int32),
            pltpu.VMEM((own, features), jnp.float32),
            all_scratch,
            pltpu.VMEM((kept // PANEL - 1 - middle, 2, PANEL, PANEL), jnp.float32),
            pltpu.VMEM((left, left), jnp.float32),
            pltpu.VMEM((PANEL, PANEL), jnp.float32),
            *work_scratch(kept),
            sem_scratch,
        ],
        compiler_params=pltpu.CompilerParams(vmem_limit_bytes=VMEM_LIMIT),
        name="last_panels_and_solution",
    )(side, keep_flags, *projected, *begun, *flat(pieces))


def solution(mesh):
    n = mesh.shape["dp"]
    others = range(2, n, 2)

    def swap(x, k):
        return lax.ppermute(x, "dp", [(d, d ^ k) for d in range(n)])

    def level(x):
        return lax.ppermute(x, "section", [(d, d ^ 1) for d in range(mesh.shape["section"])])

    def gather_kept(kept, half, tokens):
        if n != 8 or mesh.shape["section"] % 2:
            same = [kept] + [swap(kept, k) for k in others]
            pieces = [part for piece in same for part in (piece, swap(piece, 1))]
            *early, held = early_gram(pieces[:2], tokens)
            return pieces, early, same[-1], held, swap(tokens, 1)
        far = swap(half, 6)
        near = [swap(kept, 2), swap(kept, 4)]
        sibling = swap(kept, 1)
        other = level(far)
        far_sibling = swap(far, 1)
        tokens_sibling = swap(tokens, 1)
        *early, held = early_gram([kept, sibling], tokens)
        near, early, far_sibling = lax.optimization_barrier((near, early, far_sibling))
        near_sibling = [swap(piece, 1) for piece in near]
        other_sibling = swap(other, 1)
        pieces = [kept, sibling, near[0], near_sibling[0], near[1], near_sibling[1]]
        pieces += [(far, other), (far_sibling, other_sibling)]
        return pieces, early, near, held, tokens_sibling

    def on_device(tokens, orig_weight, keep_flags):
        features = tokens.shape[1]
        own = orig_weight.shape[0]
        rows = tokens.shape[0]
        side = jnp.full((1,), lax.axis_index("section") % 2, jnp.int32)
        kept, half = select_kept(side, tokens, keep_flags)
        panels = (kept.shape[0] - EXTRA) // PANEL
        begin = panels // 2
        middle = begin + 1
        tokens, kept = lax.optimization_barrier((tokens, kept))
        pieces, early, arrived, tokens, sibling = gather_kept(kept, half, tokens)
        orig_weight, arrived = lax.optimization_barrier((orig_weight, arrived))
        weights = [orig_weight] + [swap(orig_weight, k) for k in others]
        a, scale, factors, follow = first_part(side, *early, pieces[2:], rows, features, begin)
        a, weights, sibling = lax.optimization_barrier((a, weights, sibling))
        stacked = jnp.concatenate(weights, axis=0)
        projected = [
            lax.dot_general(stacked, part, NT, preferred_element_type=jnp.float32) for part in (tokens, sibling)
        ]
        projected, a = lax.optimization_barrier((jnp.concatenate(projected, axis=1), a))
        parts = [projected[i * own:(i + 1) * own] for i in range(n // 2)]
        parts = [parts[0]] + [swap(part, k) for part, k in zip(parts[1:], others)]
        rest, more, follow = middle_part(a, factors, follow, begin, middle)
        begun = (scale, a, factors, rest, more, follow)
        return last_part(keep_flags, side, parts, begun, pieces, features, begin, middle)

    in_specs = (P("dp", None), P(("section", "dp"), None), P())
    out_specs = P(("section", "dp"), None)
    return jax.shard_map(on_device, mesh=mesh, in_specs=in_specs, out_specs=out_specs, check_vma=False)
```
